512 devices in a mesh: row: 16 (over z), col: 32 (over y, x, core).
Axes of the slice: x: 4, y: 4, z: 16, core: 2. Of those that a mesh axis runs over, the one named last changes fastest.
Arguments:
- tokens: bfloat16 [2048, 8192], P('col', 'row'), may hold values from -6 to 6
- cotangent: bfloat16 [2048, 8192], P('col', 'row'), may hold values from -42.33202 to 42.33202
- gate_pre: bfloat16 [2048, 14336], P('row', 'col'), may hold values from -6 to 6
- up_act: bfloat16 [2048, 14336], P('row', 'col'), may hold values from -6 to 6
- gate_weight: bfloat16 [8192, 14336], P('row', 'col'), may hold values from -6 to 6
- up_weight: bfloat16 [8192, 14336], P('row', 'col'), may hold values from -6 to 6
- down_weight: bfloat16 [14336, 8192], P('col', 'row'), may hold values from -9 to 9
- moment_m: bfloat16 [14336, 8192], P('col', 'row'), may hold values from -6 to 6
- moment_v: bfloat16 [14336, 8192], P('col', 'row'), may hold values from 0.1 to 1.6015625
Outputs:
- grad_input: bfloat16 [2048, 8192], P('col', 'row')
- grad_gate: bfloat16 [8192, 14336], P('row', 'col')
- grad_up: bfloat16 [8192, 14336], P('row', 'col')
- new_m: bfloat16 [14336, 8192], P('col', 'row')
- new_v: bfloat16 [14336, 8192], P('col', 'row')
- step_down: bfloat16 [14336, 8192], P('col', 'row')
- trust_ratio: float32 [], replicated
The draws below stay inside these ranges and needn't reach their ends.
All inputs are finite; a program needn't handle non-finite values.
Results may differ from the reference program's by a relative error of at most 0.03.
Values may be sent and summed in bfloat16 or wider, within the bound.
No kernel may reach another device: no remote copies, remote signals or barrier semaphores. Data moves between devices by JAX's collectives and lax.ppermute only.
A program may use at most 64 MiB of HBM per device.

```python
import math
import jax
import jax.numpy as jnp
from jax import lax

D = 8192
FF = 14336
TOKENS = 2048
N_ROW = 16
N_COL = 32


def draw_cotangent(key, part):
    key = jax.random.fold_in(key, 11)
    key_rows, key_cols, key_base = jax.random.split(key, 3)
    low = math.log(0.5)
    high = math.log(2.0)
    row_scale = jnp.exp(jax.random.uniform(key_rows, (TOKENS, 1), jnp.float32, low, high))
    col_scale = jnp.exp(jax.random.uniform(key_cols, (1, D), jnp.float32, low, high))
    base = jnp.clip(jax.random.normal(key_base, (TOKENS, D), jnp.float32), -4.0, 4.0)
    overall = (float(FF) / float(TOKENS)) ** 0.5
    return (overall * row_scale * col_scale * base).astype(jnp.bfloat16)


def column_ramp(start, factor):
    position = jnp.arange(D, dtype=jnp.float32) / float(max(D - 1, 1))
    return (start * jnp.exp(math.log(factor) * position)).reshape(1, D)


def draw_down_weight(key, part):
    key = jax.random.fold_in(key, 12)
    base = jnp.clip(jax.random.normal(key, (FF, D), jnp.float32), -6.0, 6.0)
    ramp = column_ramp(0.5, 3.0)
    return (base * ramp).astype(jnp.bfloat16)


def draw_moment_v(key, part):
    key = jax.random.fold_in(key, 13)
    level = column_ramp(0.1, 8.0)
    spread = jnp.exp(jax.random.uniform(key, (FF, D), jnp.float32, 0.0, math.log(2.0)))
    return jnp.clip(level * spread, 0.10009765625, 1.6015625).astype(jnp.bfloat16)


def shard_levels(key, dims, shards, smallest, largest):
    def one(axis_at, parts):
        heights = jax.random.uniform(jax.random.fold_in(jax.random.fold_in(key, 6), axis_at), (parts,), jnp.float32, smallest / len(shards), largest / len(shards))
        return jnp.repeat(jnp.exp(heights), dims[axis_at] // parts).reshape((-1,) + (1,) * (len(dims) - axis_at - 1))

    gain = one(*shards[0])
    for cut in shards[1:]:
        gain = gain * one(*cut)
    return gain


def centred(stream_key, dims, scale, most, shards=(), held_as=jnp.bfloat16):
    entries = jax.random.normal(stream_key, dims, jnp.float32) * scale
    if len(shards) > 0:
        entries = shard_levels(stream_key, dims, shards, -0.22, 0.18) * entries
    return jnp.clip(entries, min=-most, max=most).astype(held_as)


def setup_inputs(seed: int = 0) -> dict:
    arg_keys = jax.random.split(jax.random.key(seed), 10)
    tokens = centred(arg_keys[0], (TOKENS, D), 1.0, 6.0, ((0, 32), (1, 16)))
    cotangent = draw_cotangent(jax.random.fold_in(arg_keys[9], 71), 0)
    gate_pre = centred(arg_keys[2], (TOKENS, FF), 1.5, 6.0, ((0, 16), (1, 32)))
    up_act = centred(arg_keys[3], (TOKENS, FF), 1.0, 6.0, ((0, 16), (1, 32)))
    gate_weight = centred(arg_keys[4], (D, FF), 1.0, 6.0, ((0, 16), (1, 32)))
    up_weight = centred(arg_keys[5], (D, FF), 1.0, 6.0, ((0, 16), (1, 32)))
    down_weight = draw_down_weight(jax.random.fold_in(arg_keys[9], 71), 0)
    moment_m = centred(arg_keys[7], (FF, D), 1.0, 6.0, ((0, 32), (1, 16)))
    moment_v = draw_moment_v(jax.random.fold_in(arg_keys[9], 71), 0)
    return {"tokens": tokens, "cotangent": cotangent, "gate_pre": gate_pre, "up_act": up_act, "gate_weight": gate_weight, "up_weight": up_weight, "down_weight": down_weight, "moment_m": moment_m, "moment_v": moment_v}


def rounded(values):
    return lax.optimization_barrier(values.astype(jnp.bfloat16)).astype(jnp.float32)

def reference(tokens, cotangent, gate_pre, up_act, gate_weight, up_weight, down_weight, moment_m, moment_v):
    scale_width = float(D) ** (-0.5)
    scale_hidden = float(FF) ** (-0.5)
    width_block = D // N_ROW
    grad_hidden = jnp.zeros((TOKENS, FF), jnp.float32)
    for number in range(N_ROW):
        lower = number * width_block
        piece = jnp.dot(cotangent[:, lower:lower + width_block], down_weight[:, lower:lower + width_block].T, preferred_element_type=jnp.float32) * scale_hidden
        grad_hidden = grad_hidden + rounded(piece)
    gate_vals = gate_pre.astype(jnp.float32)
    up_vals = up_act.astype(jnp.float32)
    sigma = jax.nn.sigmoid(gate_vals)
    swish = gate_vals * sigma
    hidden = (swish * up_vals).astype(jnp.bfloat16)
    grad_upact = (grad_hidden * swish).astype(jnp.bfloat16)
    grad_gateact = (grad_hidden * up_vals * sigma * (1.0 + gate_vals * (1.0 - sigma))).astype(jnp.bfloat16)
    grad_down = jnp.dot(hidden.T, cotangent, preferred_element_type=jnp.float32) * scale_hidden
    grad_gate = (jnp.dot(tokens.T, grad_gateact, preferred_element_type=jnp.float32) * scale_width).astype(jnp.bfloat16)
    grad_up = (jnp.dot(tokens.T, grad_upact, preferred_element_type=jnp.float32) * scale_width).astype(jnp.bfloat16)
    hidden_block = FF // N_COL
    input_total = jnp.zeros((TOKENS, D), jnp.float32)
    for number in range(N_COL):
        lower = number * hidden_block
        upper = lower + hidden_block
        piece = jnp.dot(grad_gateact[:, lower:upper], gate_weight[:, lower:upper].T, preferred_element_type=jnp.float32)
        piece = piece + jnp.dot(grad_upact[:, lower:upper], up_weight[:, lower:upper].T, preferred_element_type=jnp.float32)
        input_total = input_total + rounded(piece * scale_width)
    grad_input = input_total.astype(jnp.bfloat16)
    first = 0.9 * moment_m.astype(jnp.float32) + 0.1 * grad_down
    second = 0.95 * moment_v.astype(jnp.float32) + 0.05 * grad_down * grad_down
    weight_vals = down_weight.astype(jnp.float32)
    update = first / (jnp.sqrt(second) + 1e-08) + 0.1 * weight_vals
    weight_total = jnp.sum(weight_vals * weight_vals)
    update_total = jnp.sum(update * update)
    trust_ratio = jnp.sqrt(weight_total) / jnp.sqrt(update_total + 1e-06)
    step_down = (trust_ratio * update).astype(jnp.bfloat16)
    return (grad_input, grad_gate, grad_up, first.astype(jnp.bfloat16), second.astype(jnp.bfloat16), step_down, trust_ratio)
```

```python
import jax
import jax.numpy as jnp
from jax import lax
from jax.experimental import pallas as pl
from jax.experimental.pallas import tpu as pltpu
from jax.sharding import PartitionSpec as P

D = 8192
FF = 14336
Z = 16
SIDE = 4
SCALE_WIDTH = float(D) ** (-0.5)
SCALE_HIDDEN = float(FF) ** (-0.5)
BF16 = jnp.bfloat16
F32 = jnp.float32
VMEM = pl.BlockSpec(memory_space=pltpu.VMEM)
SMEM = pl.BlockSpec(memory_space=pltpu.SMEM)


def params():
    return pltpu.CompilerParams(vmem_limit_bytes=48 * 1024 * 1024)


def shift_z(v, step):
    return lax.ppermute(v, "row", [(i, (i + step) % Z) for i in range(Z)])


def col_of(y, x, core):
    return ((y % SIDE) * SIDE + x % SIDE) * 2 + core


def shift_col(v, dy, dx, swap):
    pairs = []
    for y in range(SIDE):
        for x in range(SIDE):
            for core in range(2):
                pairs.append((col_of(y, x, core), col_of(y + dy, x + dx, core ^ swap)))
    return lax.ppermute(v, "col", pairs)


def shift_x(v, step):
    return shift_col(v, 0, step, 0)


def shift_y(v, step):
    return shift_col(v, step, 0, 0)


def swap_core(v):
    return shift_col(v, 0, 0, 1)


def gather_four(v, shift):
    half = v.shape[0] // 2
    before = shift(v, 1)
    after = shift(v, -1)
    far_top = shift(before[:half], 1)
    far_bottom = shift(after[half:], -1)
    return v, after, far_top, far_bottom, before


def reduce_four(parts, shift):
    half = parts[2].shape[0] // 2
    top = shift(parts[2][:half], 1)
    bottom = shift(parts[2][half:], -1)
    ahead = jnp.concatenate([add(parts[1][:half], top), parts[1][half:]], axis=0)
    behind = jnp.concatenate([parts[3][:half], add(parts[3][half:], bottom)], axis=0)
    from_before = shift(ahead, 1)
    from_after = shift(behind, -1)
    return add(parts[0], from_before, from_after)


def add(*terms):
    total = terms[0].astype(F32)
    for term in terms[1:]:
        total = total + term.astype(F32)
    return total.astype(BF16)


def ring_gather(v, far_right):
    blocks = [None] * Z
    blocks[0] = v
    right = left = v
    for step in range(1, Z // 2 + 1):
        if step < Z // 2 or far_right:
            right = shift_z(right, 1)
            blocks[(Z - step) % Z] = right
        if step < Z // 2 or not far_right:
            left = shift_z(left, -1)
            blocks[step] = left
    return blocks


def ring_reduce(parts):
    right = shift_z(parts[Z // 2], 1)
    left = shift_z(parts[Z // 2 + 1], -1)
    for step in range(2, Z // 2 + 1):
        right = shift_z(add(right, parts[Z // 2 + 1 - step]), 1)
        if step < Z // 2:
            left = shift_z(add(left, parts[Z // 2 + step]), -1)
    return add(parts[0], right, left)


def lay_out(place_ref, pieces, whole_ref):
    core = place_ref[1]
    tokens = whole_ref.shape[0]
    chip_rows = tokens // (SIDE * SIDE)
    rows = chip_rows // 2
    for owner in range(2):
        first, after, far_top, far_bottom, before = pieces[5 * owner : 5 * owner + 5]
        side = core if owner == 0 else 1 - core
        for dy in range(SIDE):
            for dx in range(SIDE):
                chip = place_ref[4 + dy * SIDE + dx]
                start = pl.multiple_of(chip * chip_rows + side * rows, rows)
                if dy == 0:
                    block = first[dx * rows : (dx + 1) * rows, :]
                elif dy == 1:
                    block = after[dx * rows : (dx + 1) * rows, :]
                elif dy == 3:
                    block = before[dx * rows : (dx + 1) * rows, :]
                elif dx < 2:
                    block = far_top[dx * rows : (dx + 1) * rows, :]
                else:
                    block = far_bottom[(dx - 2) * rows : (dx - 1) * rows, :]
                whole_ref[pl.ds(start, rows), :] = block


def hidden_partial_body(place_ref, *refs):
    pieces = refs[:10]
    weight_ref = refs[10]
    cot_ref = refs[11]
    outs = refs[12 : 12 + Z]
    hold = refs[12 + Z]
    lay_out(place_ref, pieces, cot_ref)
    tokens = cot_ref.shape[0]
    width = tokens // Z
    span = tokens // SIDE
    for part in range(SIDE):
        product = lax.dot_general(
            weight_ref[...],
            cot_ref[part * span : (part + 1) * span, :],
            (((1,), (1,)), ((), ())),
            preferred_element_type=F32,
        )
        hold[:, part * span : (part + 1) * span] = (product * SCALE_HIDDEN).astype(BF16)
    z = place_ref[0]
    for k in range(Z):
        start = pl.multiple_of(lax.rem(z + k, Z) * width, width)
        outs[k][...] = hold[:, pl.ds(start, width)]


def hidden_partial(place, pieces, weight):
    units, depth = weight.shape
    tokens = pieces[0].shape[0] * 2 * SIDE
    width = tokens // Z
    shapes = [jax.ShapeDtypeStruct((tokens, depth), BF16)]
    shapes += [jax.ShapeDtypeStruct((units, width), BF16)] * Z
    out = pl.pallas_call(
        hidden_partial_body,
        out_shape=shapes,
        in_specs=[SMEM] + [VMEM] * 11,
        out_specs=[VMEM] * (1 + Z),
        scratch_shapes=[pltpu.VMEM((units, tokens), BF16)],
        compiler_params=params(),
        cost_estimate=pl.CostEstimate(
            flops=2 * units * depth * tokens,
            bytes_accessed=2 * (2 * tokens * depth + units * depth + units * tokens),
            transcendentals=0,
        ),
        name="hidden_partial",
    )(place, *pieces, weight)
    return out[0], out[1:]


def down_body(place_ref, *refs):
    gates = refs[:Z]
    ups = refs[Z : 2 * Z]
    cot_ref, weight_ref, m_ref, v_ref = refs[2 * Z : 2 * Z + 4]
    swish_ref, slope_ref, new_m_ref, new_v_ref, update_ref, sums_ref = refs[2 * Z + 4 : 2 * Z + 10]
    hidden, product = refs[2 * Z + 10 :]
    units, width = gates[0].shape
    chunk = 64 if units % 64 == 0 else units
    z = place_ref[0]
    for k in range(Z):
        start = pl.multiple_of(lax.rem(z + k, Z) * width, width)

        @pl.loop(0, units // chunk)
        def _(i, k=k, start=start):
            rows = pl.ds(pl.multiple_of(i * chunk, chunk), chunk)
            g = gates[k][rows, :].astype(F32)
            u = ups[k][rows, :].astype(F32)
            s = jax.nn.sigmoid(g)
            swish = g * s
            hidden[rows, pl.ds(start, width)] = (swish * u).astype(BF16)
            swish_ref[rows, k * width : (k + 1) * width] = swish.astype(BF16)
            slope_ref[rows, k * width : (k + 1) * width] = (u * s * (1.0 + g * (1.0 - s))).astype(
                BF16
            )

    product[...] = lax.dot_general(
        hidden[...], cot_ref[...], (((1,), (0,)), ((), ())), preferred_element_type=F32
    )
    step = 16
    depth = product.shape[1]

    def optimizer(i, carry):
        weight_sum, update_sum = carry
        rows = pl.ds(pl.multiple_of(i * step, step), step)
        grad = product[rows, :] * SCALE_HIDDEN
        weight = weight_ref[rows, :].astype(F32)
        first = 0.9 * m_ref[rows, :].astype(F32) + 0.1 * grad
        second = 0.95 * v_ref[rows, :].astype(F32) + 0.05 * grad * grad
        update = first / (jnp.sqrt(second) + 1e-08) + 0.1 * weight
        new_m_ref[rows, :] = first.astype(BF16)
        new_v_ref[rows, :] = second.astype(BF16)
        update_ref[rows, :] = update
        return weight_sum + weight * weight, update_sum + update * update

    zero = jnp.zeros((step, depth), F32)
    weight_sum, update_sum = lax.fori_loop(0, units // step, optimizer, (zero, zero))
    sums_ref[0:1, :] = jnp.sum(weight_sum, axis=0, keepdims=True)
    sums_ref[1:2, :] = jnp.sum(update_sum, axis=0, keepdims=True)


def down_update(place, gates, ups, cotangent, weight, moment_m, moment_v):
    units, width = gates[0].shape
    tokens, depth = cotangent.shape
    shapes = [
        jax.ShapeDtypeStruct((units, tokens), BF16),
        jax.ShapeDtypeStruct((units, tokens), BF16),
        jax.ShapeDtypeStruct((units, depth), BF16),
        jax.ShapeDtypeStruct((units, depth), BF16),
        jax.ShapeDtypeStruct((units, depth), F32),
        jax.ShapeDtypeStruct((2, depth), F32),
    ]
    return pl.pallas_call(
        down_body,
        out_shape=shapes,
        in_specs=[SMEM] + [VMEM] * (2 * Z + 4),
        out_specs=[VMEM] * 6,
        scratch_shapes=[pltpu.VMEM((units, tokens), BF16), pltpu.VMEM((units, depth), F32)],
        compiler_params=params(),
        cost_estimate=pl.CostEstimate(
            flops=2 * units * depth * tokens + 30 * units * tokens,
            bytes_accessed=8 * units * tokens + 2 * tokens * depth + 14 * units * depth,
            transcendentals=units * tokens,
        ),
        name="down_update",
    )(place, *gates, *ups, cotangent, weight, moment_m, moment_v)


def input_partial_body(place_ref, *refs):
    grads = refs[:Z]
    swish_ref, slope_ref, gate_weight_ref, up_weight_ref = refs[Z : Z + 4]
    gateact_ref, upact_ref = refs[Z + 4 : Z + 6]
    mine = refs[Z + 6 : Z + 10]
    other = refs[Z + 10 : Z + 14]
    hold = refs[Z + 14]
    units, width = grads[0].shape
    tokens = gateact_ref.shape[1]
    chunk = 64 if units % 64 == 0 else units
    z, core = place_ref[0], place_ref[1]
    for k in range(Z):
        start = pl.multiple_of(lax.rem(z + k, Z) * width, width)

        @pl.loop(0, units // chunk)
        def _(i, k=k, start=start):
            rows = pl.ds(pl.multiple_of(i * chunk, chunk), chunk)
            grad = grads[k][rows, :].astype(F32)
            swish = swish_ref[rows, k * width : (k + 1) * width].astype(F32)
            slope = slope_ref[rows, k * width : (k + 1) * width].astype(F32)
            upact_ref[rows, pl.ds(start, width)] = (grad * swish).astype(BF16)
            gateact_ref[rows, pl.ds(start, width)] = (grad * slope).astype(BF16)

    span = tokens // SIDE
    contract_first = (((0,), (0,)), ((), ()))
    for part in range(SIDE):
        cols = slice(part * span, (part + 1) * span)
        product = lax.dot_general(
            gateact_ref[:, cols], gate_weight_ref[...], contract_first, preferred_element_type=F32
        )
        product = product + lax.dot_general(
            upact_ref[:, cols], up_weight_ref[...], contract_first, preferred_element_type=F32
        )
        hold[cols, :] = (product * SCALE_WIDTH).astype(BF16)
    rows = width // 2
    for dy in range(SIDE):
        for dx in range(SIDE):
            start = place_ref[4 + dy * SIDE + dx] * width
            own = pl.ds(pl.multiple_of(start + core * rows, rows), rows)
            their = pl.ds(pl.multiple_of(start + (1 - core) * rows, rows), rows)
            mine[dy][dx * rows : (dx + 1) * rows, :] = hold[own, :]
            other[dy][dx * rows : (dx + 1) * rows, :] = hold[their, :]


def input_partial(place, grads, swish, slope, gate_weight, up_weight):
    units, width = grads[0].shape
    depth = gate_weight.shape[1]
    tokens = width * Z
    quarter = jax.ShapeDtypeStruct((tokens // 8, depth), BF16)
    acts = jax.ShapeDtypeStruct((units, tokens), BF16)
    out = pl.pallas_call(
        input_partial_body,
        out_shape=[acts, acts] + [quarter] * 8,
        in_specs=[SMEM] + [VMEM] * (Z + 4),
        out_specs=[VMEM] * 10,
        scratch_shapes=[pltpu.VMEM((tokens, depth), BF16)],
        compiler_params=params(),
        cost_estimate=pl.CostEstimate(
            flops=4 * units * depth * tokens,
            bytes_accessed=10 * units * tokens + 2 * tokens * depth + 4 * units * depth,
            transcendentals=0,
        ),
        name="input_partial",
    )(place, *grads, swish, slope, gate_weight, up_weight)
    return out[0], out[1], out[2:6], out[6:10]


def gather_col(v):
    first, after, far_top, far_bottom, before = gather_four(v, shift_x)
    stack = jnp.concatenate([first, after, far_top, far_bottom, before], axis=0)
    own = gather_four(stack, shift_y)
    return list(own) + [swap_core(piece) for piece in own]


def shards(
    tokens, cotangent, gate_pre, up_act, gate_weight, up_weight, down_weight, moment_m, moment_v
):
    z = lax.axis_index("row")
    col = lax.axis_index("col")
    core, chip = col % 2, col // 2
    y, x = chip // SIDE, chip % SIDE
    offsets = jnp.arange(SIDE)
    chips = ((y + offsets) % SIDE)[:, None] * SIDE + ((x + offsets) % SIDE)[None, :]
    place = jnp.concatenate(
        [jnp.stack([z, core, y, x]).astype(jnp.int32), chips.reshape(-1).astype(jnp.int32)]
    )

    pieces = gather_col(cotangent)
    gates = ring_gather(gate_pre.T, True)
    ups = ring_gather(up_act.T, False)
    cotangent_all, partials = hidden_partial(place, pieces, down_weight)
    tokens, _ = lax.optimization_barrier((tokens, pieces[4]))
    tokens_all = lax.all_gather(tokens, "col", axis=0, tiled=True)

    grad_hidden = ring_reduce(partials)
    grads = ring_gather(grad_hidden, True)

    swish, slope, new_m, new_v, update, sums = down_update(
        place, gates, ups, cotangent_all, down_weight, moment_m, moment_v
    )
    sums = jnp.sum(sums, axis=1).reshape(1, 2)
    sums = jnp.sum(lax.all_gather(sums, "col", axis=0, tiled=True), axis=0, keepdims=True)
    sums = jnp.sum(lax.all_gather(sums, "row", axis=0, tiled=True), axis=0)
    trust_ratio = jnp.sqrt(sums[0]) / jnp.sqrt(sums[1] + 1e-06)
    step_down = (trust_ratio * update).astype(BF16)

    gateact, upact, mine, other = input_partial(
        place, grads, swish, slope, gate_weight.T, up_weight.T
    )
    merged = [add(a, swap_core(b)) for a, b in zip(mine, other)]
    quarter = reduce_four(merged, shift_y)
    rows = quarter.shape[0] // SIDE
    grad_input = reduce_four([quarter[k * rows : (k + 1) * rows] for k in range(SIDE)], shift_x)

    contract = (((1,), (0,)), ((), ()))
    grad_gate = lax.dot_general(gateact, tokens_all, contract, preferred_element_type=F32)
    grad_up = lax.dot_general(upact, tokens_all, contract, preferred_element_type=F32)
    return (
        grad_input,
        (grad_gate * SCALE_WIDTH).astype(BF16).T,
        (grad_up * SCALE_WIDTH).astype(BF16).T,
        new_m,
        new_v,
        step_down,
        trust_ratio,
    )


def solution(mesh):
    in_specs = (
        P("col", "row"),
        P("col", "row"),
        P("row", "col"),
        P("row", "col"),
        P("row", "col"),
        P("row", "col"),
        P("col", "row"),
        P("col", "row"),
        P("col", "row"),
    )
    out_specs = (
        P("col", "row"),
        P("row", "col"),
        P("row", "col"),
        P("col", "row"),
        P("col", "row"),
        P("col", "row"),
        P(),
    )
    return jax.shard_map(shards, mesh=mesh, in_specs=in_specs, out_specs=out_specs, check_vma=False)
```

```python
import jax
import jax.numpy as jnp
from jax import lax
from jax.experimental import pallas as pl
from jax.experimental.pallas import tpu as pltpu
from jax.sharding import PartitionSpec as P

D = 8192
FF = 14336
Z = 16
SIDE = 4
CHIPS = 16
COLS = 32
SCALE_WIDTH = float(D) ** (-0.5)
SCALE_HIDDEN = float(FF) ** (-0.5)
BF16 = jnp.bfloat16
F32 = jnp.float32
VMEM = pl.BlockSpec(memory_space=pltpu.VMEM)
SMEM = pl.BlockSpec(memory_space=pltpu.SMEM)


def params():
    return pltpu.CompilerParams(vmem_limit_bytes=48 * 1024 * 1024)


def shift_z(v, step):
    pairs = []
    for z in range(Z):
        for col in range(COLS):
            way = step if col % 2 == 0 else -step
            pairs.append((z * COLS + col, (z + way) % Z * COLS + col))
    return lax.ppermute(v, ("row", "col"), pairs)


def swap_core(v):
    return lax.ppermute(v, "col", [(c, c ^ 1) for c in range(COLS)])


def exchange_chips(v):
    groups = [[2 * chip + core for chip in range(CHIPS)] for core in range(2)]
    return lax.all_to_all(v, "col", 0, 0, axis_index_groups=groups, tiled=True)


def add(*terms):
    total = terms[0].astype(F32)
    for term in terms[1:]:
        total = total + term.astype(F32)
    return total.astype(BF16)


def gather_z(block):
    far = [block[None]]
    for _ in range(SIDE - 1):
        far.append(shift_z(far[-1], SIDE))
    groups = [jnp.concatenate(far, axis=0)]
    for _ in range(SIDE - 1):
        groups.append(shift_z(groups[-1], 1))
    return groups


def reduce_z(groups):
    moving = groups[SIDE - 1]
    for b in range(SIDE - 2, -1, -1):
        moving = add(shift_z(moving, 1), groups[b])
    total = moving[SIDE - 1]
    for a in range(SIDE - 2, -1, -1):
        total = add(shift_z(total, SIDE), moving[a])
    return total


def hidden_partial_body(place_ref, mine_ref, other_ref, weight_ref, cot_ref, *refs):
    outs, hold = refs[:SIDE], refs[SIDE]
    z, core, way = place_ref[0], place_ref[1], place_ref[2]
    chips, rows, _ = mine_ref.shape
    for chip in range(chips):
        own = pl.multiple_of(chip * 2 * rows + core * rows, rows)
        their = pl.multiple_of(chip * 2 * rows + (1 - core) * rows, rows)
        cot_ref[pl.ds(own, rows), :] = mine_ref[chip]
        cot_ref[pl.ds(their, rows), :] = other_ref[chip]
    tokens = cot_ref.shape[0]
    width = tokens // Z
    span = tokens // SIDE
    for part in range(SIDE):
        product = lax.dot_general(
            weight_ref[...],
            cot_ref[part * span : (part + 1) * span, :],
            (((1,), (1,)), ((), ())),
            preferred_element_type=F32,
        )
        hold[:, part * span : (part + 1) * span] = (product * SCALE_HIDDEN).astype(BF16)
    for a in range(SIDE):
        for b in range(SIDE):
            owner = lax.rem(z + way * (4 * a + b) + Z, Z)
            start = pl.multiple_of(owner * width, width)
            outs[b][a] = hold[:, pl.ds(start, width)]


def hidden_partial(place, mine, other, weight):
    units, depth = weight.shape
    tokens = mine.shape[0] * mine.shape[1] * 2
    width = tokens // Z
    shapes = [jax.ShapeDtypeStruct((tokens, depth), BF16)]
    shapes += [jax.ShapeDtypeStruct((SIDE, units, width), BF16)] * SIDE
    out = pl.pallas_call(
        hidden_partial_body,
        out_shape=shapes,
        in_specs=[SMEM] + [VMEM] * 3,
        out_specs=[VMEM] * (1 + SIDE),
        scratch_shapes=[pltpu.VMEM((units, tokens), BF16)],
        compiler_params=params(),
        cost_estimate=pl.CostEstimate(
            flops=2 * units * depth * tokens,
            bytes_accessed=2 * (2 * tokens * depth + units * depth + units * tokens),
            transcendentals=0,
        ),
        name="hidden_partial",
    )(place, mine, other, weight)
    return out[0], out[1:]


def source(place_ref, a, b, width):
    z, way = place_ref[0], place_ref[2]
    owner = lax.rem(z - way * (4 * a + b) + Z, Z)
    return pl.multiple_of(owner * width, width)


def down_body(place_ref, *refs):
    groups = refs[:SIDE]
    cot_ref, weight_ref, m_ref, v_ref = refs[SIDE : SIDE + 4]
    swish_ref, slope_ref, new_m_ref, new_v_ref, update_ref, sums_ref = refs[SIDE + 4 : SIDE + 10]
    hidden, product = refs[SIDE + 10 :]
    width = groups[0].shape[2]
    units = groups[0].shape[1] // 2
    chunk = 64
    for a in range(SIDE):
        for b in range(SIDE):
            start = source(place_ref, a, b, width)
            k = 4 * b + a

            @pl.loop(0, units // chunk)
            def _(i, a=a, b=b, k=k, start=start):
                low = pl.multiple_of(i * chunk, chunk)
                rows = pl.ds(low, chunk)
                g = groups[b][a, rows, :].astype(F32)
                u = groups[b][a, pl.ds(low + units, chunk), :].astype(F32)
                s = jax.nn.sigmoid(g)
                swish = g * s
                slope = u * s * (1.0 + g * (1.0 - s))
                hidden[rows, pl.ds(start, width)] = (swish * u).astype(BF16)
                swish_ref[rows, k * width : (k + 1) * width] = swish.astype(BF16)
                slope_ref[rows, k * width : (k + 1) * width] = slope.astype(BF16)

    product[...] = lax.dot_general(
        hidden[...], cot_ref[...], (((1,), (0,)), ((), ())), preferred_element_type=F32
    )
    step = 16
    depth = product.shape[1]

    def optimizer(i, carry):
        weight_sum, update_sum = carry
        rows = pl.ds(pl.multiple_of(i * step, step), step)
        grad = product[rows, :] * SCALE_HIDDEN
        weight = weight_ref[rows, :].astype(F32)
        first = 0.9 * m_ref[rows, :].astype(F32) + 0.1 * grad
        second = 0.95 * v_ref[rows, :].astype(F32) + 0.05 * grad * grad
        update = first / (jnp.sqrt(second) + 1e-08) + 0.1 * weight
        new_m_ref[rows, :] = first.astype(BF16)
        new_v_ref[rows, :] = second.astype(BF16)
        update_ref[rows, :] = update
        return weight_sum + weight * weight, update_sum + update * update

    zero = jnp.zeros((step, depth), F32)
    weight_sum, update_sum = lax.fori_loop(0, units // step, optimizer, (zero, zero))
    weight_sum = jnp.sum(weight_sum, axis=0, keepdims=True)
    update_sum = jnp.sum(update_sum, axis=0, keepdims=True)
    sums_ref[...] = jnp.zeros_like(sums_ref)
    for part in range(depth // 128):
        cols = slice(part * 128, (part + 1) * 128)
        sums_ref[0:1, :] += weight_sum[:, cols]
        sums_ref[1:2, :] += update_sum[:, cols]


def down_update(place, groups, cotangent, weight, moment_m, moment_v):
    units = groups[0].shape[1] // 2
    tokens, depth = cotangent.shape
    shapes = [
        jax.ShapeDtypeStruct((units, tokens), BF16),
        jax.ShapeDtypeStruct((units, tokens), BF16),
        jax.ShapeDtypeStruct((units, depth), BF16),
        jax.ShapeDtypeStruct((units, depth), BF16),
        jax.ShapeDtypeStruct((units, depth), F32),
        jax.ShapeDtypeStruct((8, 128), F32),
    ]
    return pl.pallas_call(
        down_body,
        out_shape=shapes,
        in_specs=[SMEM] + [VMEM] * (SIDE + 4),
        out_specs=[VMEM] * 6,
        scratch_shapes=[pltpu.VMEM((units, tokens), BF16), pltpu.VMEM((units, depth), F32)],
        compiler_params=params(),
        cost_estimate=pl.CostEstimate(
            flops=2 * units * depth * tokens + 30 * units * tokens,
            bytes_accessed=8 * units * tokens + 2 * tokens * depth + 14 * units * depth,
            transcendentals=units * tokens,
        ),
        name="down_update",
    )(place, *groups, cotangent, weight, moment_m, moment_v)


def input_partial_body(place_ref, *refs):
    grads = refs[:SIDE]
    swish_ref, slope_ref, gate_weight_ref, up_weight_ref = refs[SIDE : SIDE + 4]
    gateact_ref, upact_ref, mine_ref, other_ref, hold = refs[SIDE + 4 :]
    units, width = grads[0].shape[1:]
    tokens = gateact_ref.shape[1]
    chunk = 64
    core = place_ref[1]
    for a in range(SIDE):
        for b in range(SIDE):
            start = source(place_ref, a, b, width)
            k = 4 * b + a

            @pl.loop(0, units // chunk)
            def _(i, a=a, b=b, k=k, start=start):
                rows = pl.ds(pl.multiple_of(i * chunk, chunk), chunk)
                grad = grads[b][a, rows, :].astype(F32)
                swish = swish_ref[rows, k * width : (k + 1) * width].astype(F32)
                slope = slope_ref[rows, k * width : (k + 1) * width].astype(F32)
                upact_ref[rows, pl.ds(start, width)] = (grad * swish).astype(BF16)
                gateact_ref[rows, pl.ds(start, width)] = (grad * slope).astype(BF16)

    span = tokens // SIDE
    contract_first = (((0,), (0,)), ((), ()))
    for part in range(SIDE):
        cols = slice(part * span, (part + 1) * span)
        product = lax.dot_general(
            gateact_ref[:, cols], gate_weight_ref[...], contract_first, preferred_element_type=F32
        )
        product = product + lax.dot_general(
            upact_ref[:, cols], up_weight_ref[...], contract_first, preferred_element_type=F32
        )
        hold[cols, :] = (product * SCALE_WIDTH).astype(BF16)
    chips, rows, _ = mine_ref.shape
    for chip in range(chips):
        own = pl.multiple_of(chip * 2 * rows + core * rows, rows)
        their = pl.multiple_of(chip * 2 * rows + (1 - core) * rows, rows)
        mine_ref[chip] = hold[pl.ds(own, rows), :]
        other_ref[chip] = hold[pl.ds(their, rows), :]


def input_partial(place, grads, swish, slope, gate_weight, up_weight):
    units, width = grads[0].shape[1:]
    depth = gate_weight.shape[1]
    tokens = width * Z
    half = jax.ShapeDtypeStruct((CHIPS, tokens // CHIPS // 2, depth), BF16)
    acts = jax.ShapeDtypeStruct((units, tokens), BF16)
    return pl.pallas_call(
        input_partial_body,
        out_shape=[acts, acts, half, half],
        in_specs=[SMEM] + [VMEM] * (SIDE + 4),
        out_specs=[VMEM] * 4,
        scratch_shapes=[pltpu.VMEM((tokens, depth), BF16)],
        compiler_params=params(),
        cost_estimate=pl.CostEstimate(
            flops=4 * units * depth * tokens,
            bytes_accessed=10 * units * tokens + 2 * tokens * depth + 4 * units * depth,
            transcendentals=0,
        ),
        name="input_partial",
    )(place, *grads, swish, slope, gate_weight, up_weight)


def total_of(sums):
    for axis, size in (("col", COLS), ("row", Z)):
        spread = jnp.broadcast_to(sums[None], (size, *sums.shape))
        sums = jnp.sum(lax.all_to_all(spread, axis, 0, 0, tiled=True), axis=0)
    return sums


def shards(
    tokens, cotangent, gate_pre, up_act, gate_weight, up_weight, down_weight, moment_m, moment_v
):
    z = lax.axis_index("row")
    core = lax.axis_index("col") & 1
    place = jnp.stack([z, core, 1 - 2 * core]).astype(jnp.int32)

    cot_mine = exchange_chips(jnp.broadcast_to(cotangent[None], (CHIPS, *cotangent.shape)))
    cot_other = swap_core(cot_mine)
    acts = gather_z(jnp.concatenate([gate_pre.T, up_act.T], axis=0))
    tokens_all = lax.all_gather(tokens, "col", axis=0, tiled=True)

    cotangent_all, partials = hidden_partial(place, cot_mine, cot_other, down_weight)
    grad_hidden = reduce_z(partials)
    grad_hidden, tokens_all = lax.optimization_barrier((grad_hidden, tokens_all))
    grads = gather_z(grad_hidden)

    swish, slope, new_m, new_v, update, sums = down_update(
        place, acts, cotangent_all, down_weight, moment_m, moment_v
    )
    sums = jnp.sum(total_of(sums), axis=1)
    trust_ratio = jnp.sqrt(sums[0]) / jnp.sqrt(sums[1] + 1e-06)
    step_down = (trust_ratio * update).astype(BF16)

    gateact, upact, mine, other = input_partial(
        place, grads, swish, slope, gate_weight.T, up_weight.T
    )
    arrived = exchange_chips(add(mine, swap_core(other)))
    grad_input = jnp.sum(arrived.astype(F32), axis=0).astype(BF16)

    contract = (((1,), (0,)), ((), ()))
    grad_gate = lax.dot_general(gateact, tokens_all, contract, preferred_element_type=F32)
    grad_up = lax.dot_general(upact, tokens_all, contract, preferred_element_type=F32)
    return (
        grad_input,
        (grad_gate * SCALE_WIDTH).astype(BF16).T,
        (grad_up * SCALE_WIDTH).astype(BF16).T,
        new_m,
        new_v,
        step_down,
        trust_ratio,
    )


def solution(mesh):
    in_specs = (
        P("col", "row"),
        P("col", "row"),
        P("row", "col"),
        P("row", "col"),
        P("row", "col"),
        P("row", "col"),
        P("col", "row"),
        P("col", "row"),
        P("col", "row"),
    )
    out_specs = (
        P("col", "row"),
        P("row", "col"),
        P("row", "col"),
        P("col", "row"),
        P("col", "row"),
        P("col", "row"),
        P(),
    )
    return jax.shard_map(shards, mesh=mesh, in_specs=in_specs, out_specs=out_specs, check_vma=False)
```

```python
import functools

import jax
import jax.numpy as jnp
from jax import lax
from jax.experimental import pallas as pl
from jax.experimental.pallas import tpu as pltpu
from jax.sharding import PartitionSpec as P

D = 8192
FF = 14336
Z = 16
SIDE = 4
CHIPS = 16
COLS = 32
SCALE_WIDTH = float(D) ** (-0.5)
SCALE_HIDDEN = float(FF) ** (-0.5)
BF16 = jnp.bfloat16
F32 = jnp.float32
VMEM = pl.BlockSpec(memory_space=pltpu.VMEM)
SMEM = pl.BlockSpec(memory_space=pltpu.SMEM)


def params():
    return pltpu.CompilerParams(vmem_limit_bytes=48 * 1024 * 1024)


def shift_z(v, step):
    pairs = []
    for z in range(Z):
        for col in range(COLS):
            way = step if col % 2 == 0 else -step
            pairs.append((z * COLS + col, (z + way) % Z * COLS + col))
    return lax.ppermute(v, ("row", "col"), pairs)


def swap_core(v):
    return lax.ppermute(v, "col", [(c, c ^ 1) for c in range(COLS)])


def exchange_chips(v):
    groups = [[2 * chip + core for chip in range(CHIPS)] for core in range(2)]
    return lax.all_to_all(v, "col", 0, 0, axis_index_groups=groups, tiled=True)


def gather_chips(v):
    mine = exchange_chips(jnp.broadcast_to(v[None], (CHIPS, *v.shape)))
    return mine, swap_core(mine)


def add(*terms):
    total = terms[0].astype(F32)
    for term in terms[1:]:
        total = total + term.astype(F32)
    return total.astype(BF16)


def gather_z(block):
    far = [block[None]]
    for _ in range(SIDE - 1):
        far.append(shift_z(far[-1], SIDE))
    groups = [jnp.concatenate(far, axis=0)]
    for _ in range(SIDE - 1):
        groups.append(shift_z(groups[-1], 1))
    return groups


def reduce_z(groups):
    moving = groups[SIDE - 1]
    for b in range(SIDE - 2, -1, -1):
        moving = add(shift_z(moving, 1), groups[b])
    total = moving[SIDE - 1]
    for a in range(SIDE - 2, -1, -1):
        total = add(shift_z(total, SIDE), moving[a])
    return total


def hidden_partial_body(place_ref, mine_ref, other_ref, weight_ref, cot_ref, *refs):
    outs, hold = refs[:SIDE], refs[SIDE]
    z, core, way = place_ref[0], place_ref[1], place_ref[2]
    chips, rows, _ = mine_ref.shape
    for chip in range(chips):
        own = pl.multiple_of(chip * 2 * rows + core * rows, rows)
        their = pl.multiple_of(chip * 2 * rows + (1 - core) * rows, rows)
        cot_ref[pl.ds(own, rows), :] = mine_ref[chip]
        cot_ref[pl.ds(their, rows), :] = other_ref[chip]
    tokens = cot_ref.shape[0]
    width = tokens // Z
    span = tokens // SIDE
    for part in range(SIDE):
        product = lax.dot_general(
            weight_ref[...],
            cot_ref[part * span : (part + 1) * span, :],
            (((1,), (1,)), ((), ())),
            preferred_element_type=F32,
        )
        hold[:, part * span : (part + 1) * span] = (product * SCALE_HIDDEN).astype(BF16)
    for a in range(SIDE):
        for b in range(SIDE):
            owner = lax.rem(z + way * (4 * a + b) + Z, Z)
            start = pl.multiple_of(owner * width, width)
            outs[b][a] = hold[:, pl.ds(start, width)]


def hidden_partial(place, mine, other, weight):
    units, depth = weight.shape
    tokens = mine.shape[0] * mine.shape[1] * 2
    width = tokens // Z
    shapes = [jax.ShapeDtypeStruct((tokens, depth), BF16)]
    shapes += [jax.ShapeDtypeStruct((SIDE, units, width), BF16)] * SIDE
    out = pl.pallas_call(
        hidden_partial_body,
        out_shape=shapes,
        in_specs=[SMEM] + [VMEM] * 3,
        out_specs=[VMEM] * (1 + SIDE),
        scratch_shapes=[pltpu.VMEM((units, tokens), BF16)],
        compiler_params=params(),
        cost_estimate=pl.CostEstimate(
            flops=2 * units * depth * tokens,
            bytes_accessed=2 * (2 * tokens * depth + units * depth + units * tokens),
            transcendentals=0,
        ),
        name="hidden_partial",
    )(place, mine, other, weight)
    return out[0], out[1:]


def source(place_ref, a, b, width):
    z, way = place_ref[0], place_ref[2]
    owner = lax.rem(z - way * (4 * a + b) + Z, Z)
    return pl.multiple_of(owner * width, width)


def down_body(acts_ref, cot_ref, weight_ref, m_ref, v_ref, *refs):
    swish_ref, slope_ref, new_m_ref, new_v_ref, update_ref, sums_ref = refs[:6]
    hidden, product = refs[6:]
    blocks, units, width = acts_ref.shape
    units = units // 2
    chunk = 64
    for k in range(blocks):
        cols = slice(k * width, (k + 1) * width)

        @pl.loop(0, units // chunk)
        def _(i, k=k, cols=cols):
            low = pl.multiple_of(i * chunk, chunk)
            rows = pl.ds(low, chunk)
            g = acts_ref[k, rows, :].astype(F32)
            u = acts_ref[k, pl.ds(low + units, chunk), :].astype(F32)
            s = jax.nn.sigmoid(g)
            swish = g * s
            slope = u * s * (1.0 + g * (1.0 - s))
            hidden[rows, cols] = (swish * u).astype(BF16)
            swish_ref[rows, cols] = swish.astype(BF16)
            slope_ref[rows, cols] = slope.astype(BF16)

    product[...] = lax.dot_general(
        hidden[...], cot_ref[...], (((1,), (0,)), ((), ())), preferred_element_type=F32
    )
    step = 16
    depth = product.shape[1]

    def optimizer(i, carry):
        weight_sum, update_sum = carry
        rows = pl.ds(pl.multiple_of(i * step, step), step)
        grad = product[rows, :] * SCALE_HIDDEN
        weight = weight_ref[rows, :].astype(F32)
        first = 0.9 * m_ref[rows, :].astype(F32) + 0.1 * grad
        second = 0.95 * v_ref[rows, :].astype(F32) + 0.05 * grad * grad
        update = first / (jnp.sqrt(second) + 1e-08) + 0.1 * weight
        new_m_ref[rows, :] = first.astype(BF16)
        new_v_ref[rows, :] = second.astype(BF16)
        update_ref[rows, :] = update
        return weight_sum + weight * weight, update_sum + update * update

    zero = jnp.zeros((step, depth), F32)
    weight_sum, update_sum = lax.fori_loop(0, units // step, optimizer, (zero, zero))
    weight_sum = jnp.sum(weight_sum, axis=0, keepdims=True)
    update_sum = jnp.sum(update_sum, axis=0, keepdims=True)
    sums_ref[...] = jnp.zeros_like(sums_ref)
    for part in range(depth // 128):
        cols = slice(part * 128, (part + 1) * 128)
        sums_ref[0:1, :] += weight_sum[:, cols]
        sums_ref[1:2, :] += update_sum[:, cols]


def down_update(acts, cotangent, weight, moment_m, moment_v):
    units = acts.shape[1] // 2
    tokens, depth = cotangent.shape
    shapes = [
        jax.ShapeDtypeStruct((units, tokens), BF16),
        jax.ShapeDtypeStruct((units, tokens), BF16),
        jax.ShapeDtypeStruct((units, depth), BF16),
        jax.ShapeDtypeStruct((units, depth), BF16),
        jax.ShapeDtypeStruct((units, depth), F32),
        jax.ShapeDtypeStruct((8, 128), F32),
    ]
    return pl.pallas_call(
        down_body,
        out_shape=shapes,
        in_specs=[VMEM] * 5,
        out_specs=[VMEM] * 6,
        scratch_shapes=[pltpu.VMEM((units, tokens), BF16), pltpu.VMEM((units, depth), F32)],
        compiler_params=params(),
        cost_estimate=pl.CostEstimate(
            flops=2 * units * depth * tokens + 30 * units * tokens,
            bytes_accessed=8 * units * tokens + 2 * tokens * depth + 14 * units * depth,
            transcendentals=units * tokens,
        ),
        name="down_update",
    )(acts, cotangent, weight, moment_m, moment_v)


def group_body(b, place_ref, grads_ref, swish_ref, slope_ref, gate_weight_ref, up_weight_ref, *refs):
    gateact_ref, upact_ref, mine_ref, other_ref, hold = refs
    blocks, units, width = grads_ref.shape
    chunk = 64
    core = place_ref[1]
    for a in range(blocks):
        start = source(place_ref, a, b, width)
        cols = slice(a * width, (a + 1) * width)

        @pl.loop(0, units // chunk)
        def _(i, a=a, start=start, cols=cols):
            rows = pl.ds(pl.multiple_of(i * chunk, chunk), chunk)
            grad = grads_ref[a, rows, :].astype(F32)
            swish = swish_ref[rows, pl.ds(start, width)].astype(F32)
            slope = slope_ref[rows, pl.ds(start, width)].astype(F32)
            upact_ref[rows, cols] = (grad * swish).astype(BF16)
            gateact_ref[rows, cols] = (grad * slope).astype(BF16)

    contract_first = (((0,), (0,)), ((), ()))
    product = lax.dot_general(
        gateact_ref[...], gate_weight_ref[...], contract_first, preferred_element_type=F32
    )
    product = product + lax.dot_general(
        upact_ref[...], up_weight_ref[...], contract_first, preferred_element_type=F32
    )
    hold[...] = (product * SCALE_WIDTH).astype(BF16)
    half = width // 2
    for a in range(blocks):
        own = pl.multiple_of(a * width + core * half, half)
        their = pl.multiple_of(a * width + (1 - core) * half, half)
        mine_ref[a] = hold[pl.ds(own, half), :]
        other_ref[a] = hold[pl.ds(their, half), :]


def input_group(b, place, grads, swish, slope, gate_weight, up_weight):
    blocks, units, width = grads.shape
    depth = gate_weight.shape[1]
    half = jax.ShapeDtypeStruct((blocks, width // 2, depth), BF16)
    acts = jax.ShapeDtypeStruct((units, blocks * width), BF16)
    return pl.pallas_call(
        functools.partial(group_body, b),
        out_shape=[acts, acts, half, half],
        in_specs=[SMEM] + [VMEM] * 5,
        out_specs=[VMEM] * 4,
        scratch_shapes=[pltpu.VMEM((blocks * width, depth), BF16)],
        compiler_params=params(),
        cost_estimate=pl.CostEstimate(
            flops=4 * units * depth * blocks * width,
            bytes_accessed=10 * units * blocks * width + 4 * units * depth,
            transcendentals=0,
        ),
        name="input_group",
    )(place, grads, swish, slope, gate_weight, up_weight)


def merge_body(place_ref, *refs):
    mine, other, out_ref = refs[:SIDE], refs[SIDE : 2 * SIDE], refs[2 * SIDE]
    z, way = place_ref[0], place_ref[2]
    for b in range(SIDE):
        for a in range(SIDE):
            out_ref[source(place_ref, a, b, 1)] = mine[b][a]
    for b in range(SIDE):
        for a in range(SIDE):
            chip = lax.rem(z + way * (4 * a + b) + Z, Z)
            total = out_ref[chip].astype(F32) + other[b][a].astype(F32)
            out_ref[chip] = total.astype(BF16)


def merge_cores(place, mine, other):
    _, rows, depth = mine[0].shape
    return pl.pallas_call(
        merge_body,
        out_shape=jax.ShapeDtypeStruct((CHIPS, rows, depth), BF16),
        in_specs=[SMEM] + [VMEM] * (2 * SIDE),
        out_specs=VMEM,
        compiler_params=params(),
        cost_estimate=pl.CostEstimate(
            flops=CHIPS * rows * depth, bytes_accessed=6 * CHIPS * rows * depth, transcendentals=0
        ),
        name="merge_cores",
    )(place, *mine, *other)


def weight_grads_body(place_ref, *refs):
    gateacts, upacts = refs[:SIDE], refs[SIDE : 2 * SIDE]
    mine_ref, other_ref, grad_gate_ref, grad_up_ref, tokens, act = refs[2 * SIDE :]
    core = place_ref[1]
    chips, half, _ = mine_ref.shape
    width = 2 * half
    for chip in range(chips):
        own = pl.multiple_of(chip * width + core * half, half)
        their = pl.multiple_of(chip * width + (1 - core) * half, half)
        tokens[pl.ds(own, half), :] = mine_ref[chip]
        tokens[pl.ds(their, half), :] = other_ref[chip]
    for acts, out_ref in ((gateacts, grad_gate_ref), (upacts, grad_up_ref)):
        for b in range(SIDE):
            for a in range(SIDE):
                start = source(place_ref, a, b, width)
                act[:, pl.ds(start, width)] = acts[b][:, a * width : (a + 1) * width]
        product = lax.dot_general(
            act[...], tokens[...], (((1,), (0,)), ((), ())), preferred_element_type=F32
        )
        out_ref[...] = (product * SCALE_WIDTH).astype(BF16)


def weight_grads(place, gateacts, upacts, mine, other):
    chips, half, depth = mine.shape
    units = gateacts[0].shape[0]
    tokens = chips * half * 2
    out = jax.ShapeDtypeStruct((units, depth), BF16)
    return pl.pallas_call(
        weight_grads_body,
        out_shape=[out, out],
        in_specs=[SMEM] + [VMEM] * (2 * SIDE + 2),
        out_specs=[VMEM] * 2,
        scratch_shapes=[pltpu.VMEM((tokens, depth), BF16), pltpu.VMEM((units, tokens), BF16)],
        compiler_params=params(),
        cost_estimate=pl.CostEstimate(
            flops=4 * units * depth * tokens,
            bytes_accessed=4 * units * tokens + 2 * tokens * depth + 4 * units * depth,
            transcendentals=0,
        ),
        name="weight_grads",
    )(place, *gateacts, *upacts, mine, other)


def total_of(sums):
    for axis, size in (("col", COLS), ("row", Z)):
        spread = jnp.broadcast_to(sums[None], (size, *sums.shape))
        sums = jnp.sum(lax.all_to_all(spread, axis, 0, 0, tiled=True), axis=0)
    return sums


def shards(
    tokens, cotangent, gate_pre, up_act, gate_weight, up_weight, down_weight, moment_m, moment_v
):
    z = lax.axis_index("row")
    core = lax.axis_index("col") & 1
    place = jnp.stack([z, core, 1 - 2 * core]).astype(jnp.int32)

    acts = jnp.concatenate([gate_pre.T, up_act.T], axis=0)
    acts, cotangent = lax.optimization_barrier((acts, cotangent))
    acts = lax.all_gather(acts, "row", axis=0, tiled=False)
    cot_mine, cot_other = gather_chips(cotangent)
    cotangent_all, partials = hidden_partial(place, cot_mine, cot_other, down_weight)
    tokens, _ = lax.optimization_barrier((tokens, cot_other))
    tok_mine, tok_other = gather_chips(tokens)

    grad_hidden = reduce_z(partials)
    grad_hidden, tok_other = lax.optimization_barrier((grad_hidden, tok_other))
    grads = gather_z(grad_hidden)

    swish, slope, new_m, new_v, update, sums = down_update(
        acts, cotangent_all, down_weight, moment_m, moment_v
    )
    gate_weight, up_weight = gate_weight.T, up_weight.T
    groups = [
        input_group(b, place, grads[b], swish, slope, gate_weight, up_weight) for b in range(SIDE)
    ]
    gateacts, upacts, mine, other = zip(*groups)
    merged = merge_cores(place, mine, [swap_core(part) for part in other])
    merged, tok_mine = lax.optimization_barrier((merged, tok_mine))
    arrived = exchange_chips(merged)
    grad_input = jnp.sum(arrived.astype(F32), axis=0).astype(BF16)
    grad_gate, grad_up = weight_grads(place, gateacts, upacts, tok_mine, tok_other)

    sums, grad_gate = lax.optimization_barrier((sums, grad_gate))
    sums = jnp.sum(total_of(sums), axis=1)
    trust_ratio = jnp.sqrt(sums[0]) / jnp.sqrt(sums[1] + 1e-06)
    step_down = (trust_ratio * update).astype(BF16)
    return grad_input, grad_gate.T, grad_up.T, new_m, new_v, step_down, trust_ratio


def solution(mesh):
    in_specs = (
        P("col", "row"),
        P("col", "row"),
        P("row", "col"),
        P("row", "col"),
        P("row", "col"),
        P("row", "col"),
        P("col", "row"),
        P("col", "row"),
        P("col", "row"),
    )
    out_specs = (
        P("col", "row"),
        P("row", "col"),
        P("row", "col"),
        P("col", "row"),
        P("col", "row"),
        P("col", "row"),
        P(),
    )
    return jax.shard_map(shards, mesh=mesh, in_specs=in_specs, out_specs=out_specs, check_vma=False)
```

```python
import functools

import jax
import jax.numpy as jnp
from jax import lax
from jax.experimental import pallas as pl
from jax.experimental.pallas import tpu as pltpu
from jax.sharding import PartitionSpec as P

D = 8192
FF = 14336
Z = 16
SIDE = 4
CHIPS = 16
COLS = 32
SCALE_WIDTH = float(D) ** (-0.5)
SCALE_HIDDEN = float(FF) ** (-0.5)
BF16 = jnp.bfloat16
F32 = jnp.float32
VMEM = pl.BlockSpec(memory_space=pltpu.VMEM)
SMEM = pl.BlockSpec(memory_space=pltpu.SMEM)


def params():
    return pltpu.CompilerParams(vmem_limit_bytes=48 * 1024 * 1024)


def shift_z(v, step):
    pairs = []
    for z in range(Z):
        for col in range(COLS):
            way = step if col % 2 == 0 else -step
            pairs.append((z * COLS + col, (z + way) % Z * COLS + col))
    return lax.ppermute(v, ("row", "col"), pairs)


def swap_core(v):
    return lax.ppermute(v, "col", [(c, c ^ 1) for c in range(COLS)])


def exchange_chips(v):
    groups = [[2 * chip + core for chip in range(CHIPS)] for core in range(2)]
    return lax.all_to_all(v, "col", 0, 0, axis_index_groups=groups, tiled=True)


def gather_chips(v):
    mine = exchange_chips(jnp.broadcast_to(v[None], (CHIPS, *v.shape)))
    return mine, swap_core(mine)


def add(*terms):
    total = terms[0].astype(F32)
    for term in terms[1:]:
        total = total + term.astype(F32)
    return total.astype(BF16)


def reduce_z(zero, far, odd, even, got):
    nearer = shift_z(far, 1)
    odd = jnp.concatenate([odd[:3], add(odd[3], nearer)[None], got[:4]], axis=0)
    even_terms = shift_z(odd, 1)
    held = [
        jnp.stack([even_terms[k], even_terms[4 + k]])
        if k == 0
        else add(jnp.stack([even[k - 1], got[3 + k]]), jnp.stack([even_terms[k], even_terms[4 + k]]))
        for k in range(4)
    ]
    moving = held[3]
    for k in (2, 1, 0):
        moving = add(shift_z(moving, 2), held[k])
    return add(zero, moving[0], swap_core(moving[1]))


GROUPS = ((0, -2, -4, -6), (2, 4, 6), (-1, -3, -5, -7), (1, 3, 5, 7, -8))


def owner_of(place_ref, offset):
    z, way = place_ref[0], place_ref[2]
    return lax.rem(z + way * offset + Z, Z)


def hidden_partial_body(place_ref, mine_ref, other_ref, weight_ref, cot_ref, *refs):
    zero_ref, far_ref, odd_ref, even_ref, give_ref, hold = refs
    core = place_ref[1]
    chips, rows, _ = mine_ref.shape
    for chip in range(chips):
        own = pl.multiple_of(chip * 2 * rows + core * rows, rows)
        their = pl.multiple_of(chip * 2 * rows + (1 - core) * rows, rows)
        cot_ref[pl.ds(own, rows), :] = mine_ref[chip]
        cot_ref[pl.ds(their, rows), :] = other_ref[chip]
    tokens = cot_ref.shape[0]
    width = tokens // Z
    span = tokens // SIDE
    for part in range(SIDE):
        product = lax.dot_general(
            weight_ref[...],
            cot_ref[part * span : (part + 1) * span, :],
            (((1,), (1,)), ((), ())),
            preferred_element_type=F32,
        )
        hold[:, part * span : (part + 1) * span] = (product * SCALE_HIDDEN).astype(BF16)

    def block(offset):
        start = pl.multiple_of(owner_of(place_ref, offset) * width, width)
        return hold[:, pl.ds(start, width)]

    zero_ref[...] = block(0)
    far_ref[...] = block(8)
    for k, offset in enumerate((1, 3, 5, 7)):
        odd_ref[k] = block(offset)
    for k, offset in enumerate((2, 4, 6)):
        even_ref[k] = block(offset)
    for k, offset in enumerate((1, 3, 5, 7, 2, 4, 6)):
        give_ref[k] = block(-offset)


def hidden_partial(place, mine, other, weight):
    units, depth = weight.shape
    tokens = mine.shape[0] * mine.shape[1] * 2
    width = tokens // Z
    shapes = [(tokens, depth), (units, width), (units, width)]
    shapes += [(count, units, width) for count in (4, 3, 7)]
    return pl.pallas_call(
        hidden_partial_body,
        out_shape=[jax.ShapeDtypeStruct(shape, BF16) for shape in shapes],
        in_specs=[SMEM] + [VMEM] * 3,
        out_specs=[VMEM] * 6,
        scratch_shapes=[pltpu.VMEM((units, tokens), BF16)],
        compiler_params=params(),
        cost_estimate=pl.CostEstimate(
            flops=2 * units * depth * tokens,
            bytes_accessed=2 * (2 * tokens * depth + units * depth + units * tokens),
            transcendentals=0,
        ),
        name="hidden_partial",
    )(place, mine, other, weight)


def down_body(acts_ref, cot_ref, weight_ref, m_ref, v_ref, *refs):
    swish_ref, slope_ref, new_m_ref, new_v_ref, update_ref, sums_ref = refs[:6]
    hidden, product = refs[6:]
    blocks, units, width = acts_ref.shape
    units = units // 2
    chunk = 64
    for k in range(blocks):
        cols = slice(k * width, (k + 1) * width)

        @pl.loop(0, units // chunk)
        def _(i, k=k, cols=cols):
            low = pl.multiple_of(i * chunk, chunk)
            rows = pl.ds(low, chunk)
            g = acts_ref[k, rows, :].astype(F32)
            u = acts_ref[k, pl.ds(low + units, chunk), :].astype(F32)
            s = jax.nn.sigmoid(g)
            swish = g * s
            slope = u * s * (1.0 + g * (1.0 - s))
            hidden[rows, cols] = (swish * u).astype(BF16)
            swish_ref[rows, cols] = swish.astype(BF16)
            slope_ref[rows, cols] = slope.astype(BF16)

    product[...] = lax.dot_general(
        hidden[...], cot_ref[...], (((1,), (0,)), ((), ())), preferred_element_type=F32
    )
    step = 16
    depth = product.shape[1]

    def optimizer(i, carry):
        weight_sum, update_sum = carry
        rows = pl.ds(pl.multiple_of(i * step, step), step)
        grad = product[rows, :] * SCALE_HIDDEN
        weight = weight_ref[rows, :].astype(F32)
        first = 0.9 * m_ref[rows, :].astype(F32) + 0.1 * grad
        second = 0.95 * v_ref[rows, :].astype(F32) + 0.05 * grad * grad
        update = first / (jnp.sqrt(second) + 1e-08) + 0.1 * weight
        new_m_ref[rows, :] = first.astype(BF16)
        new_v_ref[rows, :] = second.astype(BF16)
        update_ref[rows, :] = update
        return weight_sum + weight * weight, update_sum + update * update

    zero = jnp.zeros((step, depth), F32)
    weight_sum, update_sum = lax.fori_loop(0, units // step, optimizer, (zero, zero))
    weight_sum = jnp.sum(weight_sum, axis=0, keepdims=True)
    update_sum = jnp.sum(update_sum, axis=0, keepdims=True)
    sums_ref[...] = jnp.zeros_like(sums_ref)
    for part in range(depth // 128):
        cols = slice(part * 128, (part + 1) * 128)
        sums_ref[0:1, :] += weight_sum[:, cols]
        sums_ref[1:2, :] += update_sum[:, cols]


def down_update(acts, cotangent, weight, moment_m, moment_v):
    units = acts.shape[1] // 2
    tokens, depth = cotangent.shape
    shapes = [
        jax.ShapeDtypeStruct((units, tokens), BF16),
        jax.ShapeDtypeStruct((units, tokens), BF16),
        jax.ShapeDtypeStruct((units, depth), BF16),
        jax.ShapeDtypeStruct((units, depth), BF16),
        jax.ShapeDtypeStruct((units, depth), F32),
        jax.ShapeDtypeStruct((8, 128), F32),
    ]
    return pl.pallas_call(
        down_body,
        out_shape=shapes,
        in_specs=[VMEM] * 5,
        out_specs=[VMEM] * 6,
        scratch_shapes=[pltpu.VMEM((units, tokens), BF16), pltpu.VMEM((units, depth), F32)],
        compiler_params=params(),
        cost_estimate=pl.CostEstimate(
            flops=2 * units * depth * tokens + 30 * units * tokens,
            bytes_accessed=8 * units * tokens + 2 * tokens * depth + 14 * units * depth,
            transcendentals=units * tokens,
        ),
        name="down_update",
    )(acts, cotangent, weight, moment_m, moment_v)


def group_body(number, count, place_ref, *refs):
    grads = refs[:count]
    swish_ref, slope_ref, gate_weight_ref, up_weight_ref = refs[count : count + 4]
    gateact_ref, upact_ref, mine_ref, other_ref, hold = refs[count + 4 :]
    units = gateact_ref.shape[0]
    blocks, half, _ = mine_ref.shape
    width = 2 * half
    chunk = 64
    core = place_ref[1]
    for k, offset in enumerate(GROUPS[number]):
        start = pl.multiple_of(owner_of(place_ref, offset) * width, width)
        cols = slice(k * width, (k + 1) * width)

        @pl.loop(0, units // chunk)
        def _(i, k=k, start=start, cols=cols):
            rows = pl.ds(pl.multiple_of(i * chunk, chunk), chunk)
            if k == 4:
                grad = grads[1][rows, :]
            elif number % 2 == 0:
                grad = grads[0][0, k, rows, :]
            else:
                grad = grads[0][k, rows, :]
            grad = grad.astype(F32)
            swish = swish_ref[rows, pl.ds(start, width)].astype(F32)
            slope = slope_ref[rows, pl.ds(start, width)].astype(F32)
            upact_ref[rows, cols] = (grad * swish).astype(BF16)
            gateact_ref[rows, cols] = (grad * slope).astype(BF16)

    contract_first = (((0,), (0,)), ((), ()))
    product = lax.dot_general(
        gateact_ref[...], gate_weight_ref[...], contract_first, preferred_element_type=F32
    )
    product = product + lax.dot_general(
        upact_ref[...], up_weight_ref[...], contract_first, preferred_element_type=F32
    )
    hold[...] = (product * SCALE_WIDTH).astype(BF16)
    for k in range(blocks):
        own = pl.multiple_of(k * width + core * half, half)
        their = pl.multiple_of(k * width + (1 - core) * half, half)
        mine_ref[k] = hold[pl.ds(own, half), :]
        other_ref[k] = hold[pl.ds(their, half), :]


def input_group(number, place, grads, swish, slope, gate_weight, up_weight):
    units, tokens = swish.shape
    depth = gate_weight.shape[1]
    width = tokens // Z
    blocks = len(GROUPS[number])
    half = jax.ShapeDtypeStruct((blocks, width // 2, depth), BF16)
    acts = jax.ShapeDtypeStruct((units, blocks * width), BF16)
    return pl.pallas_call(
        functools.partial(group_body, number, len(grads)),
        out_shape=[acts, acts, half, half],
        in_specs=[SMEM] + [VMEM] * (4 + len(grads)),
        out_specs=[VMEM] * 4,
        scratch_shapes=[pltpu.VMEM((blocks * width, depth), BF16)],
        compiler_params=params(),
        cost_estimate=pl.CostEstimate(
            flops=4 * units * depth * blocks * width,
            bytes_accessed=10 * units * blocks * width + 4 * units * depth,
            transcendentals=0,
        ),
        name="input_group",
    )(place, *grads, swish, slope, gate_weight, up_weight)


def merge_body(place_ref, *refs):
    mine, other, out_ref = refs[:SIDE], refs[SIDE : 2 * SIDE], refs[2 * SIDE]
    for number, offsets in enumerate(GROUPS):
        for k, offset in enumerate(offsets):
            out_ref[owner_of(place_ref, offset)] = mine[number][k]
    for number, offsets in enumerate(GROUPS):
        for k, offset in enumerate(offsets):
            chip = owner_of(place_ref, -offset)
            total = out_ref[chip].astype(F32) + other[number][k].astype(F32)
            out_ref[chip] = total.astype(BF16)


def merge_cores(place, mine, other):
    _, rows, depth = mine[0].shape
    return pl.pallas_call(
        merge_body,
        out_shape=jax.ShapeDtypeStruct((CHIPS, rows, depth), BF16),
        in_specs=[SMEM] + [VMEM] * (2 * SIDE),
        out_specs=VMEM,
        compiler_params=params(),
        cost_estimate=pl.CostEstimate(
            flops=CHIPS * rows * depth, bytes_accessed=6 * CHIPS * rows * depth, transcendentals=0
        ),
        name="merge_cores",
    )(place, *mine, *other)


def weight_grads_body(place_ref, *refs):
    gateacts, upacts = refs[:SIDE], refs[SIDE : 2 * SIDE]
    mine_ref, other_ref, grad_gate_ref, grad_up_ref, tokens, act = refs[2 * SIDE :]
    core = place_ref[1]
    chips, half, _ = mine_ref.shape
    width = 2 * half
    for chip in range(chips):
        own = pl.multiple_of(chip * width + core * half, half)
        their = pl.multiple_of(chip * width + (1 - core) * half, half)
        tokens[pl.ds(own, half), :] = mine_ref[chip]
        tokens[pl.ds(their, half), :] = other_ref[chip]
    for acts, out_ref in ((gateacts, grad_gate_ref), (upacts, grad_up_ref)):
        for number, offsets in enumerate(GROUPS):
            for k, offset in enumerate(offsets):
                start = pl.multiple_of(owner_of(place_ref, offset) * width, width)
                act[:, pl.ds(start, width)] = acts[number][:, k * width : (k + 1) * width]
        product = lax.dot_general(
            act[...], tokens[...], (((1,), (0,)), ((), ())), preferred_element_type=F32
        )
        out_ref[...] = (product * SCALE_WIDTH).astype(BF16)


def weight_grads(place, gateacts, upacts, mine, other):
    chips, half, depth = mine.shape
    units = gateacts[0].shape[0]
    tokens = chips * half * 2
    out = jax.ShapeDtypeStruct((units, depth), BF16)
    return pl.pallas_call(
        weight_grads_body,
        out_shape=[out, out],
        in_specs=[SMEM] + [VMEM] * (2 * SIDE + 2),
        out_specs=[VMEM] * 2,
        scratch_shapes=[pltpu.VMEM((tokens, depth), BF16), pltpu.VMEM((units, tokens), BF16)],
        compiler_params=params(),
        cost_estimate=pl.CostEstimate(
            flops=4 * units * depth * tokens,
            bytes_accessed=4 * units * tokens + 2 * tokens * depth + 4 * units * depth,
            transcendentals=0,
        ),
        name="weight_grads",
    )(place, *gateacts, *upacts, mine, other)


def ring_pairs(step):
    return [(i, (i + step) % Z) for i in range(Z)]


def spread_add(sums, axis, pairs):
    return sums + lax.ppermute(sums, axis, pairs)


def shards(
    tokens, cotangent, gate_pre, up_act, gate_weight, up_weight, down_weight, moment_m, moment_v
):
    z = lax.axis_index("row")
    core = lax.axis_index("col") & 1
    place = jnp.stack([z, core, 1 - 2 * core]).astype(jnp.int32)

    acts = jnp.concatenate([gate_pre.T, up_act.T], axis=0)
    acts, cotangent = lax.optimization_barrier((acts, cotangent))
    acts = lax.all_gather(acts, "row", axis=0, tiled=False)
    cot_mine, cot_other = gather_chips(cotangent)
    cotangent_all, zero, far, odd, even, give = hidden_partial(
        place, cot_mine, cot_other, down_weight
    )
    tokens, _ = lax.optimization_barrier((tokens, cot_other))
    tok_mine, tok_other = gather_chips(tokens)
    grad_hidden = reduce_z(zero, far, odd, even, swap_core(give))
    grad_hidden, tok_other = lax.optimization_barrier((grad_hidden, tok_other))

    swish, slope, new_m, new_v, update, sums = down_update(
        acts, cotangent_all, down_weight, moment_m, moment_v
    )
    gate_weight, up_weight = gate_weight.T, up_weight.T

    def group(number, *grads):
        return input_group(number, place, grads, swish, slope, gate_weight, up_weight)

    pair = jnp.stack([grad_hidden, swap_core(grad_hidden)])
    second = shift_z(pair, 2)
    third = shift_z(second, 2)
    third, swish = lax.optimization_barrier((third, swish))
    fourth = shift_z(third, 2)
    for step in (1, 2):
        sums = spread_add(sums, "row", ring_pairs(step))
    fourth, sums = lax.optimization_barrier((fourth, sums))
    even = jnp.stack([pair, second, third, fourth], axis=1)
    odd = shift_z(even, 1)
    ahead_even = swap_core(even[1, 1:])
    first_groups = (group(0, even), group(1, ahead_even))
    for step in (4, 8):
        sums = spread_add(sums, "row", ring_pairs(step))
    odd, first_groups, sums = lax.optimization_barrier((odd, first_groups, sums))
    far = shift_z(odd[0, 3], 1)
    ahead_odd = swap_core(odd[1])
    groups = (*first_groups, group(2, odd), group(3, ahead_odd, far))
    gateacts, upacts, mine, other = zip(*groups)
    sums = spread_add(sums, "col", [(c, c ^ 1) for c in range(COLS)])
    merged = merge_cores(place, mine, [swap_core(part) for part in other])
    merged, sums, tok_mine = lax.optimization_barrier((merged, sums, tok_mine))
    arrived = exchange_chips(merged)
    grad_input = jnp.sum(arrived.astype(F32), axis=0).astype(BF16)
    grad_gate, grad_up = weight_grads(place, gateacts, upacts, tok_mine, tok_other)

    for step in (2, 4, 8, 16):
        sums = spread_add(sums, "col", [(c, c ^ step) for c in range(COLS)])
    sums = jnp.sum(sums, axis=1)
    trust_ratio = jnp.sqrt(sums[0]) / jnp.sqrt(sums[1] + 1e-06)
    step_down = (trust_ratio * update).astype(BF16)
    return grad_input, grad_gate.T, grad_up.T, new_m, new_v, step_down, trust_ratio


def solution(mesh):
    in_specs = (
        P("col", "row"),
        P("col", "row"),
        P("row", "col"),
        P("row", "col"),
        P("row", "col"),
        P("row", "col"),
        P("col", "row"),
        P("col", "row"),
        P("col", "row"),
    )
    out_specs = (
        P("col", "row"),
        P("row", "col"),
        P("row", "col"),
        P("col", "row"),
        P("col", "row"),
        P("col", "row"),
        P(),
    )
    return jax.shard_map(shards, mesh=mesh, in_specs=in_specs, out_specs=out_specs, check_vma=False)
```

```python
import functools

import jax
import jax.numpy as jnp
from jax import lax
from jax.experimental import pallas as pl
from jax.experimental.pallas import tpu as pltpu
from jax.sharding import PartitionSpec as P

D = 8192
FF = 14336
Z = 16
SIDE = 4
CHIPS = 16
COLS = 32
SCALE_WIDTH = float(D) ** (-0.5)
SCALE_HIDDEN = float(FF) ** (-0.5)
BF16 = jnp.bfloat16
F32 = jnp.float32
VMEM = pl.BlockSpec(memory_space=pltpu.VMEM)
SMEM = pl.BlockSpec(memory_space=pltpu.SMEM)


def params():
    return pltpu.CompilerParams(vmem_limit_bytes=48 * 1024 * 1024)


def shift_z(v, step):
    pairs = []
    for z in range(Z):
        for col in range(COLS):
            way = step if col % 2 == 0 else -step
            pairs.append((z * COLS + col, (z + way) % Z * COLS + col))
    return lax.ppermute(v, ("row", "col"), pairs)


def swap_core(v):
    return lax.ppermute(v, "col", [(c, c ^ 1) for c in range(COLS)])


def exchange_chips(v):
    groups = [[2 * chip + core for chip in range(CHIPS)] for core in range(2)]
    return lax.all_to_all(v, "col", 0, 0, axis_index_groups=groups, tiled=True)


def gather_chips(v):
    mine = exchange_chips(jnp.broadcast_to(v[None], (CHIPS, *v.shape)))
    return mine, swap_core(mine)


def add(*terms):
    total = terms[0].astype(F32)
    for term in terms[1:]:
        total = total + term.astype(F32)
    return total.astype(BF16)


def reduce_z(zero, far, odd, even, give_odd, give_even, extra):
    own = shift_z(odd, 1)
    got_odd = swap_core(give_odd)
    their = shift_z(got_odd, 1)
    far = shift_z(far, 2)
    got_even = swap_core(give_even)
    moving = jnp.stack([add(even[2], own[3], far), add(got_even[2], their[3])])
    for k in (2, 1):
        held = jnp.stack([add(even[k - 1], own[k]), add(got_even[k - 1], their[k])])
        moving = add(shift_z(moving, 2), held)
    moving = shift_z(moving, 2)
    mine = jnp.concatenate([add(zero, moving[0], own[0]), extra], axis=0)
    other = jnp.concatenate([add(moving[1], their[0]), jnp.zeros_like(extra)], axis=0)
    mine = jnp.stack([mine, other])
    other = swap_core(mine)
    return jnp.stack([add(mine[0], other[1]), add(mine[1], other[0])])


GROUPS = ((0, -2, -4, -6), (2, 4, 6), (-1, -3, -5, -7), (1, 3, 5, 7, -8))


def owner_of(place_ref, offset):
    z, way = place_ref[0], place_ref[2]
    return lax.rem(z + way * offset + Z, Z)


def hidden_partial_body(place_ref, mine_ref, other_ref, weight_ref, cot_ref, *refs):
    zero_ref, far_ref, odd_ref, even_ref, give_odd_ref, give_even_ref, hold = refs
    core = place_ref[1]
    chips, rows, _ = mine_ref.shape
    for chip in range(chips):
        own = pl.multiple_of(chip * 2 * rows + core * rows, rows)
        their = pl.multiple_of(chip * 2 * rows + (1 - core) * rows, rows)
        cot_ref[pl.ds(own, rows), :] = mine_ref[chip]
        cot_ref[pl.ds(their, rows), :] = other_ref[chip]
    tokens = cot_ref.shape[0]
    width = tokens // Z
    span = tokens // SIDE
    for part in range(SIDE):
        product = lax.dot_general(
            weight_ref[...],
            cot_ref[part * span : (part + 1) * span, :],
            (((1,), (1,)), ((), ())),
            preferred_element_type=F32,
        )
        hold[:, part * span : (part + 1) * span] = (product * SCALE_HIDDEN).astype(BF16)

    def block(offset):
        start = pl.multiple_of(owner_of(place_ref, offset) * width, width)
        return hold[:, pl.ds(start, width)]

    zero_ref[...] = block(0)
    far_ref[...] = block(8)
    for k, offset in enumerate((1, 3, 5, 7)):
        odd_ref[k] = block(offset)
        give_odd_ref[k] = block(-offset)
    for k, offset in enumerate((2, 4, 6)):
        even_ref[k] = block(offset)
        give_even_ref[k] = block(-offset)


def hidden_partial(place, mine, other, weight):
    units, depth = weight.shape
    tokens = mine.shape[0] * mine.shape[1] * 2
    width = tokens // Z
    shapes = [(tokens, depth), (units, width), (units, width)]
    shapes += [(count, units, width) for count in (4, 3, 4, 3)]
    return pl.pallas_call(
        hidden_partial_body,
        out_shape=[jax.ShapeDtypeStruct(shape, BF16) for shape in shapes],
        in_specs=[SMEM] + [VMEM] * 3,
        out_specs=[VMEM] * 7,
        scratch_shapes=[pltpu.VMEM((units, tokens), BF16)],
        compiler_params=params(),
        cost_estimate=pl.CostEstimate(
            flops=2 * units * depth * tokens,
            bytes_accessed=2 * (2 * tokens * depth + units * depth + units * tokens),
            transcendentals=0,
        ),
        name="hidden_partial",
    )(place, mine, other, weight)


def down_body(acts_ref, cot_ref, weight_ref, m_ref, v_ref, *refs):
    swish_ref, slope_ref, new_m_ref, new_v_ref, update_ref, sums_ref = refs[:6]
    hidden, product = refs[6:]
    blocks, units, width = acts_ref.shape
    units = units // 2
    chunk = 64
    for k in range(blocks):
        cols = slice(k * width, (k + 1) * width)

        @pl.loop(0, units // chunk)
        def _(i, k=k, cols=cols):
            low = pl.multiple_of(i * chunk, chunk)
            rows = pl.ds(low, chunk)
            g = acts_ref[k, rows, :].astype(F32)
            u = acts_ref[k, pl.ds(low + units, chunk), :].astype(F32)
            s = jax.nn.sigmoid(g)
            swish = g * s
            slope = u * s * (1.0 + g * (1.0 - s))
            hidden[rows, cols] = (swish * u).astype(BF16)
            swish_ref[rows, cols] = swish.astype(BF16)
            slope_ref[rows, cols] = slope.astype(BF16)

    product[...] = lax.dot_general(
        hidden[...], cot_ref[...], (((1,), (0,)), ((), ())), preferred_element_type=F32
    )
    step = 16
    depth = product.shape[1]

    def optimizer(i, carry):
        weight_sum, update_sum = carry
        rows = pl.ds(pl.multiple_of(i * step, step), step)
        grad = product[rows, :] * SCALE_HIDDEN
        weight = weight_ref[rows, :].astype(F32)
        first = 0.9 * m_ref[rows, :].astype(F32) + 0.1 * grad
        second = 0.95 * v_ref[rows, :].astype(F32) + 0.05 * grad * grad
        update = first / (jnp.sqrt(second) + 1e-08) + 0.1 * weight
        new_m_ref[rows, :] = first.astype(BF16)
        new_v_ref[rows, :] = second.astype(BF16)
        update_ref[rows, :] = update
        return weight_sum + weight * weight, update_sum + update * update

    zero = jnp.zeros((step, depth), F32)
    weight_sum, update_sum = lax.fori_loop(0, units // step, optimizer, (zero, zero))
    weight_sum = jnp.sum(weight_sum, axis=0, keepdims=True)
    update_sum = jnp.sum(update_sum, axis=0, keepdims=True)
    lanes = sums_ref.shape[1]
    parts = [slice(k, k + lanes) for k in range(0, depth, lanes)]
    weight_sum = sum(weight_sum[:, part] for part in parts)
    update_sum = sum(update_sum[:, part] for part in parts)
    sums_ref[...] = in_rows(weight_sum, update_sum)


def in_rows(first, second):
    row = lax.broadcasted_iota(jnp.int32, (16, first.shape[1]), 0)
    value = jnp.where((row & 1) == 0, first, second)
    high = value.astype(BF16).astype(F32)
    middle = (value - high).astype(BF16).astype(F32)
    low = value - high - middle
    rest = jnp.where(row < 4, middle, jnp.where(row < 6, low, 0.0))
    return jnp.where(row < 2, high, rest).astype(BF16)


def from_rows(rows):
    first = rows[0:1] + rows[2:3] + rows[4:5]
    second = rows[1:2] + rows[3:4] + rows[5:6]
    return jnp.sum(first, axis=1, keepdims=True), jnp.sum(second, axis=1, keepdims=True)


def down_update(acts, cotangent, weight, moment_m, moment_v):
    units = acts.shape[1] // 2
    tokens, depth = cotangent.shape
    shapes = [
        jax.ShapeDtypeStruct((units, tokens), BF16),
        jax.ShapeDtypeStruct((units, tokens), BF16),
        jax.ShapeDtypeStruct((units, depth), BF16),
        jax.ShapeDtypeStruct((units, depth), BF16),
        jax.ShapeDtypeStruct((units, depth), F32),
        jax.ShapeDtypeStruct((16, 128), BF16),
    ]
    return pl.pallas_call(
        down_body,
        out_shape=shapes,
        in_specs=[VMEM] * 5,
        out_specs=[VMEM] * 6,
        scratch_shapes=[pltpu.VMEM((units, tokens), BF16), pltpu.VMEM((units, depth), F32)],
        compiler_params=params(),
        cost_estimate=pl.CostEstimate(
            flops=2 * units * depth * tokens + 30 * units * tokens,
            bytes_accessed=8 * units * tokens + 2 * tokens * depth + 14 * units * depth,
            transcendentals=units * tokens,
        ),
        name="down_update",
    )(acts, cotangent, weight, moment_m, moment_v)


def group_body(number, count, place_ref, *refs):
    grads = refs[:count]
    swish_ref, slope_ref, gate_weight_ref, up_weight_ref, before_ref = refs[count : count + 5]
    gateact_ref, upact_ref, mine_ref, other_ref, sums_ref, hold = refs[count + 5 :]
    units = gateact_ref.shape[0]
    blocks, half, _ = mine_ref.shape
    width = 2 * half
    chunk = 64
    core = place_ref[1]

    def block(k, rows):
        if k == 4:
            return grads[1][rows, :].astype(F32)
        if number % 2 == 0:
            return grads[0][0, k, rows, :].astype(F32)
        return grads[0][k, rows, :].astype(F32)

    sums = before_ref[...]
    for k in range(blocks):
        sums = sums + block(k, slice(units, units + 16))
    sums_ref[...] = sums
    for k, offset in enumerate(GROUPS[number]):
        start = pl.multiple_of(owner_of(place_ref, offset) * width, width)
        cols = slice(k * width, (k + 1) * width)

        @pl.loop(0, units // chunk)
        def _(i, k=k, start=start, cols=cols):
            rows = pl.ds(pl.multiple_of(i * chunk, chunk), chunk)
            grad = block(k, rows)
            swish = swish_ref[rows, pl.ds(start, width)].astype(F32)
            slope = slope_ref[rows, pl.ds(start, width)].astype(F32)
            upact_ref[rows, cols] = (grad * swish).astype(BF16)
            gateact_ref[rows, cols] = (grad * slope).astype(BF16)

    contract_first = (((0,), (0,)), ((), ()))
    product = lax.dot_general(
        gateact_ref[...], gate_weight_ref[...], contract_first, preferred_element_type=F32
    )
    product = product + lax.dot_general(
        upact_ref[...], up_weight_ref[...], contract_first, preferred_element_type=F32
    )
    hold[...] = (product * SCALE_WIDTH).astype(BF16)
    for k in range(blocks):
        own = pl.multiple_of(k * width + core * half, half)
        their = pl.multiple_of(k * width + (1 - core) * half, half)
        mine_ref[k] = hold[pl.ds(own, half), :]
        other_ref[k] = hold[pl.ds(their, half), :]


def input_group(number, place, grads, swish, slope, gate_weight, up_weight, before):
    units, tokens = swish.shape
    depth = gate_weight.shape[1]
    width = tokens // Z
    blocks = len(GROUPS[number])
    half = jax.ShapeDtypeStruct((blocks, width // 2, depth), BF16)
    acts = jax.ShapeDtypeStruct((units, blocks * width), BF16)
    sums = jax.ShapeDtypeStruct((16, 128), F32)
    return pl.pallas_call(
        functools.partial(group_body, number, len(grads)),
        out_shape=[acts, acts, half, half, sums],
        in_specs=[SMEM] + [VMEM] * (5 + len(grads)),
        out_specs=[VMEM] * 5,
        scratch_shapes=[pltpu.VMEM((blocks * width, depth), BF16)],
        compiler_params=params(),
        cost_estimate=pl.CostEstimate(
            flops=4 * units * depth * blocks * width,
            bytes_accessed=10 * units * blocks * width + 4 * units * depth,
            transcendentals=0,
        ),
        name="input_group",
    )(place, *grads, swish, slope, gate_weight, up_weight, before)


def merge_body(place_ref, *refs):
    mine, other = refs[:SIDE], refs[SIDE : 2 * SIDE]
    sums_ref, other_sums_ref, out_ref = refs[2 * SIDE :]
    rows = mine[0].shape[1]
    for number, offsets in enumerate(GROUPS):
        for k, offset in enumerate(offsets):
            out_ref[owner_of(place_ref, offset), 0:rows, :] = mine[number][k]
    for number, offsets in enumerate(GROUPS):
        for k, offset in enumerate(offsets):
            chip = owner_of(place_ref, -offset)
            total = out_ref[chip, 0:rows, :].astype(F32) + other[number][k].astype(F32)
            out_ref[chip, 0:rows, :] = total.astype(BF16)
    first, second = from_rows(sums_ref[...] + other_sums_ref[...])
    depth = out_ref.shape[2]
    sums = in_rows(jnp.broadcast_to(first, (1, depth)), jnp.broadcast_to(second, (1, depth)))
    for chip in range(out_ref.shape[0]):
        out_ref[chip, rows : rows + 16, :] = sums


def merge_cores(place, mine, other, sums, other_sums):
    _, rows, depth = mine[0].shape
    return pl.pallas_call(
        merge_body,
        out_shape=jax.ShapeDtypeStruct((CHIPS, rows + 16, depth), BF16),
        in_specs=[SMEM] + [VMEM] * (2 * SIDE + 2),
        out_specs=VMEM,
        compiler_params=params(),
        cost_estimate=pl.CostEstimate(
            flops=CHIPS * rows * depth, bytes_accessed=6 * CHIPS * rows * depth, transcendentals=0
        ),
        name="merge_cores",
    )(place, *mine, *other, sums, other_sums)


def finish_body(arrived_ref, update_ref, grad_input_ref, step_ref, ratio_ref):
    chips, rows, _ = arrived_ref.shape
    rows = rows - 16
    step = 16
    for low in range(0, rows, step):
        total = arrived_ref[0, low : low + step, :].astype(F32)
        for chip in range(1, chips):
            total = total + arrived_ref[chip, low : low + step, :].astype(F32)
        grad_input_ref[low : low + step, :] = total.astype(BF16)
    sums = arrived_ref[0, rows : rows + 16, 0:128].astype(F32)
    for chip in range(1, chips):
        sums = sums + arrived_ref[chip, rows : rows + 16, 0:128].astype(F32)
    weight_total = sums[0:1] + sums[2:3] + sums[4:5]
    update_total = sums[1:2] + sums[3:4] + sums[5:6]
    ratio = jnp.sqrt(weight_total) / jnp.sqrt(update_total + 1e-06)
    ratio_ref[...] = ratio
    ratio = ratio[:, 0:1]

    @pl.loop(0, update_ref.shape[0] // step)
    def _(i):
        part = pl.ds(pl.multiple_of(i * step, step), step)
        step_ref[part, :] = (ratio * update_ref[part, :]).astype(BF16)


def finish(arrived, update):
    chips, rows, depth = arrived.shape
    units = update.shape[0]
    return pl.pallas_call(
        finish_body,
        out_shape=[
            jax.ShapeDtypeStruct((rows - 16, depth), BF16),
            jax.ShapeDtypeStruct((units, depth), BF16),
            jax.ShapeDtypeStruct((1, 128), F32),
        ],
        in_specs=[VMEM] * 2,
        out_specs=[VMEM] * 3,
        compiler_params=params(),
        cost_estimate=pl.CostEstimate(
            flops=chips * rows * depth,
            bytes_accessed=2 * chips * rows * depth + 6 * units * depth,
            transcendentals=0,
        ),
        name="finish",
    )(arrived, update)


def weight_grads_body(place_ref, *refs):
    gateacts, upacts = refs[:SIDE], refs[SIDE : 2 * SIDE]
    mine_ref, other_ref, grad_gate_ref, grad_up_ref, tokens, act = refs[2 * SIDE :]
    core = place_ref[1]
    chips, half, _ = mine_ref.shape
    width = 2 * half
    for chip in range(chips):
        own = pl.multiple_of(chip * width + core * half, half)
        their = pl.multiple_of(chip * width + (1 - core) * half, half)
        tokens[pl.ds(own, half), :] = mine_ref[chip]
        tokens[pl.ds(their, half), :] = other_ref[chip]
    for acts, out_ref in ((gateacts, grad_gate_ref), (upacts, grad_up_ref)):
        for number, offsets in enumerate(GROUPS):
            for k, offset in enumerate(offsets):
                start = pl.multiple_of(owner_of(place_ref, offset) * width, width)
                act[:, pl.ds(start, width)] = acts[number][:, k * width : (k + 1) * width]
        product = lax.dot_general(
            act[...], tokens[...], (((1,), (0,)), ((), ())), preferred_element_type=F32
        )
        out_ref[...] = (product * SCALE_WIDTH).astype(BF16)


def weight_grads(place, gateacts, upacts, mine, other):
    chips, half, depth = mine.shape
    units = gateacts[0].shape[0]
    tokens = chips * half * 2
    out = jax.ShapeDtypeStruct((units, depth), BF16)
    return pl.pallas_call(
        weight_grads_body,
        out_shape=[out, out],
        in_specs=[SMEM] + [VMEM] * (2 * SIDE + 2),
        out_specs=[VMEM] * 2,
        scratch_shapes=[pltpu.VMEM((tokens, depth), BF16), pltpu.VMEM((units, tokens), BF16)],
        compiler_params=params(),
        cost_estimate=pl.CostEstimate(
            flops=4 * units * depth * tokens,
            bytes_accessed=4 * units * tokens + 2 * tokens * depth + 4 * units * depth,
            transcendentals=0,
        ),
        name="weight_grads",
    )(place, *gateacts, *upacts, mine, other)


def shards(
    tokens, cotangent, gate_pre, up_act, gate_weight, up_weight, down_weight, moment_m, moment_v
):
    z = lax.axis_index("row")
    core = lax.axis_index("col") & 1
    place = jnp.stack([z, core, 1 - 2 * core]).astype(jnp.int32)

    acts = jnp.concatenate([gate_pre.T, up_act.T], axis=0)
    acts, cotangent = lax.optimization_barrier((acts, cotangent))
    acts = lax.all_gather(acts, "row", axis=0, tiled=False)
    cot_mine, cot_other = gather_chips(cotangent)
    cotangent_all, zero, far, odd, even, give_odd, give_even = hidden_partial(
        place, cot_mine, cot_other, down_weight
    )
    tokens, _ = lax.optimization_barrier((tokens, cot_other))
    tok_mine, tok_other = gather_chips(tokens)
    swish, slope, new_m, new_v, update, sums = down_update(
        acts, cotangent_all, down_weight, moment_m, moment_v
    )
    pair = reduce_z(zero, far, odd, even, give_odd, give_even, sums)
    pair, tok_other = lax.optimization_barrier((pair, tok_other))

    gate_weight, up_weight = gate_weight.T, up_weight.T

    def group(number, before, *grads):
        return input_group(
            number, place, grads, swish, slope, gate_weight, up_weight, before
        )

    second = shift_z(pair, 2)
    third = shift_z(second, 2)
    fourth = shift_z(third, 2)
    even = jnp.stack([pair, second, third, fourth], axis=1)
    odd = shift_z(even, 1)
    far = shift_z(fourth[0], 2)
    ahead_even = swap_core(even[1, 1:])
    group_0 = group(0, jnp.zeros((16, 128), F32), even)
    group_1 = group(1, group_0[4], ahead_even)
    swapped = (swap_core(group_0[3]), swap_core(group_1[3]))
    odd, group_0, group_1, swapped = lax.optimization_barrier((odd, group_0, group_1, swapped))
    ahead_odd = swap_core(odd[1])
    group_2 = group(2, group_1[4], odd)
    group_3 = group(3, group_2[4], ahead_odd, far)
    gateacts, upacts, mine, other, sums = zip(group_0, group_1, group_2, group_3)

    swapped = (*swapped, swap_core(other[2]), swap_core(other[3]))
    merged = merge_cores(place, mine, swapped, sums[3], swap_core(sums[3]))
    merged, tok_mine = lax.optimization_barrier((merged, tok_mine))
    arrived = exchange_chips(merged)
    grad_gate, grad_up = weight_grads(place, gateacts, upacts, tok_mine, tok_other)
    arrived, grad_gate, grad_up = lax.optimization_barrier((arrived, grad_gate, grad_up))
    grad_input, step_down, ratio = finish(arrived, update)
    return grad_input, grad_gate.T, grad_up.T, new_m, new_v, step_down, ratio[0, 0]


def solution(mesh):
    in_specs = (
        P("col", "row"),
        P("col", "row"),
        P("row", "col"),
        P("row", "col"),
        P("row", "col"),
        P("row", "col"),
        P("col", "row"),
        P("col", "row"),
        P("col", "row"),
    )
    out_specs = (
        P("col", "row"),
        P("row", "col"),
        P("row", "col"),
        P("col", "row"),
        P("col", "row"),
        P("col", "row"),
        P(),
    )
    return jax.shard_map(shards, mesh=mesh, in_specs=in_specs, out_specs=out_specs, check_vma=False)
```

```python
import functools

import jax
import jax.numpy as jnp
from jax import lax
from jax.experimental import pallas as pl
from jax.experimental.pallas import tpu as pltpu
from jax.sharding import PartitionSpec as P

D = 8192
FF = 14336
Z = 16
SIDE = 4
CHIPS = 16
COLS = 32
SCALE_WIDTH = float(D) ** (-0.5)
SCALE_HIDDEN = float(FF) ** (-0.5)
BF16 = jnp.bfloat16
F32 = jnp.float32
VMEM = pl.BlockSpec(memory_space=pltpu.VMEM)
SMEM = pl.BlockSpec(memory_space=pltpu.SMEM)


def params():
    return pltpu.CompilerParams(vmem_limit_bytes=48 * 1024 * 1024)


def shift_z(v, step):
    pairs = []
    for z in range(Z):
        for col in range(COLS):
            way = step if col % 2 == 0 else -step
            pairs.append((z * COLS + col, (z + way) % Z * COLS + col))
    return lax.ppermute(v, ("row", "col"), pairs)


def swap_core(v):
    return lax.ppermute(v, "col", [(c, c ^ 1) for c in range(COLS)])


def exchange_chips(v):
    groups = [[2 * chip + core for chip in range(CHIPS)] for core in range(2)]
    return lax.all_to_all(v, "col", 0, 0, axis_index_groups=groups, tiled=True)


def gather_chips(v):
    mine = exchange_chips(jnp.broadcast_to(v[None], (CHIPS, *v.shape)))
    return mine, swap_core(mine)


def add(*terms):
    total = terms[0].astype(F32)
    for term in terms[1:]:
        total = total + term.astype(F32)
    return total.astype(BF16)


def reduce_z(zero, far, odd, even, give_odd, give_even, extra):
    own = shift_z(odd, 1)
    got_odd = swap_core(give_odd)
    their = shift_z(got_odd, 1)
    far = shift_z(far, 2)
    got_even = swap_core(give_even)
    moving_their = add(got_even[2], their[3])
    moving = add(even[2], own[3], far)
    for k in (2, 1):
        moving_their = shift_z(moving_their, 2)
        moving = shift_z(moving, 2)
        if k == 1:
            moving_their, moving, extra = lax.optimization_barrier((moving_their, moving, extra))
        moving_their = add(moving_their, got_even[k - 1], their[k])
        moving = add(moving, even[k - 1], own[k])
    moving_their = shift_z(moving_their, 2)
    moving = shift_z(moving, 2)
    other = jnp.concatenate([add(moving_their, their[0]), jnp.zeros_like(extra)], axis=0)
    mine = jnp.concatenate([add(zero, moving, own[0]), extra], axis=0)
    got_mine = swap_core(other)
    got_other = swap_core(mine)
    return add(mine, got_mine), add(other, got_other)


GROUPS = ((0, -2, -4, -6), (2, 4, 6), (-1, -3, -5, -7), (1, 3, 5, 7, -8))


def owner_of(place_ref, offset):
    z, way = place_ref[0], place_ref[2]
    return lax.rem(z + way * offset + Z, Z)


def hidden_partial_body(place_ref, mine_ref, other_ref, weight_ref, cot_ref, *refs):
    zero_ref, far_ref, odd_ref, even_ref, give_odd_ref, give_even_ref, hold = refs
    core = place_ref[1]
    chips, rows, _ = mine_ref.shape
    for chip in range(chips):
        own = pl.multiple_of(chip * 2 * rows + core * rows, rows)
        their = pl.multiple_of(chip * 2 * rows + (1 - core) * rows, rows)
        cot_ref[pl.ds(own, rows), :] = mine_ref[chip]
        cot_ref[pl.ds(their, rows), :] = other_ref[chip]
    tokens = cot_ref.shape[0]
    width = tokens // Z
    span = tokens // SIDE
    for part in range(SIDE):
        product = lax.dot_general(
            weight_ref[...],
            cot_ref[part * span : (part + 1) * span, :],
            (((1,), (1,)), ((), ())),
            preferred_element_type=F32,
        )
        hold[:, part * span : (part + 1) * span] = (product * SCALE_HIDDEN).astype(BF16)

    def block(offset):
        start = pl.multiple_of(owner_of(place_ref, offset) * width, width)
        return hold[:, pl.ds(start, width)]

    zero_ref[...] = block(0)
    far_ref[...] = block(8)
    for k, offset in enumerate((1, 3, 5, 7)):
        odd_ref[k] = block(offset)
        give_odd_ref[k] = block(-offset)
    for k, offset in enumerate((2, 4, 6)):
        even_ref[k] = block(offset)
        give_even_ref[k] = block(-offset)


def hidden_partial(place, mine, other, weight):
    units, depth = weight.shape
    tokens = mine.shape[0] * mine.shape[1] * 2
    width = tokens // Z
    shapes = [(tokens, depth), (units, width), (units, width)]
    shapes += [(count, units, width) for count in (4, 3, 4, 3)]
    return pl.pallas_call(
        hidden_partial_body,
        out_shape=[jax.ShapeDtypeStruct(shape, BF16) for shape in shapes],
        in_specs=[SMEM] + [VMEM] * 3,
        out_specs=[VMEM] * 7,
        scratch_shapes=[pltpu.VMEM((units, tokens), BF16)],
        compiler_params=params(),
        cost_estimate=pl.CostEstimate(
            flops=2 * units * depth * tokens,
            bytes_accessed=2 * (2 * tokens * depth + units * depth + units * tokens),
            transcendentals=0,
        ),
        name="hidden_partial",
    )(place, mine, other, weight)


def down_body(acts_ref, cot_ref, weight_ref, m_ref, v_ref, *refs):
    swish_ref, slope_ref, new_m_ref, new_v_ref, update_ref, sums_ref = refs[:6]
    hidden, product = refs[6:]
    blocks, units, width = acts_ref.shape
    units = units // 2
    chunk = 64
    for k in range(blocks):
        cols = slice(k * width, (k + 1) * width)

        @pl.loop(0, units // chunk)
        def _(i, k=k, cols=cols):
            low = pl.multiple_of(i * chunk, chunk)
            rows = pl.ds(low, chunk)
            g = acts_ref[k, rows, :].astype(F32)
            u = acts_ref[k, pl.ds(low + units, chunk), :].astype(F32)
            s = jax.nn.sigmoid(g)
            swish = g * s
            slope = u * s * (1.0 + g * (1.0 - s))
            hidden[rows, cols] = (swish * u).astype(BF16)
            swish_ref[rows, cols] = swish.astype(BF16)
            slope_ref[rows, cols] = slope.astype(BF16)

    product[...] = lax.dot_general(
        hidden[...], cot_ref[...], (((1,), (0,)), ((), ())), preferred_element_type=F32
    )
    step = 16
    depth = product.shape[1]

    def optimizer(i, carry):
        weight_sum, update_sum = carry
        rows = pl.ds(pl.multiple_of(i * step, step), step)
        grad = product[rows, :] * SCALE_HIDDEN
        weight = weight_ref[rows, :].astype(F32)
        first = 0.9 * m_ref[rows, :].astype(F32) + 0.1 * grad
        second = 0.95 * v_ref[rows, :].astype(F32) + 0.05 * grad * grad
        update = first / (jnp.sqrt(second) + 1e-08) + 0.1 * weight
        new_m_ref[rows, :] = first.astype(BF16)
        new_v_ref[rows, :] = second.astype(BF16)
        update_ref[rows, :] = update
        return weight_sum + weight * weight, update_sum + update * update

    zero = jnp.zeros((step, depth), F32)
    weight_sum, update_sum = lax.fori_loop(0, units // step, optimizer, (zero, zero))
    weight_sum = jnp.sum(weight_sum, axis=0, keepdims=True)
    update_sum = jnp.sum(update_sum, axis=0, keepdims=True)
    lanes = sums_ref.shape[1]
    parts = [slice(k, k + lanes) for k in range(0, depth, lanes)]
    weight_sum = sum(weight_sum[:, part] for part in parts)
    update_sum = sum(update_sum[:, part] for part in parts)
    sums_ref[...] = in_rows(weight_sum, update_sum)


def in_rows(first, second):
    row = lax.broadcasted_iota(jnp.int32, (16, first.shape[1]), 0)
    value = jnp.where((row & 1) == 0, first, second)
    high = value.astype(BF16).astype(F32)
    middle = (value - high).astype(BF16).astype(F32)
    low = value - high - middle
    rest = jnp.where(row < 4, middle, jnp.where(row < 6, low, 0.0))
    return jnp.where(row < 2, high, rest).astype(BF16)


def from_rows(rows):
    first = rows[0:1] + rows[2:3] + rows[4:5]
    second = rows[1:2] + rows[3:4] + rows[5:6]
    return jnp.sum(first, axis=1, keepdims=True), jnp.sum(second, axis=1, keepdims=True)


def down_update(acts, cotangent, weight, moment_m, moment_v):
    units = acts.shape[1] // 2
    tokens, depth = cotangent.shape
    shapes = [
        jax.ShapeDtypeStruct((units, tokens), BF16),
        jax.ShapeDtypeStruct((units, tokens), BF16),
        jax.ShapeDtypeStruct((units, depth), BF16),
        jax.ShapeDtypeStruct((units, depth), BF16),
        jax.ShapeDtypeStruct((units, depth), F32),
        jax.ShapeDtypeStruct((16, 128), BF16),
    ]
    return pl.pallas_call(
        down_body,
        out_shape=shapes,
        in_specs=[VMEM] * 5,
        out_specs=[VMEM] * 6,
        scratch_shapes=[pltpu.VMEM((units, tokens), BF16), pltpu.VMEM((units, depth), F32)],
        compiler_params=params(),
        cost_estimate=pl.CostEstimate(
            flops=2 * units * depth * tokens + 30 * units * tokens,
            bytes_accessed=8 * units * tokens + 2 * tokens * depth + 14 * units * depth,
            transcendentals=units * tokens,
        ),
        name="down_update",
    )(acts, cotangent, weight, moment_m, moment_v)


def group_body(number, count, place_ref, *refs):
    grads = refs[:count]
    swish_ref, slope_ref, gate_weight_ref, up_weight_ref, before_ref = refs[count : count + 5]
    gateact_ref, upact_ref, mine_ref, other_ref, sums_ref, hold = refs[count + 5 :]
    units = gateact_ref.shape[0]
    blocks, half, _ = mine_ref.shape
    width = 2 * half
    chunk = 64
    core = place_ref[1]

    def block(k, rows):
        if k == 4:
            return grads[1][rows, :].astype(F32)
        return grads[0][k, rows, :].astype(F32)

    sums = before_ref[...]
    for k in range(blocks):
        sums = sums + block(k, slice(units, units + 16))
    sums_ref[...] = sums
    for k, offset in enumerate(GROUPS[number]):
        start = pl.multiple_of(owner_of(place_ref, offset) * width, width)
        cols = slice(k * width, (k + 1) * width)

        @pl.loop(0, units // chunk)
        def _(i, k=k, start=start, cols=cols):
            rows = pl.ds(pl.multiple_of(i * chunk, chunk), chunk)
            grad = block(k, rows)
            swish = swish_ref[rows, pl.ds(start, width)].astype(F32)
            slope = slope_ref[rows, pl.ds(start, width)].astype(F32)
            upact_ref[rows, cols] = (grad * swish).astype(BF16)
            gateact_ref[rows, cols] = (grad * slope).astype(BF16)

    contract_first = (((0,), (0,)), ((), ()))
    product = lax.dot_general(
        gateact_ref[...], gate_weight_ref[...], contract_first, preferred_element_type=F32
    )
    product = product + lax.dot_general(
        upact_ref[...], up_weight_ref[...], contract_first, preferred_element_type=F32
    )
    hold[...] = (product * SCALE_WIDTH).astype(BF16)
    for k in range(blocks):
        own = pl.multiple_of(k * width + core * half, half)
        their = pl.multiple_of(k * width + (1 - core) * half, half)
        mine_ref[k] = hold[pl.ds(own, half), :]
        other_ref[k] = hold[pl.ds(their, half), :]


def input_group(number, place, grads, swish, slope, gate_weight, up_weight, before):
    units, tokens = swish.shape
    depth = gate_weight.shape[1]
    width = tokens // Z
    blocks = len(GROUPS[number])
    half = jax.ShapeDtypeStruct((blocks, width // 2, depth), BF16)
    acts = jax.ShapeDtypeStruct((units, blocks * width), BF16)
    sums = jax.ShapeDtypeStruct((16, 128), F32)
    return pl.pallas_call(
        functools.partial(group_body, number, len(grads)),
        out_shape=[acts, acts, half, half, sums],
        in_specs=[SMEM] + [VMEM] * (5 + len(grads)),
        out_specs=[VMEM] * 5,
        scratch_shapes=[pltpu.VMEM((blocks * width, depth), BF16)],
        compiler_params=params(),
        cost_estimate=pl.CostEstimate(
            flops=4 * units * depth * blocks * width,
            bytes_accessed=10 * units * blocks * width + 4 * units * depth,
            transcendentals=0,
        ),
        name="input_group",
    )(place, *grads, swish, slope, gate_weight, up_weight, before)


def merge_body(place_ref, *refs):
    mine, other = refs[:SIDE], refs[SIDE : 2 * SIDE]
    sums_ref, other_sums_ref, out_ref = refs[2 * SIDE :]
    rows = mine[0].shape[1]
    for number, offsets in enumerate(GROUPS):
        for k, offset in enumerate(offsets):
            out_ref[owner_of(place_ref, offset), 0:rows, :] = mine[number][k]
    for number, offsets in enumerate(GROUPS):
        for k, offset in enumerate(offsets):
            chip = owner_of(place_ref, -offset)
            total = out_ref[chip, 0:rows, :].astype(F32) + other[number][k].astype(F32)
            out_ref[chip, 0:rows, :] = total.astype(BF16)
    first, second = from_rows(sums_ref[...] + other_sums_ref[...])
    depth = out_ref.shape[2]
    sums = in_rows(jnp.broadcast_to(first, (1, depth)), jnp.broadcast_to(second, (1, depth)))
    for chip in range(out_ref.shape[0]):
        out_ref[chip, rows : rows + 16, :] = sums


def merge_cores(place, mine, other, sums, other_sums):
    _, rows, depth = mine[0].shape
    return pl.pallas_call(
        merge_body,
        out_shape=jax.ShapeDtypeStruct((CHIPS, rows + 16, depth), BF16),
        in_specs=[SMEM] + [VMEM] * (2 * SIDE + 2),
        out_specs=VMEM,
        compiler_params=params(),
        cost_estimate=pl.CostEstimate(
            flops=CHIPS * rows * depth, bytes_accessed=6 * CHIPS * rows * depth, transcendentals=0
        ),
        name="merge_cores",
    )(place, *mine, *other, sums, other_sums)


def finish_body(arrived_ref, update_ref, grad_input_ref, step_ref, ratio_ref):
    chips, rows, _ = arrived_ref.shape
    rows = rows - 16
    step = 16
    for low in range(0, rows, step):
        total = arrived_ref[0, low : low + step, :].astype(F32)
        for chip in range(1, chips):
            total = total + arrived_ref[chip, low : low + step, :].astype(F32)
        grad_input_ref[low : low + step, :] = total.astype(BF16)
    sums = arrived_ref[0, rows : rows + 16, 0:128].astype(F32)
    for chip in range(1, chips):
        sums = sums + arrived_ref[chip, rows : rows + 16, 0:128].astype(F32)
    weight_total = sums[0:1] + sums[2:3] + sums[4:5]
    update_total = sums[1:2] + sums[3:4] + sums[5:6]
    ratio = jnp.sqrt(weight_total) / jnp.sqrt(update_total + 1e-06)
    ratio_ref[...] = ratio
    ratio = ratio[:, 0:1]

    @pl.loop(0, update_ref.shape[0] // step)
    def _(i):
        part = pl.ds(pl.multiple_of(i * step, step), step)
        step_ref[part, :] = (ratio * update_ref[part, :]).astype(BF16)


def finish(arrived, update):
    chips, rows, depth = arrived.shape
    units = update.shape[0]
    return pl.pallas_call(
        finish_body,
        out_shape=[
            jax.ShapeDtypeStruct((rows - 16, depth), BF16),
            jax.ShapeDtypeStruct((units, depth), BF16),
            jax.ShapeDtypeStruct((1, 128), F32),
        ],
        in_specs=[VMEM] * 2,
        out_specs=[VMEM] * 3,
        compiler_params=params(),
        cost_estimate=pl.CostEstimate(
            flops=chips * rows * depth,
            bytes_accessed=2 * chips * rows * depth + 6 * units * depth,
            transcendentals=0,
        ),
        name="finish",
    )(arrived, update)


def weight_grads_body(place_ref, *refs):
    gateacts, upacts = refs[:SIDE], refs[SIDE : 2 * SIDE]
    mine_ref, other_ref, grad_gate_ref, grad_up_ref, tokens, act = refs[2 * SIDE :]
    core = place_ref[1]
    chips, half, _ = mine_ref.shape
    width = 2 * half
    for chip in range(chips):
        own = pl.multiple_of(chip * width + core * half, half)
        their = pl.multiple_of(chip * width + (1 - core) * half, half)
        tokens[pl.ds(own, half), :] = mine_ref[chip]
        tokens[pl.ds(their, half), :] = other_ref[chip]
    for acts, out_ref in ((gateacts, grad_gate_ref), (upacts, grad_up_ref)):
        for number, offsets in enumerate(GROUPS):
            for k, offset in enumerate(offsets):
                start = pl.multiple_of(owner_of(place_ref, offset) * width, width)
                act[:, pl.ds(start, width)] = acts[number][:, k * width : (k + 1) * width]
        product = lax.dot_general(
            act[...], tokens[...], (((1,), (0,)), ((), ())), preferred_element_type=F32
        )
        out_ref[...] = (product * SCALE_WIDTH).astype(BF16)


def weight_grads(place, gateacts, upacts, mine, other):
    chips, half, depth = mine.shape
    units = gateacts[0].shape[0]
    tokens = chips * half * 2
    out = jax.ShapeDtypeStruct((units, depth), BF16)
    return pl.pallas_call(
        weight_grads_body,
        out_shape=[out, out],
        in_specs=[SMEM] + [VMEM] * (2 * SIDE + 2),
        out_specs=[VMEM] * 2,
        scratch_shapes=[pltpu.VMEM((tokens, depth), BF16), pltpu.VMEM((units, tokens), BF16)],
        compiler_params=params(),
        cost_estimate=pl.CostEstimate(
            flops=4 * units * depth * tokens,
            bytes_accessed=4 * units * tokens + 2 * tokens * depth + 4 * units * depth,
            transcendentals=0,
        ),
        name="weight_grads",
    )(place, *gateacts, *upacts, mine, other)


def shards(
    tokens, cotangent, gate_pre, up_act, gate_weight, up_weight, down_weight, moment_m, moment_v
):
    z = lax.axis_index("row")
    core = lax.axis_index("col") & 1
    place = jnp.stack([z, core, 1 - 2 * core]).astype(jnp.int32)

    acts = jnp.concatenate([gate_pre.T, up_act.T], axis=0)
    acts, cotangent = lax.optimization_barrier((acts, cotangent))
    acts = lax.all_gather(acts, "row", axis=0, tiled=False)
    cot_mine, cot_other = gather_chips(cotangent)
    cotangent_all, zero, far, odd, even, give_odd, give_even = hidden_partial(
        place, cot_mine, cot_other, down_weight
    )
    tokens, _ = lax.optimization_barrier((tokens, cot_other))
    tok_mine, tok_other = gather_chips(tokens)
    swish, slope, new_m, new_v, update, sums = down_update(
        acts, cotangent_all, down_weight, moment_m, moment_v
    )
    own, other = reduce_z(zero, far, odd, even, give_odd, give_even, sums)
    own, tok_other = lax.optimization_barrier((own, tok_other))

    gate_weight, up_weight = gate_weight.T, up_weight.T

    def group(number, before, *grads):
        return input_group(
            number, place, grads, swish, slope, gate_weight, up_weight, before
        )

    others, owns = [other], [own]
    for _ in range(3):
        others.append(shift_z(others[-1], 2))
        owns.append(shift_z(owns[-1], 2))
    even_other, even = jnp.stack(others), jnp.stack(owns)
    odd_other = shift_z(even_other, 1)
    odd = shift_z(even, 1)
    far = shift_z(owns[3], 2)
    ahead_even = swap_core(even_other[1:])
    group_0 = group(0, jnp.zeros((16, 128), F32), even)
    group_1 = group(1, group_0[4], ahead_even)
    swapped = (swap_core(group_0[3]), swap_core(group_1[3]))
    odd_other, odd, far, group_0, group_1, swapped = lax.optimization_barrier(
        (odd_other, odd, far, group_0, group_1, swapped)
    )
    ahead_odd = swap_core(odd_other)
    group_2 = group(2, group_1[4], odd)
    group_3 = group(3, group_2[4], ahead_odd, far)
    gateacts, upacts, mine, other, sums = zip(group_0, group_1, group_2, group_3)

    swapped = (*swapped, swap_core(other[2]), swap_core(other[3]))
    merged = merge_cores(place, mine, swapped, sums[3], swap_core(sums[3]))
    merged, tok_mine = lax.optimization_barrier((merged, tok_mine))
    arrived = exchange_chips(merged)
    grad_gate, grad_up = weight_grads(place, gateacts, upacts, tok_mine, tok_other)
    arrived, grad_gate, grad_up = lax.optimization_barrier((arrived, grad_gate, grad_up))
    grad_input, step_down, ratio = finish(arrived, update)
    return grad_input, grad_gate.T, grad_up.T, new_m, new_v, step_down, ratio[0, 0]


def solution(mesh):
    in_specs = (
        P("col", "row"),
        P("col", "row"),
        P("row", "col"),
        P("row", "col"),
        P("row", "col"),
        P("row", "col"),
        P("col", "row"),
        P("col", "row"),
        P("col", "row"),
    )
    out_specs = (
        P("col", "row"),
        P("row", "col"),
        P("row", "col"),
        P("col", "row"),
        P("col", "row"),
        P("col", "row"),
        P(),
    )
    return jax.shard_map(shards, mesh=mesh, in_specs=in_specs, out_specs=out_specs, check_vma=False)
```

```python
import functools

import jax
import jax.numpy as jnp
from jax import lax
from jax.experimental import pallas as pl
from jax.experimental.pallas import tpu as pltpu
from jax.sharding import PartitionSpec as P

D = 8192
FF = 14336
Z = 16
SIDE = 4
CHIPS = 16
COLS = 32
SCALE_WIDTH = float(D) ** (-0.5)
SCALE_HIDDEN = float(FF) ** (-0.5)
BF16 = jnp.bfloat16
F32 = jnp.float32
VMEM = pl.BlockSpec(memory_space=pltpu.VMEM)
SMEM = pl.BlockSpec(memory_space=pltpu.SMEM)


def params():
    return pltpu.CompilerParams(vmem_limit_bytes=20 * 1024 * 1024)


def shift_z(v, step):
    pairs = []
    for z in range(Z):
        for col in range(COLS):
            way = step if col % 2 == 0 else -step
            pairs.append((z * COLS + col, (z + way) % Z * COLS + col))
    return lax.ppermute(v, ("row", "col"), pairs)


def swap_core(v):
    return lax.ppermute(v, "col", [(c, c ^ 1) for c in range(COLS)])


def exchange_chips(v):
    groups = [[2 * chip + core for chip in range(CHIPS)] for core in range(2)]
    return lax.all_to_all(v, "col", 0, 0, axis_index_groups=groups, tiled=True)


def gather_chips(v):
    mine = exchange_chips(jnp.broadcast_to(v[None], (CHIPS, *v.shape)))
    return mine, swap_core(mine)


def add(*terms):
    total = terms[0].astype(F32)
    for term in terms[1:]:
        total = total + term.astype(F32)
    return total.astype(BF16)


def reduce_z(zero, far, odd, even, give_odd, give_even, extra):
    own = shift_z(odd, 1)
    got_odd = swap_core(give_odd)
    their = shift_z(got_odd, 1)
    far = shift_z(far, SIDE)
    got_even = swap_core(give_even)
    moving_their = add(got_even[2], their[3])
    moving = add(even[2], own[3])
    for k in (2, 1):
        moving_their = shift_z(moving_their, 2)
        moving = shift_z(moving, 2)
        if k == 1:
            moving_their, moving, extra = lax.optimization_barrier((moving_their, moving, extra))
        moving_their = add(moving_their, got_even[k - 1], their[k])
        moving = add(moving, even[k - 1], own[k], *([far] if k == 2 else []))
    moving_their = shift_z(moving_their, 2)
    moving = shift_z(moving, 2)
    other = jnp.concatenate([add(moving_their, their[0]), jnp.zeros_like(extra)], axis=0)
    mine = jnp.concatenate([add(zero, moving, own[0]), extra], axis=0)
    got_mine = swap_core(other)
    got_other = swap_core(mine)
    return add(mine, got_mine), add(other, got_other)


GROUPS = ((0, -2, -4, -6), (2, 4, 6), (-1, -3, -5, -7), (1, 3, 5, 7, -8))


def owner_of(place_ref, offset):
    z, way = place_ref[0], place_ref[2]
    return lax.rem(z + way * offset + Z, Z)


def hidden_partial_body(place_ref, mine_ref, other_ref, weight_ref, cot_ref, *refs):
    zero_ref, far_ref, odd_ref, even_ref, give_odd_ref, give_even_ref, hold = refs
    core = place_ref[1]
    chips, rows, _ = mine_ref.shape
    for chip in range(chips):
        own = pl.multiple_of(chip * 2 * rows + core * rows, rows)
        their = pl.multiple_of(chip * 2 * rows + (1 - core) * rows, rows)
        cot_ref[pl.ds(own, rows), :] = mine_ref[chip]
        cot_ref[pl.ds(their, rows), :] = other_ref[chip]
    tokens = cot_ref.shape[0]
    width = tokens // Z
    span = tokens // SIDE
    for part in range(SIDE):
        product = lax.dot_general(
            weight_ref[...],
            cot_ref[part * span : (part + 1) * span, :],
            (((1,), (1,)), ((), ())),
            preferred_element_type=F32,
        )
        hold[:, part * span : (part + 1) * span] = (product * SCALE_HIDDEN).astype(BF16)

    def block(offset):
        start = pl.multiple_of(owner_of(place_ref, offset) * width, width)
        return hold[:, pl.ds(start, width)]

    zero_ref[...] = block(0)
    far_ref[...] = block(8)
    for k, offset in enumerate((1, 3, 5, 7)):
        odd_ref[k] = block(offset)
        give_odd_ref[k] = block(-offset)
    for k, offset in enumerate((2, 4, 6)):
        even_ref[k] = block(offset)
        give_even_ref[k] = block(-offset)


def hidden_partial(place, mine, other, weight):
    units, depth = weight.shape
    tokens = mine.shape[0] * mine.shape[1] * 2
    width = tokens // Z
    shapes = [(tokens, depth), (units, width), (units, width)]
    shapes += [(count, units, width) for count in (4, 3, 4, 3)]
    return pl.pallas_call(
        hidden_partial_body,
        out_shape=[jax.ShapeDtypeStruct(shape, BF16) for shape in shapes],
        in_specs=[SMEM] + [VMEM] * 3,
        out_specs=[VMEM] * 7,
        scratch_shapes=[pltpu.VMEM((units, tokens), BF16)],
        compiler_params=params(),
        cost_estimate=pl.CostEstimate(
            flops=2 * units * depth * tokens,
            bytes_accessed=2 * (2 * tokens * depth + units * depth + units * tokens),
            transcendentals=0,
        ),
        name="hidden_partial",
    )(place, mine, other, weight)


def down_body(acts_ref, cot_ref, weight_ref, m_ref, v_ref, *refs):
    swish_ref, slope_ref, new_m_ref, new_v_ref, update_ref, sums_ref = refs[:6]
    hidden, product = refs[6:]
    blocks, units, width = acts_ref.shape
    units = units // 2
    chunk = 64
    for k in range(blocks):
        cols = slice(k * width, (k + 1) * width)

        @pl.loop(0, units // chunk)
        def _(i, k=k, cols=cols):
            low = pl.multiple_of(i * chunk, chunk)
            rows = pl.ds(low, chunk)
            g = acts_ref[k, rows, :].astype(F32)
            u = acts_ref[k, pl.ds(low + units, chunk), :].astype(F32)
            s = jax.nn.sigmoid(g)
            swish = g * s
            slope = u * s * (1.0 + g * (1.0 - s))
            hidden[rows, cols] = (swish * u).astype(BF16)
            swish_ref[rows, cols] = swish.astype(BF16)
            slope_ref[rows, cols] = slope.astype(BF16)

    product[...] = lax.dot_general(
        hidden[...], cot_ref[...], (((1,), (0,)), ((), ())), preferred_element_type=F32
    )
    step = 16
    depth = product.shape[1]

    def optimizer(i, carry):
        weight_sum, update_sum = carry
        rows = pl.ds(pl.multiple_of(i * step, step), step)
        grad = product[rows, :] * SCALE_HIDDEN
        weight = weight_ref[rows, :].astype(F32)
        first = 0.9 * m_ref[rows, :].astype(F32) + 0.1 * grad
        second = 0.95 * v_ref[rows, :].astype(F32) + 0.05 * grad * grad
        update = first / (jnp.sqrt(second) + 1e-08) + 0.1 * weight
        new_m_ref[rows, :] = first.astype(BF16)
        new_v_ref[rows, :] = second.astype(BF16)
        update_ref[rows, :] = update
        return weight_sum + weight * weight, update_sum + update * update

    zero = jnp.zeros((step, depth), F32)
    weight_sum, update_sum = lax.fori_loop(0, units // step, optimizer, (zero, zero))
    weight_sum = jnp.sum(weight_sum, axis=0, keepdims=True)
    update_sum = jnp.sum(update_sum, axis=0, keepdims=True)
    lanes = sums_ref.shape[1]
    parts = [slice(k, k + lanes) for k in range(0, depth, lanes)]
    weight_sum = sum(weight_sum[:, part] for part in parts)
    update_sum = sum(update_sum[:, part] for part in parts)
    sums_ref[...] = in_rows(weight_sum, update_sum)


def in_rows(first, second):
    row = lax.broadcasted_iota(jnp.int32, (16, first.shape[1]), 0)
    value = jnp.where((row & 1) == 0, first, second)
    high = value.astype(BF16).astype(F32)
    middle = (value - high).astype(BF16).astype(F32)
    low = value - high - middle
    rest = jnp.where(row < 4, middle, jnp.where(row < 6, low, 0.0))
    return jnp.where(row < 2, high, rest).astype(BF16)


def from_rows(rows):
    first = rows[0:1] + rows[2:3] + rows[4:5]
    second = rows[1:2] + rows[3:4] + rows[5:6]
    return jnp.sum(first, axis=1, keepdims=True), jnp.sum(second, axis=1, keepdims=True)


def down_update(acts, cotangent, weight, moment_m, moment_v):
    units = acts.shape[1] // 2
    tokens, depth = cotangent.shape
    shapes = [
        jax.ShapeDtypeStruct((units, tokens), BF16),
        jax.ShapeDtypeStruct((units, tokens), BF16),
        jax.ShapeDtypeStruct((units, depth), BF16),
        jax.ShapeDtypeStruct((units, depth), BF16),
        jax.ShapeDtypeStruct((units, depth), F32),
        jax.ShapeDtypeStruct((16, 128), BF16),
    ]
    return pl.pallas_call(
        down_body,
        out_shape=shapes,
        in_specs=[VMEM] * 5,
        out_specs=[VMEM] * 6,
        scratch_shapes=[pltpu.VMEM((units, tokens), BF16), pltpu.VMEM((units, depth), F32)],
        compiler_params=params(),
        cost_estimate=pl.CostEstimate(
            flops=2 * units * depth * tokens + 30 * units * tokens,
            bytes_accessed=8 * units * tokens + 2 * tokens * depth + 14 * units * depth,
            transcendentals=units * tokens,
        ),
        name="down_update",
    )(acts, cotangent, weight, moment_m, moment_v)


def group_body(number, count, place_ref, *refs):
    grads = refs[:count]
    swish_ref, slope_ref, gate_weight_ref, up_weight_ref = refs[count : count + 4]
    befores = refs[count + 4 : -6]
    gateact_ref, upact_ref, mine_ref, other_ref, sums_ref, hold = refs[-6:]
    units = gateact_ref.shape[0]
    blocks, half, _ = mine_ref.shape
    width = 2 * half
    chunk = 64
    core = place_ref[1]

    def block(k, rows):
        if k == 4:
            return grads[1][rows, :].astype(F32)
        return grads[0][k, rows, :].astype(F32)

    sums = befores[0][...] if befores else 0.0
    for k in range(blocks):
        sums = sums + block(k, slice(units, units + 16))
    sums_ref[...] = sums
    for k, offset in enumerate(GROUPS[number]):
        start = pl.multiple_of(owner_of(place_ref, offset) * width, width)
        cols = slice(k * width, (k + 1) * width)

        @pl.loop(0, units // chunk)
        def _(i, k=k, start=start, cols=cols):
            rows = pl.ds(pl.multiple_of(i * chunk, chunk), chunk)
            grad = block(k, rows)
            swish = swish_ref[rows, pl.ds(start, width)].astype(F32)
            slope = slope_ref[rows, pl.ds(start, width)].astype(F32)
            upact_ref[rows, cols] = (grad * swish).astype(BF16)
            gateact_ref[rows, cols] = (grad * slope).astype(BF16)

    contract_first = (((0,), (0,)), ((), ()))
    product = lax.dot_general(
        gateact_ref[...], gate_weight_ref[...], contract_first, preferred_element_type=F32
    )
    product = product + lax.dot_general(
        upact_ref[...], up_weight_ref[...], contract_first, preferred_element_type=F32
    )
    hold[...] = (product * SCALE_WIDTH).astype(BF16)
    for k in range(blocks):
        own = pl.multiple_of(k * width + core * half, half)
        their = pl.multiple_of(k * width + (1 - core) * half, half)
        mine_ref[k] = hold[pl.ds(own, half), :]
        low = other_ref.shape[0] - (blocks - k) * half - (16 if number == 3 else 0)
        other_ref[low : low + half, :] = hold[pl.ds(their, half), :]
    if number == 3:
        other_ref[blocks * half :, :] = jnp.zeros((16, other_ref.shape[1]), BF16)
        first = sums[0:1] + sums[2:3] + sums[4:5]
        second = sums[1:2] + sums[3:4] + sums[5:6]
        other_ref[blocks * half :, 0:128] = in_rows(first, second)
    elif number > 0:
        earlier = befores[1].shape[0]
        other_ref[0:earlier, :] = befores[1][...]


def input_group(number, place, grads, swish, slope, gate_weight, up_weight, *befores):
    units, tokens = swish.shape
    depth = gate_weight.shape[1]
    width = tokens // Z
    blocks = len(GROUPS[number])
    half = jax.ShapeDtypeStruct((blocks, width // 2, depth), BF16)
    if number == 3:
        other_rows = blocks * width // 2 + 16
    else:
        other_rows = sum(len(offsets) for offsets in GROUPS[: number + 1]) * width // 2
    other = jax.ShapeDtypeStruct((other_rows, depth), BF16)
    acts = jax.ShapeDtypeStruct((units, blocks * width), BF16)
    sums = jax.ShapeDtypeStruct((16, 128), F32)
    return pl.pallas_call(
        functools.partial(group_body, number, len(grads)),
        out_shape=[acts, acts, half, other, sums],
        in_specs=[SMEM] + [VMEM] * (4 + len(grads) + len(befores)),
        out_specs=[VMEM] * 5,
        scratch_shapes=[pltpu.VMEM((blocks * width, depth), BF16)],
        compiler_params=params(),
        cost_estimate=pl.CostEstimate(
            flops=4 * units * depth * blocks * width,
            bytes_accessed=10 * units * blocks * width + 4 * units * depth,
            transcendentals=0,
        ),
        name="input_group",
    )(place, *grads, swish, slope, gate_weight, up_weight, *befores)


def merge_body(place_ref, *refs):
    mine = refs[:SIDE]
    first_other_ref, last_other_ref, sums_ref, out_ref = refs[SIDE:]
    rows, depth = mine[0].shape[1:]
    parts = [(q * rows, slice(q * 128, (q + 1) * 128)) for q in range(depth // 128)]
    for number, offsets in enumerate(GROUPS):
        for k, offset in enumerate(offsets):
            chip = owner_of(place_ref, offset)
            for low, cols in parts:
                out_ref[chip, low : low + rows, :] = mine[number][k, :, cols]
    first = [offset for offsets in GROUPS[:3] for offset in offsets]
    for ref, offsets in ((first_other_ref, first), (last_other_ref, GROUPS[3])):
        for k, offset in enumerate(offsets):
            chip = owner_of(place_ref, -offset)
            for low, cols in parts:
                total = out_ref[chip, low : low + rows, :].astype(F32)
                total = total + ref[k * rows : (k + 1) * rows, cols].astype(F32)
                out_ref[chip, low : low + rows, :] = total.astype(BF16)
    their = last_other_ref[len(GROUPS[3]) * rows :, 0:128].astype(F32)
    first, second = from_rows(sums_ref[...] + their)
    sums = in_rows(jnp.broadcast_to(first, (1, 128)), jnp.broadcast_to(second, (1, 128)))
    for chip in range(out_ref.shape[0]):
        out_ref[chip, len(parts) * rows :, :] = sums


def merge_cores(place, mine, first_other, last_other, sums):
    _, rows, depth = mine[0].shape
    return pl.pallas_call(
        merge_body,
        out_shape=jax.ShapeDtypeStruct((CHIPS, rows * depth // 128 + 16, 128), BF16),
        in_specs=[SMEM] + [VMEM] * (SIDE + 3),
        out_specs=VMEM,
        compiler_params=params(),
        cost_estimate=pl.CostEstimate(
            flops=CHIPS * rows * depth, bytes_accessed=6 * CHIPS * rows * depth, transcendentals=0
        ),
        name="merge_cores",
    )(place, *mine, first_other, last_other, sums)


def finish_body(arrived_ref, update_ref, grad_input_ref, step_ref, ratio_ref):
    chips = arrived_ref.shape[0]
    rows, depth = grad_input_ref.shape
    for q in range(depth // 128):
        for low in range(0, rows, 32):
            part = slice(q * rows + low, q * rows + low + 32)
            total = arrived_ref[0, part, :].astype(F32)
            for chip in range(1, chips):
                total = total + arrived_ref[chip, part, :].astype(F32)
            grad_input_ref[low : low + 32, q * 128 : (q + 1) * 128] = total.astype(BF16)
    part = slice(rows * depth // 128, rows * depth // 128 + 16)
    sums = arrived_ref[0, part, :].astype(F32)
    for chip in range(1, chips):
        sums = sums + arrived_ref[chip, part, :].astype(F32)
    weight_total = sums[0:1] + sums[2:3] + sums[4:5]
    update_total = sums[1:2] + sums[3:4] + sums[5:6]
    ratio = jnp.sqrt(weight_total) / jnp.sqrt(update_total + 1e-06)
    ratio_ref[...] = ratio
    ratio = ratio[:, 0:1]
    step = 16

    @pl.loop(0, update_ref.shape[0] // step)
    def _(i):
        part = pl.ds(pl.multiple_of(i * step, step), step)
        step_ref[part, :] = (ratio * update_ref[part, :]).astype(BF16)


def finish(arrived, update):
    chips, rows, _ = arrived.shape
    units, depth = update.shape
    return pl.pallas_call(
        finish_body,
        out_shape=[
            jax.ShapeDtypeStruct(((rows - 16) * 128 // depth, depth), BF16),
            jax.ShapeDtypeStruct((units, depth), BF16),
            jax.ShapeDtypeStruct((1, 128), F32),
        ],
        in_specs=[VMEM] * 2,
        out_specs=[VMEM] * 3,
        compiler_params=params(),
        cost_estimate=pl.CostEstimate(
            flops=chips * rows * 128,
            bytes_accessed=2 * chips * rows * 128 + 6 * units * depth,
            transcendentals=0,
        ),
        name="finish",
    )(arrived, update)


def weight_grads_body(place_ref, *refs):
    gateacts, upacts = refs[:SIDE], refs[SIDE : 2 * SIDE]
    mine_ref, other_ref, grad_gate_ref, grad_up_ref, tokens, act = refs[2 * SIDE :]
    core = place_ref[1]
    chips, half, _ = mine_ref.shape
    width = 2 * half
    for chip in range(chips):
        own = pl.multiple_of(chip * width + core * half, half)
        their = pl.multiple_of(chip * width + (1 - core) * half, half)
        tokens[pl.ds(own, half), :] = mine_ref[chip]
        tokens[pl.ds(their, half), :] = other_ref[chip]
    for acts, out_ref in ((gateacts, grad_gate_ref), (upacts, grad_up_ref)):
        for number, offsets in enumerate(GROUPS):
            for k, offset in enumerate(offsets):
                start = pl.multiple_of(owner_of(place_ref, offset) * width, width)
                act[:, pl.ds(start, width)] = acts[number][:, k * width : (k + 1) * width]
        product = lax.dot_general(
            act[...], tokens[...], (((1,), (0,)), ((), ())), preferred_element_type=F32
        )
        out_ref[...] = (product * SCALE_WIDTH).astype(BF16)


def weight_grads(place, gateacts, upacts, mine, other):
    chips, half, depth = mine.shape
    units = gateacts[0].shape[0]
    tokens = chips * half * 2
    out = jax.ShapeDtypeStruct((units, depth), BF16)
    return pl.pallas_call(
        weight_grads_body,
        out_shape=[out, out],
        in_specs=[SMEM] + [VMEM] * (2 * SIDE + 2),
        out_specs=[VMEM] * 2,
        scratch_shapes=[pltpu.VMEM((tokens, depth), BF16), pltpu.VMEM((units, tokens), BF16)],
        compiler_params=params(),
        cost_estimate=pl.CostEstimate(
            flops=4 * units * depth * tokens,
            bytes_accessed=4 * units * tokens + 2 * tokens * depth + 4 * units * depth,
            transcendentals=0,
        ),
        name="weight_grads",
    )(place, *gateacts, *upacts, mine, other)


def shards(
    tokens, cotangent, gate_pre, up_act, gate_weight, up_weight, down_weight, moment_m, moment_v
):
    z = lax.axis_index("row")
    core = lax.axis_index("col") & 1
    place = jnp.stack([z, core, 1 - 2 * core]).astype(jnp.int32)

    acts = jnp.concatenate([gate_pre.T, up_act.T], axis=0)
    acts, cotangent = lax.optimization_barrier((acts, cotangent))
    acts = lax.all_gather(acts, "row", axis=0, tiled=False)
    cot_mine, cot_other = gather_chips(cotangent)
    cotangent_all, zero, far, odd, even, give_odd, give_even = hidden_partial(
        place, cot_mine, cot_other, down_weight
    )
    tokens, _ = lax.optimization_barrier((tokens, cot_other))
    tok_mine, tok_other = gather_chips(tokens)
    swish, slope, new_m, new_v, update, sums = down_update(
        acts, cotangent_all, down_weight, moment_m, moment_v
    )
    own, other = reduce_z(zero, far, odd, even, give_odd, give_even, sums)
    own, tok_other = lax.optimization_barrier((own, tok_other))

    gate_weight, up_weight = gate_weight.T, up_weight.T

    def group(number, grads, *befores):
        return input_group(
            number, place, grads, swish, slope, gate_weight, up_weight, *befores
        )

    others, owns = [other], [own]
    for _ in range(3):
        others.append(shift_z(others[-1], 2))
        owns.append(shift_z(owns[-1], 2))
    even_other, even = jnp.stack(others), jnp.stack(owns)
    odd_other = shift_z(even_other, 1)
    odd = shift_z(even, 1)
    far = shift_z(owns[3], 2)
    ahead_even = swap_core(even_other[1:])
    group_0 = group(0, (even,))
    group_1 = group(1, (ahead_even,), group_0[4], group_0[3])
    odd_other, odd, far, group_0, group_1 = lax.optimization_barrier(
        (odd_other, odd, far, group_0, group_1)
    )
    ahead_odd = swap_core(odd_other)
    group_2 = group(2, (odd,), group_1[4], group_1[3])
    group_3 = group(3, (ahead_odd, far), group_2[4])
    gateacts, upacts, mine, _, _ = zip(group_0, group_1, group_2, group_3)
    merged = merge_cores(
        place, mine, swap_core(group_2[3]), swap_core(group_3[3]), group_3[4]
    )
    merged, tok_mine = lax.optimization_barrier((merged, tok_mine))
    arrived = exchange_chips(merged)
    grad_gate, grad_up = weight_grads(place, gateacts, upacts, tok_mine, tok_other)
    arrived, grad_gate, grad_up = lax.optimization_barrier((arrived, grad_gate, grad_up))
    grad_input, step_down, ratio = finish(arrived, update)
    return grad_input, grad_gate.T, grad_up.T, new_m, new_v, step_down, ratio[0, 0]


def solution(mesh):
    in_specs = (
        P("col", "row"),
        P("col", "row"),
        P("row", "col"),
        P("row", "col"),
        P("row", "col"),
        P("row", "col"),
        P("col", "row"),
        P("col", "row"),
        P("col", "row"),
    )
    out_specs = (
        P("col", "row"),
        P("row", "col"),
        P("row", "col"),
        P("col", "row"),
        P("col", "row"),
        P("col", "row"),
        P(),
    )
    return jax.shard_map(shards, mesh=mesh, in_specs=in_specs, out_specs=out_specs, check_vma=False)
```

```python
import functools

import jax
import jax.numpy as jnp
from jax import lax
from jax.experimental import pallas as pl
from jax.experimental.pallas import tpu as pltpu
from jax.sharding import PartitionSpec as P

D = 8192
FF = 14336
Z = 16
SIDE = 4
CHIPS = 16
COLS = 32
SCALE_WIDTH = float(D) ** (-0.5)
SCALE_HIDDEN = float(FF) ** (-0.5)
BF16 = jnp.bfloat16
F32 = jnp.float32
VMEM = pl.BlockSpec(memory_space=pltpu.VMEM)
SMEM = pl.BlockSpec(memory_space=pltpu.SMEM)


def params():
    return pltpu.CompilerParams(vmem_limit_bytes=20 * 1024 * 1024)


def shift_z(v, step):
    pairs = []
    for z in range(Z):
        for col in range(COLS):
            way = step if col % 2 == 0 else -step
            pairs.append((z * COLS + col, (z + way) % Z * COLS + col))
    return lax.ppermute(v, ("row", "col"), pairs)


def swap_core(v):
    return lax.ppermute(v, "col", [(c, c ^ 1) for c in range(COLS)])


def exchange_chips(v):
    groups = [[2 * chip + core for chip in range(CHIPS)] for core in range(2)]
    return lax.all_to_all(v, "col", 0, 0, axis_index_groups=groups, tiled=True)


def add(*terms):
    total = terms[0].astype(F32)
    for term in terms[1:]:
        total = total + term.astype(F32)
    return total.astype(BF16)


def reduce_z(zero, far, ahead, give, first_ready, second_ready):
    their = swap_core(give)
    moving = shift_z(far, 1)
    moving = shift_z(add(moving, ahead[6]), 1)
    moving_their = shift_z(their[6], 1)
    for k in range(5, -1, -1):
        if k == 1:
            moving, moving_their, first_ready = lax.optimization_barrier(
                (moving, moving_their, first_ready)
            )
        moving_their = shift_z(add(moving_their, their[k]), 1)
        moving = shift_z(add(moving, ahead[k]), 1)
    moving, moving_their, extra = lax.optimization_barrier((moving, moving_their, second_ready))
    other = jnp.concatenate([moving_their, jnp.zeros_like(extra)], axis=0)
    mine = jnp.concatenate([add(zero, moving), extra], axis=0)
    got_mine = swap_core(other)
    got_other = swap_core(mine)
    return add(mine, got_mine), add(other, got_other), first_ready


GROUPS = ((0, -2, -4, -6), (2, 4, 6), (-1, -3, -5, -7), (1, 3, 5, 7, -8))


def owner_of(place_ref, offset):
    z, way = place_ref[0], place_ref[2]
    return lax.rem(z + way * offset + Z, Z)


def hidden_partial_body(place_ref, mine_ref, other_ref, weight_ref, cot_ref, *refs):
    zero_ref, far_ref, ahead_ref, give_ref, hold = refs
    core = place_ref[1]
    chips, rows, _ = mine_ref.shape
    for chip in range(chips):
        own = pl.multiple_of(chip * 2 * rows + core * rows, rows)
        their = pl.multiple_of(chip * 2 * rows + (1 - core) * rows, rows)
        cot_ref[pl.ds(own, rows), :] = mine_ref[chip]
        cot_ref[pl.ds(their, rows), :] = other_ref[chip]
    tokens = cot_ref.shape[0]
    width = tokens // Z
    span = tokens // SIDE
    for part in range(SIDE):
        product = lax.dot_general(
            weight_ref[...],
            cot_ref[part * span : (part + 1) * span, :],
            (((1,), (1,)), ((), ())),
            preferred_element_type=F32,
        )
        hold[:, part * span : (part + 1) * span] = (product * SCALE_HIDDEN).astype(BF16)

    def block(offset):
        start = pl.multiple_of(owner_of(place_ref, offset) * width, width)
        return hold[:, pl.ds(start, width)]

    zero_ref[...] = block(0)
    far_ref[...] = block(8)
    for k in range(7):
        ahead_ref[k] = block(k + 1)
        give_ref[k] = block(-(k + 1))


def hidden_partial(place, mine, other, weight):
    units, depth = weight.shape
    tokens = mine.shape[0] * mine.shape[1] * 2
    width = tokens // Z
    shapes = [(tokens, depth)] + [(units, width)] * 2 + [(7, units, width)] * 2
    return pl.pallas_call(
        hidden_partial_body,
        out_shape=[jax.ShapeDtypeStruct(shape, BF16) for shape in shapes],
        in_specs=[SMEM] + [VMEM] * 3,
        out_specs=[VMEM] * 5,
        scratch_shapes=[pltpu.VMEM((units, tokens), BF16)],
        compiler_params=params(),
        cost_estimate=pl.CostEstimate(
            flops=2 * units * depth * tokens,
            bytes_accessed=2 * (2 * tokens * depth + units * depth + units * tokens),
            transcendentals=0,
        ),
        name="hidden_partial",
    )(place, mine, other, weight)


def activations_body(acts_ref, swish_ref, slope_ref, hidden_ref):
    blocks, units, width = acts_ref.shape
    units = units // 2
    chunk = 64
    for k in range(blocks):
        cols = slice(k * width, (k + 1) * width)

        @pl.loop(0, units // chunk)
        def _(i, k=k, cols=cols):
            low = pl.multiple_of(i * chunk, chunk)
            rows = pl.ds(low, chunk)
            g = acts_ref[k, rows, :].astype(F32)
            u = acts_ref[k, pl.ds(low + units, chunk), :].astype(F32)
            s = jax.nn.sigmoid(g)
            swish = g * s
            slope = u * s * (1.0 + g * (1.0 - s))
            hidden_ref[rows, cols] = (swish * u).astype(BF16)
            swish_ref[rows, cols] = swish.astype(BF16)
            slope_ref[rows, cols] = slope.astype(BF16)


def activations(acts):
    blocks, units, width = acts.shape
    units, tokens = units // 2, blocks * width
    return pl.pallas_call(
        activations_body,
        out_shape=[jax.ShapeDtypeStruct((units, tokens), BF16)] * 3,
        in_specs=[VMEM],
        out_specs=[VMEM] * 3,
        compiler_params=params(),
        cost_estimate=pl.CostEstimate(
            flops=30 * units * tokens,
            bytes_accessed=10 * units * tokens,
            transcendentals=units * tokens,
        ),
        name="activations",
    )(acts)


def down_body(hidden_ref, cot_ref, weight_ref, m_ref, v_ref, *refs):
    new_m_ref, new_v_ref, update_ref, sums_ref, product = refs
    units = weight_ref.shape[0]
    product[...] = lax.dot_general(
        hidden_ref[...], cot_ref[...], (((1,), (0,)), ((), ())), preferred_element_type=F32
    )
    step = 16
    depth = product.shape[1]

    def optimizer(i, carry):
        weight_sum, update_sum = carry
        rows = pl.ds(pl.multiple_of(i * step, step), step)
        grad = product[rows, :] * SCALE_HIDDEN
        weight = weight_ref[rows, :].astype(F32)
        first = 0.9 * m_ref[rows, :].astype(F32) + 0.1 * grad
        second = 0.95 * v_ref[rows, :].astype(F32) + 0.05 * grad * grad
        update = first / (jnp.sqrt(second) + 1e-08) + 0.1 * weight
        new_m_ref[rows, :] = first.astype(BF16)
        new_v_ref[rows, :] = second.astype(BF16)
        update_ref[rows, :] = update
        return weight_sum + weight * weight, update_sum + update * update

    zero = jnp.zeros((step, depth), F32)
    weight_sum, update_sum = lax.fori_loop(0, units // step, optimizer, (zero, zero))
    weight_sum = jnp.sum(weight_sum, axis=0, keepdims=True)
    update_sum = jnp.sum(update_sum, axis=0, keepdims=True)
    lanes = sums_ref.shape[1]
    parts = [slice(k, k + lanes) for k in range(0, depth, lanes)]
    weight_sum = sum(weight_sum[:, part] for part in parts)
    update_sum = sum(update_sum[:, part] for part in parts)
    sums_ref[...] = in_rows(weight_sum, update_sum)


def in_rows(first, second):
    row = lax.broadcasted_iota(jnp.int32, (16, first.shape[1]), 0)
    value = jnp.where((row & 1) == 0, first, second)
    high = value.astype(BF16).astype(F32)
    middle = (value - high).astype(BF16).astype(F32)
    low = value - high - middle
    rest = jnp.where(row < 4, middle, jnp.where(row < 6, low, 0.0))
    return jnp.where(row < 2, high, rest).astype(BF16)


def from_rows(rows):
    first = rows[0:1] + rows[2:3] + rows[4:5]
    second = rows[1:2] + rows[3:4] + rows[5:6]
    return jnp.sum(first, axis=1, keepdims=True), jnp.sum(second, axis=1, keepdims=True)


def down_update(hidden, cotangent, weight, moment_m, moment_v):
    units, tokens = hidden.shape
    depth = cotangent.shape[1]
    shapes = [
        jax.ShapeDtypeStruct((units, depth), BF16),
        jax.ShapeDtypeStruct((units, depth), BF16),
        jax.ShapeDtypeStruct((units, depth), F32),
        jax.ShapeDtypeStruct((16, 128), BF16),
    ]
    return pl.pallas_call(
        down_body,
        out_shape=shapes,
        in_specs=[VMEM] * 5,
        out_specs=[VMEM] * 4,
        scratch_shapes=[pltpu.VMEM((units, depth), F32)],
        compiler_params=params(),
        cost_estimate=pl.CostEstimate(
            flops=2 * units * depth * tokens,
            bytes_accessed=2 * units * tokens + 2 * tokens * depth + 14 * units * depth,
            transcendentals=0,
        ),
        name="down_update",
    )(hidden, cotangent, weight, moment_m, moment_v)


def group_body(number, count, place_ref, *refs):
    grads = refs[:count]
    swish_ref, slope_ref, gate_weight_ref, up_weight_ref = refs[count : count + 4]
    befores = refs[count + 4 : -6]
    gateact_ref, upact_ref, mine_ref, other_ref, sums_ref, hold = refs[-6:]
    units = gateact_ref.shape[0]
    blocks, half, _ = mine_ref.shape
    width = 2 * half
    chunk = 64
    core = place_ref[1]

    def block(k, rows):
        if k == 4:
            return grads[1][rows, :].astype(F32)
        return grads[0][k, rows, :].astype(F32)

    sums = befores[0][...] if befores else 0.0
    for k in range(blocks):
        sums = sums + block(k, slice(units, units + 16))
    sums_ref[...] = sums
    for k, offset in enumerate(GROUPS[number]):
        start = pl.multiple_of(owner_of(place_ref, offset) * width, width)
        cols = slice(k * width, (k + 1) * width)

        @pl.loop(0, units // chunk)
        def _(i, k=k, start=start, cols=cols):
            rows = pl.ds(pl.multiple_of(i * chunk, chunk), chunk)
            grad = block(k, rows)
            swish = swish_ref[rows, pl.ds(start, width)].astype(F32)
            slope = slope_ref[rows, pl.ds(start, width)].astype(F32)
            upact_ref[rows, cols] = (grad * swish).astype(BF16)
            gateact_ref[rows, cols] = (grad * slope).astype(BF16)

    contract_first = (((0,), (0,)), ((), ()))
    product = lax.dot_general(
        gateact_ref[...], gate_weight_ref[...], contract_first, preferred_element_type=F32
    )
    product = product + lax.dot_general(
        upact_ref[...], up_weight_ref[...], contract_first, preferred_element_type=F32
    )
    hold[...] = (product * SCALE_WIDTH).astype(BF16)
    for k in range(blocks):
        own = pl.multiple_of(k * width + core * half, half)
        their = pl.multiple_of(k * width + (1 - core) * half, half)
        mine_ref[k] = hold[pl.ds(own, half), :]
        low = other_ref.shape[0] - (blocks - k) * half - (16 if number == 3 else 0)
        other_ref[low : low + half, :] = hold[pl.ds(their, half), :]
    if number == 3:
        other_ref[blocks * half :, :] = jnp.zeros((16, other_ref.shape[1]), BF16)
        first = sums[0:1] + sums[2:3] + sums[4:5]
        second = sums[1:2] + sums[3:4] + sums[5:6]
        other_ref[blocks * half :, 0:128] = in_rows(first, second)
    elif number > 0:
        earlier = befores[1].shape[0]
        other_ref[0:earlier, :] = befores[1][...]


def input_group(number, place, grads, swish, slope, gate_weight, up_weight, *befores):
    units, tokens = swish.shape
    depth = gate_weight.shape[1]
    width = tokens // Z
    blocks = len(GROUPS[number])
    half = jax.ShapeDtypeStruct((blocks, width // 2, depth), BF16)
    if number == 3:
        other_rows = blocks * width // 2 + 16
    else:
        other_rows = sum(len(offsets) for offsets in GROUPS[: number + 1]) * width // 2
    other = jax.ShapeDtypeStruct((other_rows, depth), BF16)
    acts = jax.ShapeDtypeStruct((units, blocks * width), BF16)
    sums = jax.ShapeDtypeStruct((16, 128), F32)
    return pl.pallas_call(
        functools.partial(group_body, number, len(grads)),
        out_shape=[acts, acts, half, other, sums],
        in_specs=[SMEM] + [VMEM] * (4 + len(grads) + len(befores)),
        out_specs=[VMEM] * 5,
        scratch_shapes=[pltpu.VMEM((blocks * width, depth), BF16)],
        compiler_params=params(),
        cost_estimate=pl.CostEstimate(
            flops=4 * units * depth * blocks * width,
            bytes_accessed=10 * units * blocks * width + 4 * units * depth,
            transcendentals=0,
        ),
        name="input_group",
    )(place, *grads, swish, slope, gate_weight, up_weight, *befores)


def merge_body(place_ref, *refs):
    mine = refs[:SIDE]
    first_other_ref, last_other_ref, sums_ref, out_ref = refs[SIDE:]
    rows, depth = mine[0].shape[1:]
    parts = [(q * rows, slice(q * 128, (q + 1) * 128)) for q in range(depth // 128)]
    for number, offsets in enumerate(GROUPS):
        for k, offset in enumerate(offsets):
            chip = owner_of(place_ref, offset)
            for low, cols in parts:
                out_ref[chip, low : low + rows, :] = mine[number][k, :, cols]
    first = [offset for offsets in GROUPS[:3] for offset in offsets]
    for ref, offsets in ((first_other_ref, first), (last_other_ref, GROUPS[3])):
        for k, offset in enumerate(offsets):
            chip = owner_of(place_ref, -offset)
            for low, cols in parts:
                total = out_ref[chip, low : low + rows, :].astype(F32)
                total = total + ref[k * rows : (k + 1) * rows, cols].astype(F32)
                out_ref[chip, low : low + rows, :] = total.astype(BF16)
    their = last_other_ref[len(GROUPS[3]) * rows :, 0:128].astype(F32)
    first, second = from_rows(sums_ref[...] + their)
    sums = in_rows(jnp.broadcast_to(first, (1, 128)), jnp.broadcast_to(second, (1, 128)))
    for chip in range(out_ref.shape[0]):
        out_ref[chip, len(parts) * rows :, :] = sums


def merge_cores(place, mine, first_other, last_other, sums):
    _, rows, depth = mine[0].shape
    return pl.pallas_call(
        merge_body,
        out_shape=jax.ShapeDtypeStruct((CHIPS, rows * depth // 128 + 16, 128), BF16),
        in_specs=[SMEM] + [VMEM] * (SIDE + 3),
        out_specs=VMEM,
        compiler_params=params(),
        cost_estimate=pl.CostEstimate(
            flops=CHIPS * rows * depth, bytes_accessed=6 * CHIPS * rows * depth, transcendentals=0
        ),
        name="merge_cores",
    )(place, *mine, first_other, last_other, sums)


def finish_body(arrived_ref, update_ref, grad_input_ref, step_ref, ratio_ref):
    chips = arrived_ref.shape[0]
    rows, depth = grad_input_ref.shape
    for q in range(depth // 128):
        for low in range(0, rows, 32):
            part = slice(q * rows + low, q * rows + low + 32)
            total = arrived_ref[0, part, :].astype(F32)
            for chip in range(1, chips):
                total = total + arrived_ref[chip, part, :].astype(F32)
            grad_input_ref[low : low + 32, q * 128 : (q + 1) * 128] = total.astype(BF16)
    part = slice(rows * depth // 128, rows * depth // 128 + 16)
    sums = arrived_ref[0, part, :].astype(F32)
    for chip in range(1, chips):
        sums = sums + arrived_ref[chip, part, :].astype(F32)
    weight_total = sums[0:1] + sums[2:3] + sums[4:5]
    update_total = sums[1:2] + sums[3:4] + sums[5:6]
    ratio = jnp.sqrt(weight_total) / jnp.sqrt(update_total + 1e-06)
    ratio_ref[...] = ratio
    ratio = ratio[:, 0:1]
    step = 16

    @pl.loop(0, update_ref.shape[0] // step)
    def _(i):
        part = pl.ds(pl.multiple_of(i * step, step), step)
        step_ref[part, :] = (ratio * update_ref[part, :]).astype(BF16)


def finish(arrived, update):
    chips, rows, _ = arrived.shape
    units, depth = update.shape
    return pl.pallas_call(
        finish_body,
        out_shape=[
            jax.ShapeDtypeStruct(((rows - 16) * 128 // depth, depth), BF16),
            jax.ShapeDtypeStruct((units, depth), BF16),
            jax.ShapeDtypeStruct((1, 128), F32),
        ],
        in_specs=[VMEM] * 2,
        out_specs=[VMEM] * 3,
        compiler_params=params(),
        cost_estimate=pl.CostEstimate(
            flops=chips * rows * 128,
            bytes_accessed=2 * chips * rows * 128 + 6 * units * depth,
            transcendentals=0,
        ),
        name="finish",
    )(arrived, update)


def weight_grads_body(place_ref, *refs):
    gateacts, upacts = refs[:SIDE], refs[SIDE : 2 * SIDE]
    mine_ref, other_ref, grad_gate_ref, grad_up_ref, tokens, act = refs[2 * SIDE :]
    core = place_ref[1]
    chips, half, _ = mine_ref.shape
    width = 2 * half
    for chip in range(chips):
        own = pl.multiple_of(chip * width + core * half, half)
        their = pl.multiple_of(chip * width + (1 - core) * half, half)
        tokens[pl.ds(own, half), :] = mine_ref[chip]
        tokens[pl.ds(their, half), :] = other_ref[chip]
    for acts, out_ref in ((gateacts, grad_gate_ref), (upacts, grad_up_ref)):
        for number, offsets in enumerate(GROUPS):
            for k, offset in enumerate(offsets):
                start = pl.multiple_of(owner_of(place_ref, offset) * width, width)
                act[:, pl.ds(start, width)] = acts[number][:, k * width : (k + 1) * width]
        product = lax.dot_general(
            act[...], tokens[...], (((1,), (0,)), ((), ())), preferred_element_type=F32
        )
        out_ref[...] = (product * SCALE_WIDTH).astype(BF16)


def weight_grads(place, gateacts, upacts, mine, other):
    chips, half, depth = mine.shape
    units = gateacts[0].shape[0]
    tokens = chips * half * 2
    out = jax.ShapeDtypeStruct((units, depth), BF16)
    return pl.pallas_call(
        weight_grads_body,
        out_shape=[out, out],
        in_specs=[SMEM] + [VMEM] * (2 * SIDE + 2),
        out_specs=[VMEM] * 2,
        scratch_shapes=[pltpu.VMEM((tokens, depth), BF16), pltpu.VMEM((units, tokens), BF16)],
        compiler_params=params(),
        cost_estimate=pl.CostEstimate(
            flops=4 * units * depth * tokens,
            bytes_accessed=4 * units * tokens + 2 * tokens * depth + 4 * units * depth,
            transcendentals=0,
        ),
        name="weight_grads",
    )(place, *gateacts, *upacts, mine, other)


def shards(
    tokens, cotangent, gate_pre, up_act, gate_weight, up_weight, down_weight, moment_m, moment_v
):
    z = lax.axis_index("row")
    core = lax.axis_index("col") & 1
    place = jnp.stack([z, core, 1 - 2 * core]).astype(jnp.int32)

    acts = jnp.concatenate([gate_pre.T, up_act.T], axis=0)
    acts, cotangent = lax.optimization_barrier((acts, cotangent))
    acts = lax.all_gather(acts, "row", axis=0, tiled=False)
    cot_mine = exchange_chips(jnp.broadcast_to(cotangent[None], (CHIPS, *cotangent.shape)))
    cot_other = swap_core(cot_mine)
    cotangent_all, zero, far, ahead, give = hidden_partial(
        place, cot_mine, cot_other, down_weight
    )
    tokens, _ = lax.optimization_barrier((tokens, cot_other))
    tok_mine = exchange_chips(jnp.broadcast_to(tokens[None], (CHIPS, *tokens.shape)))
    swish, slope, hidden = activations(acts)
    new_m, new_v, update, sums = down_update(
        hidden, cotangent_all, down_weight, moment_m, moment_v
    )
    own, other, (swish, tok_mine) = reduce_z(zero, far, ahead, give, (swish, tok_mine), sums)

    gate_weight, up_weight = gate_weight.T, up_weight.T

    def group(number, grads, *befores):
        return input_group(
            number, place, grads, swish, slope, gate_weight, up_weight, *befores
        )

    others, owns = [other], [own]
    for _ in range(3):
        others.append(shift_z(others[-1], 2))
        owns.append(shift_z(owns[-1], 2))
    even_other, even = jnp.stack(others), jnp.stack(owns)
    odd_other = shift_z(even_other, 1)
    odd = shift_z(even, 1)
    far = shift_z(owns[3], 2)
    ahead_even = swap_core(even_other[1:])
    group_0 = group(0, (even,))
    group_1 = group(1, (ahead_even,), group_0[4], group_0[3])
    tok_other = swap_core(tok_mine)
    odd_other, odd, far, group_0, group_1, tok_other = lax.optimization_barrier(
        (odd_other, odd, far, group_0, group_1, tok_other)
    )
    ahead_odd = swap_core(odd_other)
    group_2 = group(2, (odd,), group_1[4], group_1[3])
    group_3 = group(3, (ahead_odd, far), group_2[4])
    gateacts, upacts, mine, _, _ = zip(group_0, group_1, group_2, group_3)
    merged = merge_cores(
        place, mine, swap_core(group_2[3]), swap_core(group_3[3]), group_3[4]
    )
    merged, tok_mine = lax.optimization_barrier((merged, tok_mine))
    arrived = exchange_chips(merged)
    grad_gate, grad_up = weight_grads(place, gateacts, upacts, tok_mine, tok_other)
    arrived, grad_gate, grad_up = lax.optimization_barrier((arrived, grad_gate, grad_up))
    grad_input, step_down, ratio = finish(arrived, update)
    return grad_input, grad_gate.T, grad_up.T, new_m, new_v, step_down, ratio[0, 0]


def solution(mesh):
    in_specs = (
        P("col", "row"),
        P("col", "row"),
        P("row", "col"),
        P("row", "col"),
        P("row", "col"),
        P("row", "col"),
        P("col", "row"),
        P("col", "row"),
        P("col", "row"),
    )
    out_specs = (
        P("col", "row"),
        P("row", "col"),
        P("row", "col"),
        P("col", "row"),
        P("col", "row"),
        P("col", "row"),
        P(),
    )
    return jax.shard_map(shards, mesh=mesh, in_specs=in_specs, out_specs=out_specs, check_vma=False)
```

```python
import functools

import jax
import jax.numpy as jnp
from jax import lax
from jax.experimental import pallas as pl
from jax.experimental.pallas import tpu as pltpu
from jax.sharding import PartitionSpec as P

D = 8192
FF = 14336
Z = 16
SIDE = 4
CHIPS = 16
COLS = 32
SCALE_WIDTH = float(D) ** (-0.5)
SCALE_HIDDEN = float(FF) ** (-0.5)
BF16 = jnp.bfloat16
F32 = jnp.float32
VMEM = pl.BlockSpec(memory_space=pltpu.VMEM)
SMEM = pl.BlockSpec(memory_space=pltpu.SMEM)
HBM = pl.BlockSpec(memory_space=pltpu.HBM)
DMA = pltpu.SemaphoreType.DMA


def params(mebibytes=20):
    return pltpu.CompilerParams(vmem_limit_bytes=mebibytes * 1024 * 1024)


def shift_z(v, step):
    pairs = []
    for z in range(Z):
        for col in range(COLS):
            way = step if col % 2 == 0 else -step
            pairs.append((z * COLS + col, (z + way) % Z * COLS + col))
    return lax.ppermute(v, ("row", "col"), pairs)


def swap_core(v):
    return lax.ppermute(v, "col", [(c, c ^ 1) for c in range(COLS)])


def exchange_chips(v):
    groups = [[2 * chip + core for chip in range(CHIPS)] for core in range(2)]
    return lax.all_to_all(v, "col", 0, 0, axis_index_groups=groups, tiled=True)


def add(*terms):
    total = terms[0].astype(F32)
    for term in terms[1:]:
        total = total + term.astype(F32)
    return total.astype(BF16)


def reduce_z(zero, far, ahead, give, first_ready, second_ready):
    their = swap_core(give)
    moving = shift_z(far, 1)
    moving = shift_z(add(moving, ahead[6]), 1)
    moving_their = shift_z(their[6], 1)
    for k in range(5, -1, -1):
        if k == 1:
            moving, moving_their, first_ready = lax.optimization_barrier(
                (moving, moving_their, first_ready)
            )
        moving_their = shift_z(add(moving_their, their[k]), 1)
        moving = shift_z(add(moving, ahead[k]), 1)
    moving, moving_their, extra = lax.optimization_barrier((moving, moving_their, second_ready))
    other = jnp.concatenate([moving_their, jnp.zeros_like(extra)], axis=0)
    mine = jnp.concatenate([add(zero, moving), extra], axis=0)
    got_mine = swap_core(other)
    got_other = swap_core(mine)
    return add(mine, got_mine), add(other, got_other), first_ready


GROUPS = ((0, -2, -4, -6), (2, 4, 6), (-1, -3, -5, -7), (1, 3, 5, 7, -8))


def owner_of(place_ref, offset):
    z, way = place_ref[0], place_ref[2]
    return lax.rem(z + way * offset + Z, Z)


def start(source, target, sem):
    copy = pltpu.make_async_copy(source, target, sem)
    copy.start()
    return copy


def hidden_partial_body(place_ref, mine_ref, other_ref, weight_ref, cot_out_ref, *refs):
    zero_ref, far_ref, ahead_ref, give_ref, cot_ref, hold, in_sems, out_sem = refs
    core = place_ref[1]
    chips, rows, _ = mine_ref.shape
    copies = []
    for chip in range(chips):
        own = pl.multiple_of(chip * 2 * rows + core * rows, rows)
        their = pl.multiple_of(chip * 2 * rows + (1 - core) * rows, rows)
        own, their = pl.ds(own, rows), pl.ds(their, rows)
        copies.append(start(mine_ref.at[chip], cot_ref.at[own], in_sems.at[0, chip]))
        copies.append(start(other_ref.at[chip], cot_ref.at[their], in_sems.at[1, chip]))
    for copy in copies:
        copy.wait()
    copy = start(cot_ref, cot_out_ref, out_sem)
    tokens = cot_ref.shape[0]
    width = tokens // Z
    span = tokens // SIDE
    for part in range(SIDE):
        product = lax.dot_general(
            weight_ref[...],
            cot_ref[part * span : (part + 1) * span, :],
            (((1,), (1,)), ((), ())),
            preferred_element_type=F32,
        )
        hold[:, part * span : (part + 1) * span] = (product * SCALE_HIDDEN).astype(BF16)

    def block(offset):
        low = pl.multiple_of(owner_of(place_ref, offset) * width, width)
        return hold[:, pl.ds(low, width)]

    zero_ref[...] = block(0)
    far_ref[...] = block(8)
    for k in range(7):
        ahead_ref[k] = block(k + 1)
        give_ref[k] = block(-(k + 1))
    copy.wait()


def hidden_partial(place, mine, other, weight):
    units, depth = weight.shape
    tokens = mine.shape[0] * mine.shape[1] * 2
    width = tokens // Z
    shapes = [(tokens, depth)] + [(units, width)] * 2 + [(7, units, width)] * 2
    return pl.pallas_call(
        hidden_partial_body,
        out_shape=[jax.ShapeDtypeStruct(shape, BF16) for shape in shapes],
        in_specs=[SMEM, HBM, HBM, VMEM],
        out_specs=[HBM] + [VMEM] * 4,
        scratch_shapes=[
            pltpu.VMEM((tokens, depth), BF16),
            pltpu.VMEM((units, tokens), BF16),
            DMA((2, mine.shape[0])),
            DMA,
        ],
        compiler_params=params(),
        cost_estimate=pl.CostEstimate(
            flops=2 * units * depth * tokens,
            bytes_accessed=2 * (2 * tokens * depth + units * depth + units * tokens),
            transcendentals=0,
        ),
        name="hidden_partial",
    )(place, mine, other, weight)


def activations_body(acts_hbm, *refs):
    outs, (acts_ref, swish_ref, slope_ref, hidden_ref, in_sems, out_sems) = refs[:3], refs[3:]
    blocks, units, width = acts_ref.shape
    units = units // 2
    chunk = 64
    arriving = [start(acts_hbm.at[k], acts_ref.at[k], in_sems.at[k]) for k in range(blocks)]
    leaving = []
    for k in range(blocks):
        cols = slice(k * width, (k + 1) * width)
        arriving[k].wait()

        @pl.loop(0, units // chunk)
        def _(i, k=k, cols=cols):
            low = pl.multiple_of(i * chunk, chunk)
            rows = pl.ds(low, chunk)
            g = acts_ref[k, rows, :].astype(F32)
            u = acts_ref[k, pl.ds(low + units, chunk), :].astype(F32)
            s = jax.nn.sigmoid(g)
            swish = g * s
            slope = u * s * (1.0 + g * (1.0 - s))
            hidden_ref[rows, cols] = (swish * u).astype(BF16)
            swish_ref[rows, cols] = swish.astype(BF16)
            slope_ref[rows, cols] = slope.astype(BF16)

        if k % 4 == 3:
            part = slice((k - 3) * width, (k + 1) * width)
            for n, ref in enumerate((swish_ref, slope_ref, hidden_ref)):
                leaving.append(
                    start(ref.at[:, part], outs[n].at[:, part], out_sems.at[n, k // 4])
                )
    for copy in leaving:
        copy.wait()


def activations(acts):
    blocks, units, width = acts.shape
    units, tokens = units // 2, blocks * width
    return pl.pallas_call(
        activations_body,
        out_shape=[jax.ShapeDtypeStruct((units, tokens), BF16)] * 3,
        in_specs=[HBM],
        out_specs=[HBM] * 3,
        scratch_shapes=[pltpu.VMEM(acts.shape, BF16)]
        + [pltpu.VMEM((units, tokens), BF16)] * 3
        + [DMA((blocks,)), DMA((3, blocks // 4))],
        compiler_params=params(56),
        cost_estimate=pl.CostEstimate(
            flops=30 * units * tokens,
            bytes_accessed=10 * units * tokens,
            transcendentals=units * tokens,
        ),
        name="activations",
    )(acts)


def down_body(hidden_hbm, cot_hbm, weight_hbm, m_hbm, v_hbm, *refs):
    outs, sums_ref = refs[:3], refs[3]
    hidden_ref, cot_ref, weight_ref, m_ref, v_ref = refs[4:9]
    new_m_ref, new_v_ref, update_ref, product, sems, out_sems = refs[9:]
    units = weight_ref.shape[0]
    span = cot_ref.shape[0] // SIDE
    parts = [slice(k * span, (k + 1) * span) for k in range(SIDE)]
    arriving = []
    for k, part in enumerate(parts):
        arriving.append(
            (
                start(hidden_hbm.at[:, part], hidden_ref.at[:, part], sems.at[0, k]),
                start(cot_hbm.at[part], cot_ref.at[part], sems.at[1, k]),
            )
        )
    moments = [
        start(weight_hbm, weight_ref, sems.at[2, 0]),
        start(m_hbm, m_ref, sems.at[2, 1]),
        start(v_hbm, v_ref, sems.at[2, 2]),
    ]
    for k, part in enumerate(parts):
        for copy in arriving[k]:
            copy.wait()
        term = lax.dot_general(
            hidden_ref[:, part],
            cot_ref[part, :],
            (((1,), (0,)), ((), ())),
            preferred_element_type=F32,
        )
        product[...] = term if k == 0 else product[...] + term
    for copy in moments:
        copy.wait()
    step = 16
    depth = product.shape[1]

    def optimizer(i, carry):
        weight_sum, update_sum = carry
        rows = pl.ds(pl.multiple_of(i * step, step), step)
        grad = product[rows, :] * SCALE_HIDDEN
        weight = weight_ref[rows, :].astype(F32)
        first = 0.9 * m_ref[rows, :].astype(F32) + 0.1 * grad
        second = 0.95 * v_ref[rows, :].astype(F32) + 0.05 * grad * grad
        update = first / (jnp.sqrt(second) + 1e-08) + 0.1 * weight
        new_m_ref[rows, :] = first.astype(BF16)
        new_v_ref[rows, :] = second.astype(BF16)
        update_ref[rows, :] = update
        return weight_sum + weight * weight, update_sum + update * update

    zero = jnp.zeros((step, depth), F32)
    weight_sum, update_sum = lax.fori_loop(0, units // step, optimizer, (zero, zero))
    leaving = [
        start(ref, outs[n], out_sems.at[n]) for n, ref in enumerate((new_m_ref, new_v_ref, update_ref))
    ]
    weight_sum = jnp.sum(weight_sum, axis=0, keepdims=True)
    update_sum = jnp.sum(update_sum, axis=0, keepdims=True)
    lanes = sums_ref.shape[1]
    parts = [slice(k, k + lanes) for k in range(0, depth, lanes)]
    weight_sum = sum(weight_sum[:, part] for part in parts)
    update_sum = sum(update_sum[:, part] for part in parts)
    sums_ref[...] = in_rows(weight_sum, update_sum)
    for copy in leaving:
        copy.wait()


def in_rows(first, second):
    row = lax.broadcasted_iota(jnp.int32, (16, first.shape[1]), 0)
    value = jnp.where((row & 1) == 0, first, second)
    high = value.astype(BF16).astype(F32)
    middle = (value - high).astype(BF16).astype(F32)
    low = value - high - middle
    rest = jnp.where(row < 4, middle, jnp.where(row < 6, low, 0.0))
    return jnp.where(row < 2, high, rest).astype(BF16)


def from_rows(rows):
    first = rows[0:1] + rows[2:3] + rows[4:5]
    second = rows[1:2] + rows[3:4] + rows[5:6]
    return jnp.sum(first, axis=1, keepdims=True), jnp.sum(second, axis=1, keepdims=True)


def down_update(hidden, cotangent, weight, moment_m, moment_v):
    units, tokens = hidden.shape
    depth = cotangent.shape[1]
    shapes = [
        jax.ShapeDtypeStruct((units, depth), BF16),
        jax.ShapeDtypeStruct((units, depth), BF16),
        jax.ShapeDtypeStruct((units, depth), F32),
        jax.ShapeDtypeStruct((16, 128), BF16),
    ]
    return pl.pallas_call(
        down_body,
        out_shape=shapes,
        in_specs=[HBM] * 5,
        out_specs=[HBM] * 3 + [VMEM],
        scratch_shapes=[pltpu.VMEM((units, tokens), BF16), pltpu.VMEM((tokens, depth), BF16)]
        + [pltpu.VMEM((units, depth), BF16)] * 5
        + [pltpu.VMEM((units, depth), F32)] * 2
        + [DMA((3, SIDE)), DMA((3,))],
        compiler_params=params(56),
        cost_estimate=pl.CostEstimate(
            flops=2 * units * depth * tokens,
            bytes_accessed=2 * units * tokens + 2 * tokens * depth + 14 * units * depth,
            transcendentals=0,
        ),
        name="down_update",
    )(hidden, cotangent, weight, moment_m, moment_v)


def group_body(number, count, place_ref, *refs):
    grads = refs[:count]
    swish_ref, slope_ref, gate_weight_ref, up_weight_ref = refs[count : count + 4]
    befores = refs[count + 4 : -9]
    gateact_hbm, upact_hbm, mine_ref, other_ref, sums_ref = refs[-9:-4]
    gateact_ref, upact_ref, hold, sems = refs[-4:]
    units = gateact_ref.shape[0]
    blocks, half, _ = mine_ref.shape
    width = 2 * half
    chunk = 64
    core = place_ref[1]

    def block(k, rows):
        if k == 4:
            return grads[1][rows, :].astype(F32)
        return grads[0][k, rows, :].astype(F32)

    sums = befores[0][...] if befores else 0.0
    for k in range(blocks):
        sums = sums + block(k, slice(units, units + 16))
    sums_ref[...] = sums
    for k, offset in enumerate(GROUPS[number]):
        low = pl.multiple_of(owner_of(place_ref, offset) * width, width)
        cols = slice(k * width, (k + 1) * width)

        @pl.loop(0, units // chunk)
        def _(i, k=k, low=low, cols=cols):
            rows = pl.ds(pl.multiple_of(i * chunk, chunk), chunk)
            grad = block(k, rows)
            swish = swish_ref[rows, pl.ds(low, width)].astype(F32)
            slope = slope_ref[rows, pl.ds(low, width)].astype(F32)
            upact_ref[rows, cols] = (grad * swish).astype(BF16)
            gateact_ref[rows, cols] = (grad * slope).astype(BF16)

    leaving = [
        start(gateact_ref, gateact_hbm, sems.at[0]),
        start(upact_ref, upact_hbm, sems.at[1]),
    ]
    contract_first = (((0,), (0,)), ((), ()))
    product = lax.dot_general(
        gateact_ref[...], gate_weight_ref[...], contract_first, preferred_element_type=F32
    )
    product = product + lax.dot_general(
        upact_ref[...], up_weight_ref[...], contract_first, preferred_element_type=F32
    )
    hold[...] = (product * SCALE_WIDTH).astype(BF16)
    for k in range(blocks):
        own = pl.multiple_of(k * width + core * half, half)
        their = pl.multiple_of(k * width + (1 - core) * half, half)
        mine_ref[k] = hold[pl.ds(own, half), :]
        low = other_ref.shape[0] - (blocks - k) * half - (16 if number == 3 else 0)
        other_ref[low : low + half, :] = hold[pl.ds(their, half), :]
    if number == 3:
        other_ref[blocks * half :, :] = jnp.zeros((16, other_ref.shape[1]), BF16)
        first = sums[0:1] + sums[2:3] + sums[4:5]
        second = sums[1:2] + sums[3:4] + sums[5:6]
        other_ref[blocks * half :, 0:128] = in_rows(first, second)
    elif number > 0:
        earlier = befores[1].shape[0]
        other_ref[0:earlier, :] = befores[1][...]
    for copy in leaving:
        copy.wait()


def input_group(number, place, grads, swish, slope, gate_weight, up_weight, *befores):
    units, tokens = swish.shape
    depth = gate_weight.shape[1]
    width = tokens // Z
    blocks = len(GROUPS[number])
    half = jax.ShapeDtypeStruct((blocks, width // 2, depth), BF16)
    if number == 3:
        other_rows = blocks * width // 2 + 16
    else:
        other_rows = sum(len(offsets) for offsets in GROUPS[: number + 1]) * width // 2
    other = jax.ShapeDtypeStruct((other_rows, depth), BF16)
    acts = jax.ShapeDtypeStruct((units, blocks * width), BF16)
    sums = jax.ShapeDtypeStruct((16, 128), F32)
    return pl.pallas_call(
        functools.partial(group_body, number, len(grads)),
        out_shape=[acts, acts, half, other, sums],
        in_specs=[SMEM] + [VMEM] * (4 + len(grads) + len(befores)),
        out_specs=[HBM] * 2 + [VMEM] * 3,
        scratch_shapes=[pltpu.VMEM((units, blocks * width), BF16)] * 2
        + [pltpu.VMEM((blocks * width, depth), BF16), DMA((2,))],
        compiler_params=params(),
        cost_estimate=pl.CostEstimate(
            flops=4 * units * depth * blocks * width,
            bytes_accessed=10 * units * blocks * width + 4 * units * depth,
            transcendentals=0,
        ),
        name="input_group",
    )(place, *grads, swish, slope, gate_weight, up_weight, *befores)


def merge_body(place_ref, *refs):
    mine = refs[:SIDE]
    first_other_ref, last_other_ref, sums_ref, out_ref = refs[SIDE:]
    rows, depth = mine[0].shape[1:]
    parts = [(q * rows, slice(q * 128, (q + 1) * 128)) for q in range(depth // 128)]
    for number, offsets in enumerate(GROUPS):
        for k, offset in enumerate(offsets):
            chip = owner_of(place_ref, offset)
            for low, cols in parts:
                out_ref[chip, low : low + rows, :] = mine[number][k, :, cols]
    first = [offset for offsets in GROUPS[:3] for offset in offsets]
    for ref, offsets in ((first_other_ref, first), (last_other_ref, GROUPS[3])):
        for k, offset in enumerate(offsets):
            chip = owner_of(place_ref, -offset)
            for low, cols in parts:
                total = out_ref[chip, low : low + rows, :].astype(F32)
                total = total + ref[k * rows : (k + 1) * rows, cols].astype(F32)
                out_ref[chip, low : low + rows, :] = total.astype(BF16)
    their = last_other_ref[len(GROUPS[3]) * rows :, 0:128].astype(F32)
    first, second = from_rows(sums_ref[...] + their)
    sums = in_rows(jnp.broadcast_to(first, (1, 128)), jnp.broadcast_to(second, (1, 128)))
    for chip in range(out_ref.shape[0]):
        out_ref[chip, len(parts) * rows :, :] = sums


def merge_cores(place, mine, first_other, last_other, sums):
    _, rows, depth = mine[0].shape
    return pl.pallas_call(
        merge_body,
        out_shape=jax.ShapeDtypeStruct((CHIPS, rows * depth // 128 + 16, 128), BF16),
        in_specs=[SMEM] + [VMEM] * (SIDE + 3),
        out_specs=VMEM,
        compiler_params=params(),
        cost_estimate=pl.CostEstimate(
            flops=CHIPS * rows * depth, bytes_accessed=6 * CHIPS * rows * depth, transcendentals=0
        ),
        name="merge_cores",
    )(place, *mine, first_other, last_other, sums)


def finish_body(arrived_ref, update_hbm, grad_input_ref, step_ref, ratio_ref, update_ref, sem):
    copy = start(update_hbm, update_ref, sem)
    chips = arrived_ref.shape[0]
    rows, depth = grad_input_ref.shape
    for q in range(depth // 128):
        for low in range(0, rows, 32):
            part = slice(q * rows + low, q * rows + low + 32)
            total = arrived_ref[0, part, :].astype(F32)
            for chip in range(1, chips):
                total = total + arrived_ref[chip, part, :].astype(F32)
            grad_input_ref[low : low + 32, q * 128 : (q + 1) * 128] = total.astype(BF16)
    part = slice(rows * depth // 128, rows * depth // 128 + 16)
    sums = arrived_ref[0, part, :].astype(F32)
    for chip in range(1, chips):
        sums = sums + arrived_ref[chip, part, :].astype(F32)
    weight_total = sums[0:1] + sums[2:3] + sums[4:5]
    update_total = sums[1:2] + sums[3:4] + sums[5:6]
    ratio = jnp.sqrt(weight_total) / jnp.sqrt(update_total + 1e-06)
    ratio_ref[...] = ratio
    ratio = ratio[:, 0:1]
    step = 16
    copy.wait()

    @pl.loop(0, update_ref.shape[0] // step)
    def _(i):
        part = pl.ds(pl.multiple_of(i * step, step), step)
        step_ref[part, :] = (ratio * update_ref[part, :]).astype(BF16)


def finish(arrived, update):
    chips, rows, _ = arrived.shape
    units, depth = update.shape
    return pl.pallas_call(
        finish_body,
        out_shape=[
            jax.ShapeDtypeStruct(((rows - 16) * 128 // depth, depth), BF16),
            jax.ShapeDtypeStruct((units, depth), BF16),
            jax.ShapeDtypeStruct((1, 128), F32),
        ],
        in_specs=[VMEM, HBM],
        out_specs=[VMEM] * 3,
        scratch_shapes=[pltpu.VMEM((units, depth), F32), DMA],
        compiler_params=params(),
        cost_estimate=pl.CostEstimate(
            flops=chips * rows * 128,
            bytes_accessed=2 * chips * rows * 128 + 6 * units * depth,
            transcendentals=0,
        ),
        name="finish",
    )(arrived, update)


def weight_grads_body(place_ref, *refs):
    gateacts, upacts = refs[:SIDE], refs[SIDE : 2 * SIDE]
    mine_ref, other_ref, grad_gate_ref, grad_up_ref, tokens, act = refs[2 * SIDE :]
    core = place_ref[1]
    chips, half, _ = mine_ref.shape
    width = 2 * half
    for chip in range(chips):
        own = pl.multiple_of(chip * width + core * half, half)
        their = pl.multiple_of(chip * width + (1 - core) * half, half)
        tokens[pl.ds(own, half), :] = mine_ref[chip]
        tokens[pl.ds(their, half), :] = other_ref[chip]
    for acts, out_ref in ((gateacts, grad_gate_ref), (upacts, grad_up_ref)):
        for number, offsets in enumerate(GROUPS):
            for k, offset in enumerate(offsets):
                low = pl.multiple_of(owner_of(place_ref, offset) * width, width)
                act[:, pl.ds(low, width)] = acts[number][:, k * width : (k + 1) * width]
        product = lax.dot_general(
            act[...], tokens[...], (((1,), (0,)), ((), ())), preferred_element_type=F32
        )
        out_ref[...] = (product * SCALE_WIDTH).astype(BF16)


def weight_grads(place, gateacts, upacts, mine, other):
    chips, half, depth = mine.shape
    units = gateacts[0].shape[0]
    tokens = chips * half * 2
    out = jax.ShapeDtypeStruct((units, depth), BF16)
    return pl.pallas_call(
        weight_grads_body,
        out_shape=[out, out],
        in_specs=[SMEM] + [VMEM] * (2 * SIDE + 2),
        out_specs=[VMEM] * 2,
        scratch_shapes=[pltpu.VMEM((tokens, depth), BF16), pltpu.VMEM((units, tokens), BF16)],
        compiler_params=params(),
        cost_estimate=pl.CostEstimate(
            flops=4 * units * depth * tokens,
            bytes_accessed=4 * units * tokens + 2 * tokens * depth + 4 * units * depth,
            transcendentals=0,
        ),
        name="weight_grads",
    )(place, *gateacts, *upacts, mine, other)


def shards(
    tokens, cotangent, gate_pre, up_act, gate_weight, up_weight, down_weight, moment_m, moment_v
):
    z = lax.axis_index("row")
    core = lax.axis_index("col") & 1
    place = jnp.stack([z, core, 1 - 2 * core]).astype(jnp.int32)

    acts = jnp.concatenate([gate_pre.T, up_act.T], axis=0)
    acts, cotangent = lax.optimization_barrier((acts, cotangent))
    acts = lax.all_gather(acts, "row", axis=0, tiled=False)
    cot_mine = exchange_chips(jnp.broadcast_to(cotangent[None], (CHIPS, *cotangent.shape)))
    cot_other = swap_core(cot_mine)
    cotangent_all, zero, far, ahead, give = hidden_partial(
        place, cot_mine, cot_other, down_weight
    )
    tokens, _ = lax.optimization_barrier((tokens, cot_other))
    tok_mine = exchange_chips(jnp.broadcast_to(tokens[None], (CHIPS, *tokens.shape)))
    swish, slope, hidden = activations(acts)
    new_m, new_v, update, sums = down_update(
        hidden, cotangent_all, down_weight, moment_m, moment_v
    )
    beside = (swish, tok_mine, swap_core(tok_mine))
    own, other, beside = reduce_z(zero, far, ahead, give, beside, sums)
    swish, tok_mine, tok_other = beside

    gate_weight, up_weight = gate_weight.T, up_weight.T

    def group(number, grads, *befores):
        return input_group(
            number, place, grads, swish, slope, gate_weight, up_weight, *befores
        )

    others, owns = [other], [own]
    for _ in range(3):
        others.append(shift_z(others[-1], 2))
        owns.append(shift_z(owns[-1], 2))
    even_other, even = jnp.stack(others), jnp.stack(owns)
    odd_other = shift_z(even_other, 1)
    odd = shift_z(even, 1)
    far = shift_z(owns[3], 2)
    ahead_even = swap_core(even_other[1:])
    group_0 = group(0, (even,))
    group_1 = group(1, (ahead_even,), group_0[4], group_0[3])
    odd_other, odd, far, group_0, group_1 = lax.optimization_barrier(
        (odd_other, odd, far, group_0, group_1)
    )
    ahead_odd = swap_core(odd_other)
    group_2 = group(2, (odd,), group_1[4], group_1[3])
    group_3 = group(3, (ahead_odd, far), group_2[4])
    gateacts, upacts, mine, _, _ = zip(group_0, group_1, group_2, group_3)
    merged = merge_cores(
        place, mine, swap_core(group_2[3]), swap_core(group_3[3]), group_3[4]
    )
    merged, tok_mine = lax.optimization_barrier((merged, tok_mine))
    arrived = exchange_chips(merged)
    grad_gate, grad_up = weight_grads(place, gateacts, upacts, tok_mine, tok_other)
    arrived, grad_gate, grad_up = lax.optimization_barrier((arrived, grad_gate, grad_up))
    grad_input, step_down, ratio = finish(arrived, update)
    return grad_input, grad_gate.T, grad_up.T, new_m, new_v, step_down, ratio[0, 0]


def solution(mesh):
    in_specs = (
        P("col", "row"),
        P("col", "row"),
        P("row", "col"),
        P("row", "col"),
        P("row", "col"),
        P("row", "col"),
        P("col", "row"),
        P("col", "row"),
        P("col", "row"),
    )
    out_specs = (
        P("col", "row"),
        P("row", "col"),
        P("row", "col"),
        P("col", "row"),
        P("col", "row"),
        P("col", "row"),
        P(),
    )
    return jax.shard_map(shards, mesh=mesh, in_specs=in_specs, out_specs=out_specs, check_vma=False)
```

```python
import functools

import jax
import jax.numpy as jnp
from jax import lax
from jax.experimental import pallas as pl
from jax.experimental.pallas import tpu as pltpu
from jax.sharding import PartitionSpec as P

D = 8192
FF = 14336
Z = 16
SIDE = 4
CHIPS = 16
COLS = 32
SCALE_WIDTH = float(D) ** (-0.5)
SCALE_HIDDEN = float(FF) ** (-0.5)
BF16 = jnp.bfloat16
F32 = jnp.float32
VMEM = pl.BlockSpec(memory_space=pltpu.VMEM)
SMEM = pl.BlockSpec(memory_space=pltpu.SMEM)
HBM = pl.BlockSpec(memory_space=pltpu.HBM)
DMA = pltpu.SemaphoreType.DMA


def params(mebibytes=20):
    return pltpu.CompilerParams(vmem_limit_bytes=mebibytes * 1024 * 1024)


def shift_z(v, step):
    pairs = []
    for z in range(Z):
        for col in range(COLS):
            way = step if col % 2 == 0 else -step
            pairs.append((z * COLS + col, (z + way) % Z * COLS + col))
    return lax.ppermute(v, ("row", "col"), pairs)


def swap_core(v):
    return lax.ppermute(v, "col", [(c, c ^ 1) for c in range(COLS)])


def exchange_chips(v):
    groups = [[2 * chip + core for chip in range(CHIPS)] for core in range(2)]
    return lax.all_to_all(v, "col", 0, 0, axis_index_groups=groups, tiled=True)


def gather_chips(v):
    mine = exchange_chips(jnp.broadcast_to(v[None], (CHIPS, *v.shape)))
    return mine, swap_core(mine)


def add(*terms):
    total = terms[0].astype(F32)
    for term in terms[1:]:
        total = total + term.astype(F32)
    return total.astype(BF16)


def reduce_z(zero, far, odd, even, give_odd, give_even, beside):
    own = shift_z(odd, 1)
    got_odd = swap_core(give_odd)
    their = shift_z(got_odd, 1)
    far = shift_z(far, SIDE)
    got_even = swap_core(give_even)
    moving_their = add(got_even[2], their[3])
    moving = add(even[2], own[3])
    done = []
    for k in (2, 1, 0):
        moving_their = shift_z(moving_their, 2)
        moving = shift_z(moving, 2)
        moving, ready = lax.optimization_barrier((moving, beside[2 - k]))
        done.append(ready)
        if k == 2:
            moving = add(moving, even[1], own[2], far)
        elif k == 1:
            moving = add(moving, even[0], own[1])
        if k > 0:
            moving_their = add(moving_their, got_even[k - 1], their[k])
    extra = done[2]
    other = jnp.concatenate([add(moving_their, their[0]), jnp.zeros_like(extra)], axis=0)
    mine = jnp.concatenate([add(zero, moving, own[0]), extra], axis=0)
    got_mine = swap_core(other)
    got_other = swap_core(mine)
    return add(mine, got_mine), add(other, got_other), done


GROUPS = ((0, -2, -4, -6), (2, 4, 6), (-1, -3, -5, -7), (1, 3, 5, 7, -8))


def owner_of(place_ref, offset):
    z, way = place_ref[0], place_ref[2]
    return lax.rem(z + way * offset + Z, Z)


def hidden_partial_body(place_ref, mine_ref, other_ref, weight_ref, cot_ref, *refs):
    zero_ref, far_ref, odd_ref, even_ref, give_odd_ref, give_even_ref, hold = refs
    core = place_ref[1]
    chips, rows, _ = mine_ref.shape
    for chip in range(chips):
        own = pl.multiple_of(chip * 2 * rows + core * rows, rows)
        their = pl.multiple_of(chip * 2 * rows + (1 - core) * rows, rows)
        cot_ref[pl.ds(own, rows), :] = mine_ref[chip]
        cot_ref[pl.ds(their, rows), :] = other_ref[chip]
    tokens = cot_ref.shape[0]
    width = tokens // Z
    span = tokens // SIDE
    for part in range(SIDE):
        product = lax.dot_general(
            weight_ref[...],
            cot_ref[part * span : (part + 1) * span, :],
            (((1,), (1,)), ((), ())),
            preferred_element_type=F32,
        )
        hold[:, part * span : (part + 1) * span] = (product * SCALE_HIDDEN).astype(BF16)

    def block(offset):
        low = pl.multiple_of(owner_of(place_ref, offset) * width, width)
        return hold[:, pl.ds(low, width)]

    zero_ref[...] = block(0)
    far_ref[...] = block(8)
    for k, offset in enumerate((1, 3, 5, 7)):
        odd_ref[k] = block(offset)
        give_odd_ref[k] = block(-offset)
    for k, offset in enumerate((2, 4, 6)):
        even_ref[k] = block(offset)
        give_even_ref[k] = block(-offset)


def hidden_partial(place, mine, other, weight):
    units, depth = weight.shape
    tokens = mine.shape[0] * mine.shape[1] * 2
    width = tokens // Z
    shapes = [(tokens, depth), (units, width), (units, width)]
    shapes += [(count, units, width) for count in (4, 3, 4, 3)]
    return pl.pallas_call(
        hidden_partial_body,
        out_shape=[jax.ShapeDtypeStruct(shape, BF16) for shape in shapes],
        in_specs=[SMEM] + [VMEM] * 3,
        out_specs=[VMEM] * 7,
        scratch_shapes=[pltpu.VMEM((units, tokens), BF16)],
        compiler_params=params(),
        cost_estimate=pl.CostEstimate(
            flops=2 * units * depth * tokens,
            bytes_accessed=2 * (2 * tokens * depth + units * depth + units * tokens),
            transcendentals=0,
        ),
        name="hidden_partial",
    )(place, mine, other, weight)


def start(source, target, sem):
    copy = pltpu.make_async_copy(source, target, sem)
    copy.start()
    return copy


def activations_body(acts_hbm, *refs):
    outs, (acts_ref, swish_ref, slope_ref, hidden_ref, in_sems, out_sems) = refs[:3], refs[3:]
    blocks, units, width = acts_ref.shape
    units = units // 2
    chunk = 64
    arriving = [start(acts_hbm.at[k], acts_ref.at[k], in_sems.at[k]) for k in range(blocks)]
    leaving = []
    for k in range(blocks):
        cols = slice(k * width, (k + 1) * width)
        arriving[k].wait()

        @pl.loop(0, units // chunk)
        def _(i, k=k, cols=cols):
            low = pl.multiple_of(i * chunk, chunk)
            rows = pl.ds(low, chunk)
            g = acts_ref[k, rows, :].astype(F32)
            u = acts_ref[k, pl.ds(low + units, chunk), :].astype(F32)
            s = jax.nn.sigmoid(g)
            swish = g * s
            slope = u * s * (1.0 + g * (1.0 - s))
            hidden_ref[rows, cols] = (swish * u).astype(BF16)
            swish_ref[rows, cols] = swish.astype(BF16)
            slope_ref[rows, cols] = slope.astype(BF16)

        if k % 4 == 3:
            part = slice((k - 3) * width, (k + 1) * width)
            for n, ref in enumerate((swish_ref, slope_ref, hidden_ref)):
                leaving.append(
                    start(ref.at[:, part], outs[n].at[:, part], out_sems.at[n, k // 4])
                )
    for copy in leaving:
        copy.wait()


def activations(acts):
    blocks, units, width = acts.shape
    units, tokens = units // 2, blocks * width
    return pl.pallas_call(
        activations_body,
        out_shape=[jax.ShapeDtypeStruct((units, tokens), BF16)] * 3,
        in_specs=[HBM],
        out_specs=[HBM] * 3,
        scratch_shapes=[pltpu.VMEM(acts.shape, BF16)]
        + [pltpu.VMEM((units, tokens), BF16)] * 3
        + [DMA((blocks,)), DMA((3, blocks // 4))],
        compiler_params=params(56),
        cost_estimate=pl.CostEstimate(
            flops=30 * units * tokens,
            bytes_accessed=10 * units * tokens,
            transcendentals=units * tokens,
        ),
        name="activations",
    )(acts)


def down_body(hidden_hbm, cot_hbm, weight_hbm, m_hbm, v_hbm, *refs):
    outs, sums_ref = refs[:3], refs[3]
    hidden_ref, cot_ref, weight_ref, m_ref, v_ref = refs[4:9]
    new_m_ref, new_v_ref, update_ref, product, sems, out_sems = refs[9:]
    units = weight_ref.shape[0]
    span = cot_ref.shape[0] // SIDE
    parts = [slice(k * span, (k + 1) * span) for k in range(SIDE)]
    arriving = []
    for k, part in enumerate(parts):
        arriving.append(
            (
                start(hidden_hbm.at[:, part], hidden_ref.at[:, part], sems.at[0, k]),
                start(cot_hbm.at[part], cot_ref.at[part], sems.at[1, k]),
            )
        )
    moments = [
        start(weight_hbm, weight_ref, sems.at[2, 0]),
        start(m_hbm, m_ref, sems.at[2, 1]),
        start(v_hbm, v_ref, sems.at[2, 2]),
    ]
    for k, part in enumerate(parts):
        for copy in arriving[k]:
            copy.wait()
        term = lax.dot_general(
            hidden_ref[:, part],
            cot_ref[part, :],
            (((1,), (0,)), ((), ())),
            preferred_element_type=F32,
        )
        product[...] = term if k == 0 else product[...] + term
    for copy in moments:
        copy.wait()
    step = 16
    depth = product.shape[1]

    def optimizer(i, carry):
        weight_sum, update_sum = carry
        rows = pl.ds(pl.multiple_of(i * step, step), step)
        grad = product[rows, :] * SCALE_HIDDEN
        weight = weight_ref[rows, :].astype(F32)
        first = 0.9 * m_ref[rows, :].astype(F32) + 0.1 * grad
        second = 0.95 * v_ref[rows, :].astype(F32) + 0.05 * grad * grad
        update = first / (jnp.sqrt(second) + 1e-08) + 0.1 * weight
        new_m_ref[rows, :] = first.astype(BF16)
        new_v_ref[rows, :] = second.astype(BF16)
        update_ref[rows, :] = update
        return weight_sum + weight * weight, update_sum + update * update

    zero = jnp.zeros((step, depth), F32)
    weight_sum, update_sum = lax.fori_loop(0, units // step, optimizer, (zero, zero))
    leaving = [
        start(ref, outs[n], out_sems.at[n]) for n, ref in enumerate((new_m_ref, new_v_ref, update_ref))
    ]
    weight_sum = jnp.sum(weight_sum, axis=0, keepdims=True)
    update_sum = jnp.sum(update_sum, axis=0, keepdims=True)
    lanes = sums_ref.shape[1]
    parts = [slice(k, k + lanes) for k in range(0, depth, lanes)]
    weight_sum = sum(weight_sum[:, part] for part in parts)
    update_sum = sum(update_sum[:, part] for part in parts)
    sums_ref[...] = in_rows(weight_sum, update_sum)
    for copy in leaving:
        copy.wait()


def in_rows(first, second):
    row = lax.broadcasted_iota(jnp.int32, (16, first.shape[1]), 0)
    value = jnp.where((row & 1) == 0, first, second)
    high = value.astype(BF16).astype(F32)
    middle = (value - high).astype(BF16).astype(F32)
    low = value - high - middle
    rest = jnp.where(row < 4, middle, jnp.where(row < 6, low, 0.0))
    return jnp.where(row < 2, high, rest).astype(BF16)


def from_rows(rows):
    first = rows[0:1] + rows[2:3] + rows[4:5]
    second = rows[1:2] + rows[3:4] + rows[5:6]
    return jnp.sum(first, axis=1, keepdims=True), jnp.sum(second, axis=1, keepdims=True)


def down_update(hidden, cotangent, weight, moment_m, moment_v):
    units, tokens = hidden.shape
    depth = cotangent.shape[1]
    shapes = [
        jax.ShapeDtypeStruct((units, depth), BF16),
        jax.ShapeDtypeStruct((units, depth), BF16),
        jax.ShapeDtypeStruct((units, depth), F32),
        jax.ShapeDtypeStruct((16, 128), BF16),
    ]
    return pl.pallas_call(
        down_body,
        out_shape=shapes,
        in_specs=[HBM] * 5,
        out_specs=[HBM] * 3 + [VMEM],
        scratch_shapes=[pltpu.VMEM((units, tokens), BF16), pltpu.VMEM((tokens, depth), BF16)]
        + [pltpu.VMEM((units, depth), BF16)] * 5
        + [pltpu.VMEM((units, depth), F32)] * 2
        + [DMA((3, SIDE)), DMA((3,))],
        compiler_params=params(56),
        cost_estimate=pl.CostEstimate(
            flops=2 * units * depth * tokens,
            bytes_accessed=2 * units * tokens + 2 * tokens * depth + 14 * units * depth,
            transcendentals=0,
        ),
        name="down_update",
    )(hidden, cotangent, weight, moment_m, moment_v)


def group_body(number, count, place_ref, *refs):
    grads = refs[:count]
    swish_ref, slope_ref, gate_weight_ref, up_weight_ref = refs[count : count + 4]
    befores = refs[count + 4 : -6]
    gateact_ref, upact_ref, mine_ref, other_ref, sums_ref, hold = refs[-6:]
    units = gateact_ref.shape[0]
    blocks, half, _ = mine_ref.shape
    width = 2 * half
    chunk = 64
    core = place_ref[1]

    def block(k, rows):
        if k == 4:
            return grads[1][rows, :].astype(F32)
        return grads[0][k, rows, :].astype(F32)

    sums = befores[0][...] if befores else 0.0
    for k in range(blocks):
        sums = sums + block(k, slice(units, units + 16))
    sums_ref[...] = sums
    for k, offset in enumerate(GROUPS[number]):
        start = pl.multiple_of(owner_of(place_ref, offset) * width, width)
        cols = slice(k * width, (k + 1) * width)

        @pl.loop(0, units // chunk)
        def _(i, k=k, start=start, cols=cols):
            rows = pl.ds(pl.multiple_of(i * chunk, chunk), chunk)
            grad = block(k, rows)
            swish = swish_ref[rows, pl.ds(start, width)].astype(F32)
            slope = slope_ref[rows, pl.ds(start, width)].astype(F32)
            upact_ref[rows, cols] = (grad * swish).astype(BF16)
            gateact_ref[rows, cols] = (grad * slope).astype(BF16)

    contract_first = (((0,), (0,)), ((), ()))
    product = lax.dot_general(
        gateact_ref[...], gate_weight_ref[...], contract_first, preferred_element_type=F32
    )
    product = product + lax.dot_general(
        upact_ref[...], up_weight_ref[...], contract_first, preferred_element_type=F32
    )
    hold[...] = (product * SCALE_WIDTH).astype(BF16)
    for k in range(blocks):
        own = pl.multiple_of(k * width + core * half, half)
        their = pl.multiple_of(k * width + (1 - core) * half, half)
        mine_ref[k] = hold[pl.ds(own, half), :]
        low = other_ref.shape[0] - (blocks - k) * half - (16 if number == 3 else 0)
        other_ref[low : low + half, :] = hold[pl.ds(their, half), :]
    if number == 3:
        other_ref[blocks * half :, :] = jnp.zeros((16, other_ref.shape[1]), BF16)
        first = sums[0:1] + sums[2:3] + sums[4:5]
        second = sums[1:2] + sums[3:4] + sums[5:6]
        other_ref[blocks * half :, 0:128] = in_rows(first, second)
    elif number > 0:
        earlier = befores[1].shape[0]
        other_ref[0:earlier, :] = befores[1][...]


def input_group(number, place, grads, swish, slope, gate_weight, up_weight, *befores):
    units, tokens = swish.shape
    depth = gate_weight.shape[1]
    width = tokens // Z
    blocks = len(GROUPS[number])
    half = jax.ShapeDtypeStruct((blocks, width // 2, depth), BF16)
    if number == 3:
        other_rows = blocks * width // 2 + 16
    else:
        other_rows = sum(len(offsets) for offsets in GROUPS[: number + 1]) * width // 2
    other = jax.ShapeDtypeStruct((other_rows, depth), BF16)
    acts = jax.ShapeDtypeStruct((units, blocks * width), BF16)
    sums = jax.ShapeDtypeStruct((16, 128), F32)
    return pl.pallas_call(
        functools.partial(group_body, number, len(grads)),
        out_shape=[acts, acts, half, other, sums],
        in_specs=[SMEM] + [VMEM] * (4 + len(grads) + len(befores)),
        out_specs=[VMEM] * 5,
        scratch_shapes=[pltpu.VMEM((blocks * width, depth), BF16)],
        compiler_params=params(),
        cost_estimate=pl.CostEstimate(
            flops=4 * units * depth * blocks * width,
            bytes_accessed=10 * units * blocks * width + 4 * units * depth,
            transcendentals=0,
        ),
        name="input_group",
    )(place, *grads, swish, slope, gate_weight, up_weight, *befores)


def merge_body(place_ref, *refs):
    mine = refs[:SIDE]
    first_other_ref, last_other_ref, sums_ref, out_ref = refs[SIDE:]
    rows, depth = mine[0].shape[1:]
    parts = [(q * rows, slice(q * 128, (q + 1) * 128)) for q in range(depth // 128)]
    for number, offsets in enumerate(GROUPS):
        for k, offset in enumerate(offsets):
            chip = owner_of(place_ref, offset)
            for low, cols in parts:
                out_ref[chip, low : low + rows, :] = mine[number][k, :, cols]
    first = [offset for offsets in GROUPS[:3] for offset in offsets]
    for ref, offsets in ((first_other_ref, first), (last_other_ref, GROUPS[3])):
        for k, offset in enumerate(offsets):
            chip = owner_of(place_ref, -offset)
            for low, cols in parts:
                total = out_ref[chip, low : low + rows, :].astype(F32)
                total = total + ref[k * rows : (k + 1) * rows, cols].astype(F32)
                out_ref[chip, low : low + rows, :] = total.astype(BF16)
    their = last_other_ref[len(GROUPS[3]) * rows :, 0:128].astype(F32)
    first, second = from_rows(sums_ref[...] + their)
    sums = in_rows(jnp.broadcast_to(first, (1, 128)), jnp.broadcast_to(second, (1, 128)))
    for chip in range(out_ref.shape[0]):
        out_ref[chip, len(parts) * rows :, :] = sums


def merge_cores(place, mine, first_other, last_other, sums):
    _, rows, depth = mine[0].shape
    return pl.pallas_call(
        merge_body,
        out_shape=jax.ShapeDtypeStruct((CHIPS, rows * depth // 128 + 16, 128), BF16),
        in_specs=[SMEM] + [VMEM] * (SIDE + 3),
        out_specs=VMEM,
        compiler_params=params(),
        cost_estimate=pl.CostEstimate(
            flops=CHIPS * rows * depth, bytes_accessed=6 * CHIPS * rows * depth, transcendentals=0
        ),
        name="merge_cores",
    )(place, *mine, first_other, last_other, sums)


def finish_body(arrived_ref, update_hbm, grad_input_ref, step_ref, ratio_ref, update_ref, sem):
    copy = start(update_hbm, update_ref, sem)
    chips = arrived_ref.shape[0]
    rows, depth = grad_input_ref.shape
    for q in range(depth // 128):
        for low in range(0, rows, 32):
            part = slice(q * rows + low, q * rows + low + 32)
            total = arrived_ref[0, part, :].astype(F32)
            for chip in range(1, chips):
                total = total + arrived_ref[chip, part, :].astype(F32)
            grad_input_ref[low : low + 32, q * 128 : (q + 1) * 128] = total.astype(BF16)
    part = slice(rows * depth // 128, rows * depth // 128 + 16)
    sums = arrived_ref[0, part, :].astype(F32)
    for chip in range(1, chips):
        sums = sums + arrived_ref[chip, part, :].astype(F32)
    weight_total = sums[0:1] + sums[2:3] + sums[4:5]
    update_total = sums[1:2] + sums[3:4] + sums[5:6]
    ratio = jnp.sqrt(weight_total) / jnp.sqrt(update_total + 1e-06)
    ratio_ref[...] = ratio
    ratio = ratio[:, 0:1]
    step = 16
    copy.wait()

    @pl.loop(0, update_ref.shape[0] // step)
    def _(i):
        part = pl.ds(pl.multiple_of(i * step, step), step)
        step_ref[part, :] = (ratio * update_ref[part, :]).astype(BF16)


def finish(arrived, update):
    chips, rows, _ = arrived.shape
    units, depth = update.shape
    return pl.pallas_call(
        finish_body,
        out_shape=[
            jax.ShapeDtypeStruct(((rows - 16) * 128 // depth, depth), BF16),
            jax.ShapeDtypeStruct((units, depth), BF16),
            jax.ShapeDtypeStruct((1, 128), F32),
        ],
        in_specs=[VMEM, HBM],
        out_specs=[VMEM] * 3,
        scratch_shapes=[pltpu.VMEM((units, depth), F32), DMA],
        compiler_params=params(),
        cost_estimate=pl.CostEstimate(
            flops=chips * rows * 128,
            bytes_accessed=2 * chips * rows * 128 + 6 * units * depth,
            transcendentals=0,
        ),
        name="finish",
    )(arrived, update)


def weight_grads_body(place_ref, *refs):
    gateacts, upacts = refs[:SIDE], refs[SIDE : 2 * SIDE]
    mine_ref, other_ref, grad_gate_ref, grad_up_ref, tokens, act = refs[2 * SIDE :]
    core = place_ref[1]
    chips, half, _ = mine_ref.shape
    width = 2 * half
    for chip in range(chips):
        own = pl.multiple_of(chip * width + core * half, half)
        their = pl.multiple_of(chip * width + (1 - core) * half, half)
        tokens[pl.ds(own, half), :] = mine_ref[chip]
        tokens[pl.ds(their, half), :] = other_ref[chip]
    for acts, out_ref in ((gateacts, grad_gate_ref), (upacts, grad_up_ref)):
        for number, offsets in enumerate(GROUPS):
            for k, offset in enumerate(offsets):
                start = pl.multiple_of(owner_of(place_ref, offset) * width, width)
                act[:, pl.ds(start, width)] = acts[number][:, k * width : (k + 1) * width]
        product = lax.dot_general(
            act[...], tokens[...], (((1,), (0,)), ((), ())), preferred_element_type=F32
        )
        out_ref[...] = (product * SCALE_WIDTH).astype(BF16)


def weight_grads(place, gateacts, upacts, mine, other):
    chips, half, depth = mine.shape
    units = gateacts[0].shape[0]
    tokens = chips * half * 2
    out = jax.ShapeDtypeStruct((units, depth), BF16)
    return pl.pallas_call(
        weight_grads_body,
        out_shape=[out, out],
        in_specs=[SMEM] + [VMEM] * (2 * SIDE + 2),
        out_specs=[VMEM] * 2,
        scratch_shapes=[pltpu.VMEM((tokens, depth), BF16), pltpu.VMEM((units, tokens), BF16)],
        compiler_params=params(),
        cost_estimate=pl.CostEstimate(
            flops=4 * units * depth * tokens,
            bytes_accessed=4 * units * tokens + 2 * tokens * depth + 4 * units * depth,
            transcendentals=0,
        ),
        name="weight_grads",
    )(place, *gateacts, *upacts, mine, other)


def shards(
    tokens, cotangent, gate_pre, up_act, gate_weight, up_weight, down_weight, moment_m, moment_v
):
    z = lax.axis_index("row")
    core = lax.axis_index("col") & 1
    place = jnp.stack([z, core, 1 - 2 * core]).astype(jnp.int32)

    acts = jnp.concatenate([gate_pre.T, up_act.T], axis=0)
    acts, cotangent = lax.optimization_barrier((acts, cotangent))
    acts = lax.all_gather(acts, "row", axis=0, tiled=False)
    cot_mine, cot_other = gather_chips(cotangent)
    cotangent_all, zero, far, odd, even, give_odd, give_even = hidden_partial(
        place, cot_mine, cot_other, down_weight
    )
    tokens, _ = lax.optimization_barrier((tokens, cot_other))
    tok_mine, tok_other = gather_chips(tokens)
    swish, slope, hidden = activations(acts)
    new_m, new_v, update, sums = down_update(
        hidden, cotangent_all, down_weight, moment_m, moment_v
    )
    own, other, (tok_other, swish, _) = reduce_z(
        zero, far, odd, even, give_odd, give_even, (tok_other, swish, sums)
    )

    gate_weight, up_weight = gate_weight.T, up_weight.T

    def group(number, grads, *befores):
        return input_group(
            number, place, grads, swish, slope, gate_weight, up_weight, *befores
        )

    others, owns = [other], [own]
    for _ in range(3):
        others.append(shift_z(others[-1], 2))
        owns.append(shift_z(owns[-1], 2))
    even_other, even = jnp.stack(others), jnp.stack(owns)
    odd_other = shift_z(even_other, 1)
    odd = shift_z(even, 1)
    far = shift_z(owns[3], 2)
    ahead_even = swap_core(even_other[1:])
    group_0 = group(0, (even,))
    group_1 = group(1, (ahead_even,), group_0[4], group_0[3])
    odd_other, odd, far, group_0, group_1 = lax.optimization_barrier(
        (odd_other, odd, far, group_0, group_1)
    )
    ahead_odd = swap_core(odd_other)
    group_2 = group(2, (odd,), group_1[4], group_1[3])
    group_3 = group(3, (ahead_odd, far), group_2[4])
    gateacts, upacts, mine, _, _ = zip(group_0, group_1, group_2, group_3)
    merged = merge_cores(
        place, mine, swap_core(group_2[3]), swap_core(group_3[3]), group_3[4]
    )
    merged, tok_mine = lax.optimization_barrier((merged, tok_mine))
    arrived = exchange_chips(merged)
    grad_gate, grad_up = weight_grads(place, gateacts, upacts, tok_mine, tok_other)
    arrived, grad_gate, grad_up = lax.optimization_barrier((arrived, grad_gate, grad_up))
    grad_input, step_down, ratio = finish(arrived, update)
    return grad_input, grad_gate.T, grad_up.T, new_m, new_v, step_down, ratio[0, 0]


def solution(mesh):
    in_specs = (
        P("col", "row"),
        P("col", "row"),
        P("row", "col"),
        P("row", "col"),
        P("row", "col"),
        P("row", "col"),
        P("col", "row"),
        P("col", "row"),
        P("col", "row"),
    )
    out_specs = (
        P("col", "row"),
        P("row", "col"),
        P("row", "col"),
        P("col", "row"),
        P("col", "row"),
        P("col", "row"),
        P(),
    )
    return jax.shard_map(shards, mesh=mesh, in_specs=in_specs, out_specs=out_specs, check_vma=False)
```

```python
import functools

import jax
import jax.numpy as jnp
from jax import lax
from jax.experimental import pallas as pl
from jax.experimental.pallas import tpu as pltpu
from jax.sharding import PartitionSpec as P

D = 8192
FF = 14336
Z = 16
SIDE = 4
CHIPS = 16
COLS = 32
SCALE_WIDTH = float(D) ** (-0.5)
SCALE_HIDDEN = float(FF) ** (-0.5)
BF16 = jnp.bfloat16
F32 = jnp.float32
VMEM = pl.BlockSpec(memory_space=pltpu.VMEM)
SMEM = pl.BlockSpec(memory_space=pltpu.SMEM)
HBM = pl.BlockSpec(memory_space=pltpu.HBM)
DMA = pltpu.SemaphoreType.DMA


def params(mebibytes=20):
    return pltpu.CompilerParams(vmem_limit_bytes=mebibytes * 1024 * 1024)


def shift_z(v, step):
    pairs = []
    for z in range(Z):
        for col in range(COLS):
            way = step if col % 2 == 0 else -step
            pairs.append((z * COLS + col, (z + way) % Z * COLS + col))
    return lax.ppermute(v, ("row", "col"), pairs)


def swap_core(v):
    return lax.ppermute(v, "col", [(c, c ^ 1) for c in range(COLS)])


def exchange_chips(v):
    groups = [[2 * chip + core for chip in range(CHIPS)] for core in range(2)]
    return lax.all_to_all(v, "col", 0, 0, axis_index_groups=groups, tiled=True)


def gather_chips(v):
    mine = exchange_chips(jnp.broadcast_to(v[None], (CHIPS, *v.shape)))
    return mine, swap_core(mine)


def add(*terms):
    total = terms[0].astype(F32)
    for term in terms[1:]:
        total = total + term.astype(F32)
    return total.astype(BF16)


def reduce_z(zero, far, odd, even, give_odd, give_even, beside):
    own = shift_z(odd, 1)
    got_odd = swap_core(give_odd)
    their = shift_z(got_odd, 1)
    far = shift_z(far, SIDE)
    got_even = swap_core(give_even)
    moving_their = add(got_even[2], their[3])
    moving = add(even[2], own[3])
    done = []
    for k in (2, 1, 0):
        moving_their = shift_z(moving_their, 2)
        moving = shift_z(moving, 2)
        if k < 2:
            moving, ready = lax.optimization_barrier((moving, beside[1 - k]))
            done.append(ready)
        if k == 2:
            moving = add(moving, even[1], own[2], far)
        elif k == 1:
            moving = add(moving, even[0], own[1])
        if k > 0:
            moving_their = add(moving_their, got_even[k - 1], their[k])
    extra = done[1]
    other = jnp.concatenate([add(moving_their, their[0]), jnp.zeros_like(extra)], axis=0)
    mine = jnp.concatenate([add(zero, moving, own[0]), extra], axis=0)
    got_mine = swap_core(other)
    got_other = swap_core(mine)
    return add(mine, got_mine), add(other, got_other), done


GROUPS = ((0, -2, -4, -6), (2, 4, 6), (-1, -3, -5, -7), (1, 3, 5, 7, -8))


def owner_of(place_ref, offset):
    z, way = place_ref[0], place_ref[2]
    return lax.rem(z + way * offset + Z, Z)


def hidden_partial_body(place_ref, mine_ref, other_ref, weight_ref, cot_ref, *refs):
    zero_ref, far_ref, odd_ref, even_ref, give_odd_ref, give_even_ref, hold = refs
    core = place_ref[1]
    chips, rows, _ = mine_ref.shape
    for chip in range(chips):
        own = pl.multiple_of(chip * 2 * rows + core * rows, rows)
        their = pl.multiple_of(chip * 2 * rows + (1 - core) * rows, rows)
        cot_ref[pl.ds(own, rows), :] = mine_ref[chip]
        cot_ref[pl.ds(their, rows), :] = other_ref[chip]
    tokens = cot_ref.shape[0]
    width = tokens // Z
    span = tokens // SIDE
    for part in range(SIDE):
        product = lax.dot_general(
            weight_ref[...],
            cot_ref[part * span : (part + 1) * span, :],
            (((1,), (1,)), ((), ())),
            preferred_element_type=F32,
        )
        hold[:, part * span : (part + 1) * span] = (product * SCALE_HIDDEN).astype(BF16)

    def block(offset):
        low = pl.multiple_of(owner_of(place_ref, offset) * width, width)
        return hold[:, pl.ds(low, width)]

    zero_ref[...] = block(0)
    far_ref[...] = block(8)
    for k, offset in enumerate((1, 3, 5, 7)):
        odd_ref[k] = block(offset)
        give_odd_ref[k] = block(-offset)
    for k, offset in enumerate((2, 4, 6)):
        even_ref[k] = block(offset)
        give_even_ref[k] = block(-offset)


def hidden_partial(place, mine, other, weight):
    units, depth = weight.shape
    tokens = mine.shape[0] * mine.shape[1] * 2
    width = tokens // Z
    shapes = [(tokens, depth), (units, width), (units, width)]
    shapes += [(count, units, width) for count in (4, 3, 4, 3)]
    return pl.pallas_call(
        hidden_partial_body,
        out_shape=[jax.ShapeDtypeStruct(shape, BF16) for shape in shapes],
        in_specs=[SMEM] + [VMEM] * 3,
        out_specs=[VMEM] * 7,
        scratch_shapes=[pltpu.VMEM((units, tokens), BF16)],
        compiler_params=params(),
        cost_estimate=pl.CostEstimate(
            flops=2 * units * depth * tokens,
            bytes_accessed=2 * (2 * tokens * depth + units * depth + units * tokens),
            transcendentals=0,
        ),
        name="hidden_partial",
    )(place, mine, other, weight)


def start(source, target, sem):
    copy = pltpu.make_async_copy(source, target, sem)
    copy.start()
    return copy


def activations_body(acts_hbm, *refs):
    outs, (acts_ref, swish_ref, slope_ref, hidden_ref, in_sems, out_sems) = refs[:3], refs[3:]
    blocks, units, width = acts_ref.shape
    units = units // 2
    chunk = 64
    arriving = [start(acts_hbm.at[k], acts_ref.at[k], in_sems.at[k]) for k in range(blocks)]
    leaving = []
    for k in range(blocks):
        cols = slice(k * width, (k + 1) * width)
        arriving[k].wait()

        @pl.loop(0, units // chunk)
        def _(i, k=k, cols=cols):
            low = pl.multiple_of(i * chunk, chunk)
            rows = pl.ds(low, chunk)
            g = acts_ref[k, rows, :].astype(F32)
            u = acts_ref[k, pl.ds(low + units, chunk), :].astype(F32)
            s = jax.nn.sigmoid(g)
            swish = g * s
            slope = u * s * (1.0 + g * (1.0 - s))
            hidden_ref[rows, cols] = (swish * u).astype(BF16)
            swish_ref[rows, cols] = swish.astype(BF16)
            slope_ref[rows, cols] = slope.astype(BF16)

        if k % 4 == 3:
            part = slice((k - 3) * width, (k + 1) * width)
            for n, ref in enumerate((swish_ref, slope_ref, hidden_ref)):
                leaving.append(
                    start(ref.at[:, part], outs[n].at[:, part], out_sems.at[n, k // 4])
                )
    for copy in leaving:
        copy.wait()


def activations(acts):
    blocks, units, width = acts.shape
    units, tokens = units // 2, blocks * width
    return pl.pallas_call(
        activations_body,
        out_shape=[jax.ShapeDtypeStruct((units, tokens), BF16)] * 3,
        in_specs=[HBM],
        out_specs=[HBM] * 3,
        scratch_shapes=[pltpu.VMEM(acts.shape, BF16)]
        + [pltpu.VMEM((units, tokens), BF16)] * 3
        + [DMA((blocks,)), DMA((3, blocks // 4))],
        compiler_params=params(56),
        cost_estimate=pl.CostEstimate(
            flops=30 * units * tokens,
            bytes_accessed=10 * units * tokens,
            transcendentals=units * tokens,
        ),
        name="activations",
    )(acts)


def down_body(hidden_hbm, cot_hbm, weight_hbm, m_hbm, v_hbm, *refs):
    outs, sums_ref = refs[:3], refs[3]
    hidden_ref, cot_ref, weight_ref, m_ref, v_ref = refs[4:9]
    new_m_ref, new_v_ref, update_ref, product, sems, out_sems = refs[9:]
    units = weight_ref.shape[0]
    span = cot_ref.shape[0] // SIDE
    parts = [slice(k * span, (k + 1) * span) for k in range(SIDE)]
    arriving = []
    for k, part in enumerate(parts):
        arriving.append(
            (
                start(hidden_hbm.at[:, part], hidden_ref.at[:, part], sems.at[0, k]),
                start(cot_hbm.at[part], cot_ref.at[part], sems.at[1, k]),
            )
        )
    moments = [
        start(weight_hbm, weight_ref, sems.at[2, 0]),
        start(m_hbm, m_ref, sems.at[2, 1]),
        start(v_hbm, v_ref, sems.at[2, 2]),
    ]
    for k, part in enumerate(parts):
        for copy in arriving[k]:
            copy.wait()
        term = lax.dot_general(
            hidden_ref[:, part],
            cot_ref[part, :],
            (((1,), (0,)), ((), ())),
            preferred_element_type=F32,
        )
        product[...] = term if k == 0 else product[...] + term
    for copy in moments:
        copy.wait()
    step = 16
    depth = product.shape[1]

    def optimizer(i, carry):
        weight_sum, update_sum = carry
        rows = pl.ds(pl.multiple_of(i * step, step), step)
        grad = product[rows, :] * SCALE_HIDDEN
        weight = weight_ref[rows, :].astype(F32)
        first = 0.9 * m_ref[rows, :].astype(F32) + 0.1 * grad
        second = 0.95 * v_ref[rows, :].astype(F32) + 0.05 * grad * grad
        update = first / (jnp.sqrt(second) + 1e-08) + 0.1 * weight
        new_m_ref[rows, :] = first.astype(BF16)
        new_v_ref[rows, :] = second.astype(BF16)
        update_ref[rows, :] = update
        return weight_sum + weight * weight, update_sum + update * update

    zero = jnp.zeros((step, depth), F32)
    weight_sum, update_sum = lax.fori_loop(0, units // step, optimizer, (zero, zero))
    leaving = [
        start(ref, outs[n], out_sems.at[n]) for n, ref in enumerate((new_m_ref, new_v_ref, update_ref))
    ]
    weight_sum = jnp.sum(weight_sum, axis=0, keepdims=True)
    update_sum = jnp.sum(update_sum, axis=0, keepdims=True)
    lanes = sums_ref.shape[1]
    parts = [slice(k, k + lanes) for k in range(0, depth, lanes)]
    weight_sum = sum(weight_sum[:, part] for part in parts)
    update_sum = sum(update_sum[:, part] for part in parts)
    sums_ref[...] = in_rows(weight_sum, update_sum)
    for copy in leaving:
        copy.wait()


def in_rows(first, second):
    row = lax.broadcasted_iota(jnp.int32, (16, first.shape[1]), 0)
    value = jnp.where((row & 1) == 0, first, second)
    high = value.astype(BF16).astype(F32)
    middle = (value - high).astype(BF16).astype(F32)
    low = value - high - middle
    rest = jnp.where(row < 4, middle, jnp.where(row < 6, low, 0.0))
    return jnp.where(row < 2, high, rest).astype(BF16)


def from_rows(rows):
    first = rows[0:1] + rows[2:3] + rows[4:5]
    second = rows[1:2] + rows[3:4] + rows[5:6]
    return jnp.sum(first, axis=1, keepdims=True), jnp.sum(second, axis=1, keepdims=True)


def down_update(hidden, cotangent, weight, moment_m, moment_v):
    units, tokens = hidden.shape
    depth = cotangent.shape[1]
    shapes = [
        jax.ShapeDtypeStruct((units, depth), BF16),
        jax.ShapeDtypeStruct((units, depth), BF16),
        jax.ShapeDtypeStruct((units, depth), F32),
        jax.ShapeDtypeStruct((16, 128), BF16),
    ]
    return pl.pallas_call(
        down_body,
        out_shape=shapes,
        in_specs=[HBM] * 5,
        out_specs=[HBM] * 3 + [VMEM],
        scratch_shapes=[pltpu.VMEM((units, tokens), BF16), pltpu.VMEM((tokens, depth), BF16)]
        + [pltpu.VMEM((units, depth), BF16)] * 5
        + [pltpu.VMEM((units, depth), F32)] * 2
        + [DMA((3, SIDE)), DMA((3,))],
        compiler_params=params(56),
        cost_estimate=pl.CostEstimate(
            flops=2 * units * depth * tokens,
            bytes_accessed=2 * units * tokens + 2 * tokens * depth + 14 * units * depth,
            transcendentals=0,
        ),
        name="down_update",
    )(hidden, cotangent, weight, moment_m, moment_v)


def group_body(number, count, place_ref, *refs):
    grads = refs[:count]
    swish_ref, slope_ref, gate_weight_ref, up_weight_ref = refs[count : count + 4]
    befores = refs[count + 4 : -6]
    gateact_ref, upact_ref, mine_ref, other_ref, sums_ref, hold = refs[-6:]
    units = gateact_ref.shape[0]
    blocks, half, _ = mine_ref.shape
    width = 2 * half
    chunk = 64
    core = place_ref[1]

    def block(k, rows):
        if k == 4:
            return grads[1][rows, :].astype(F32)
        return grads[0][k, rows, :].astype(F32)

    sums = befores[0][...] if befores else 0.0
    for k in range(blocks):
        sums = sums + block(k, slice(units, units + 16))
    sums_ref[...] = sums
    for k, offset in enumerate(GROUPS[number]):
        start = pl.multiple_of(owner_of(place_ref, offset) * width, width)
        cols = slice(k * width, (k + 1) * width)

        @pl.loop(0, units // chunk)
        def _(i, k=k, start=start, cols=cols):
            rows = pl.ds(pl.multiple_of(i * chunk, chunk), chunk)
            grad = block(k, rows)
            swish = swish_ref[rows, pl.ds(start, width)].astype(F32)
            slope = slope_ref[rows, pl.ds(start, width)].astype(F32)
            upact_ref[rows, cols] = (grad * swish).astype(BF16)
            gateact_ref[rows, cols] = (grad * slope).astype(BF16)

    contract_first = (((0,), (0,)), ((), ()))
    product = lax.dot_general(
        gateact_ref[...], gate_weight_ref[...], contract_first, preferred_element_type=F32
    )
    product = product + lax.dot_general(
        upact_ref[...], up_weight_ref[...], contract_first, preferred_element_type=F32
    )
    hold[...] = (product * SCALE_WIDTH).astype(BF16)
    for k in range(blocks):
        own = pl.multiple_of(k * width + core * half, half)
        their = pl.multiple_of(k * width + (1 - core) * half, half)
        mine_ref[k] = hold[pl.ds(own, half), :]
        low = other_ref.shape[0] - (blocks - k) * half - (16 if number == 3 else 0)
        other_ref[low : low + half, :] = hold[pl.ds(their, half), :]
    if number == 3:
        other_ref[blocks * half :, :] = jnp.zeros((16, other_ref.shape[1]), BF16)
        first = sums[0:1] + sums[2:3] + sums[4:5]
        second = sums[1:2] + sums[3:4] + sums[5:6]
        other_ref[blocks * half :, 0:128] = in_rows(first, second)
    elif number > 0:
        earlier = befores[1].shape[0]
        other_ref[0:earlier, :] = befores[1][...]


def input_group(number, place, grads, swish, slope, gate_weight, up_weight, *befores):
    units, tokens = swish.shape
    depth = gate_weight.shape[1]
    width = tokens // Z
    blocks = len(GROUPS[number])
    half = jax.ShapeDtypeStruct((blocks, width // 2, depth), BF16)
    if number == 3:
        other_rows = blocks * width // 2 + 16
    else:
        other_rows = sum(len(offsets) for offsets in GROUPS[: number + 1]) * width // 2
    other = jax.ShapeDtypeStruct((other_rows, depth), BF16)
    acts = jax.ShapeDtypeStruct((units, blocks * width), BF16)
    sums = jax.ShapeDtypeStruct((16, 128), F32)
    return pl.pallas_call(
        functools.partial(group_body, number, len(grads)),
        out_shape=[acts, acts, half, other, sums],
        in_specs=[SMEM] + [VMEM] * (4 + len(grads) + len(befores)),
        out_specs=[VMEM] * 5,
        scratch_shapes=[pltpu.VMEM((blocks * width, depth), BF16)],
        compiler_params=params(),
        cost_estimate=pl.CostEstimate(
            flops=4 * units * depth * blocks * width,
            bytes_accessed=10 * units * blocks * width + 4 * units * depth,
            transcendentals=0,
        ),
        name="input_group",
    )(place, *grads, swish, slope, gate_weight, up_weight, *befores)


def merge_body(place_ref, *refs):
    mine = refs[:SIDE]
    first_other_ref, last_other_ref, sums_ref, out_ref = refs[SIDE:]
    rows, depth = mine[0].shape[1:]
    parts = [(q * rows, slice(q * 128, (q + 1) * 128)) for q in range(depth // 128)]
    for number, offsets in enumerate(GROUPS):
        for k, offset in enumerate(offsets):
            chip = owner_of(place_ref, offset)
            for low, cols in parts:
                out_ref[chip, low : low + rows, :] = mine[number][k, :, cols]
    first = [offset for offsets in GROUPS[:3] for offset in offsets]
    for ref, offsets in ((first_other_ref, first), (last_other_ref, GROUPS[3])):
        for k, offset in enumerate(offsets):
            chip = owner_of(place_ref, -offset)
            for low, cols in parts:
                total = out_ref[chip, low : low + rows, :].astype(F32)
                total = total + ref[k * rows : (k + 1) * rows, cols].astype(F32)
                out_ref[chip, low : low + rows, :] = total.astype(BF16)
    their = last_other_ref[len(GROUPS[3]) * rows :, 0:128].astype(F32)
    first, second = from_rows(sums_ref[...] + their)
    sums = in_rows(jnp.broadcast_to(first, (1, 128)), jnp.broadcast_to(second, (1, 128)))
    for chip in range(out_ref.shape[0]):
        out_ref[chip, len(parts) * rows :, :] = sums


def merge_cores(place, mine, first_other, last_other, sums):
    _, rows, depth = mine[0].shape
    return pl.pallas_call(
        merge_body,
        out_shape=jax.ShapeDtypeStruct((CHIPS, rows * depth // 128 + 16, 128), BF16),
        in_specs=[SMEM] + [VMEM] * (SIDE + 3),
        out_specs=VMEM,
        compiler_params=params(),
        cost_estimate=pl.CostEstimate(
            flops=CHIPS * rows * depth, bytes_accessed=6 * CHIPS * rows * depth, transcendentals=0
        ),
        name="merge_cores",
    )(place, *mine, first_other, last_other, sums)


def finish_body(arrived_ref, update_hbm, grad_input_ref, step_ref, ratio_ref, update_ref, sem):
    copy = start(update_hbm, update_ref, sem)
    chips = arrived_ref.shape[0]
    rows, depth = grad_input_ref.shape
    for q in range(depth // 128):
        for low in range(0, rows, 32):
            part = slice(q * rows + low, q * rows + low + 32)
            total = arrived_ref[0, part, :].astype(F32)
            for chip in range(1, chips):
                total = total + arrived_ref[chip, part, :].astype(F32)
            grad_input_ref[low : low + 32, q * 128 : (q + 1) * 128] = total.astype(BF16)
    part = slice(rows * depth // 128, rows * depth // 128 + 16)
    sums = arrived_ref[0, part, :].astype(F32)
    for chip in range(1, chips):
        sums = sums + arrived_ref[chip, part, :].astype(F32)
    weight_total = sums[0:1] + sums[2:3] + sums[4:5]
    update_total = sums[1:2] + sums[3:4] + sums[5:6]
    ratio = jnp.sqrt(weight_total) / jnp.sqrt(update_total + 1e-06)
    ratio_ref[...] = ratio
    ratio = ratio[:, 0:1]
    step = 16
    copy.wait()

    @pl.loop(0, update_ref.shape[0] // step)
    def _(i):
        part = pl.ds(pl.multiple_of(i * step, step), step)
        step_ref[part, :] = (ratio * update_ref[part, :]).astype(BF16)


def finish(arrived, update):
    chips, rows, _ = arrived.shape
    units, depth = update.shape
    return pl.pallas_call(
        finish_body,
        out_shape=[
            jax.ShapeDtypeStruct(((rows - 16) * 128 // depth, depth), BF16),
            jax.ShapeDtypeStruct((units, depth), BF16),
            jax.ShapeDtypeStruct((1, 128), F32),
        ],
        in_specs=[VMEM, HBM],
        out_specs=[VMEM] * 3,
        scratch_shapes=[pltpu.VMEM((units, depth), F32), DMA],
        compiler_params=params(),
        cost_estimate=pl.CostEstimate(
            flops=chips * rows * 128,
            bytes_accessed=2 * chips * rows * 128 + 6 * units * depth,
            transcendentals=0,
        ),
        name="finish",
    )(arrived, update)


def weight_grads_body(place_ref, *refs):
    gateacts, upacts = refs[:SIDE], refs[SIDE : 2 * SIDE]
    mine_ref, other_ref, grad_gate_ref, grad_up_ref, tokens, act = refs[2 * SIDE :]
    core = place_ref[1]
    chips, half, _ = mine_ref.shape
    width = 2 * half
    for chip in range(chips):
        own = pl.multiple_of(chip * width + core * half, half)
        their = pl.multiple_of(chip * width + (1 - core) * half, half)
        tokens[pl.ds(own, half), :] = mine_ref[chip]
        tokens[pl.ds(their, half), :] = other_ref[chip]
    for acts, out_ref in ((gateacts, grad_gate_ref), (upacts, grad_up_ref)):
        for number, offsets in enumerate(GROUPS):
            for k, offset in enumerate(offsets):
                start = pl.multiple_of(owner_of(place_ref, offset) * width, width)
                act[:, pl.ds(start, width)] = acts[number][:, k * width : (k + 1) * width]
        product = lax.dot_general(
            act[...], tokens[...], (((1,), (0,)), ((), ())), preferred_element_type=F32
        )
        out_ref[...] = (product * SCALE_WIDTH).astype(BF16)


def weight_grads(place, gateacts, upacts, mine, other):
    chips, half, depth = mine.shape
    units = gateacts[0].shape[0]
    tokens = chips * half * 2
    out = jax.ShapeDtypeStruct((units, depth), BF16)
    return pl.pallas_call(
        weight_grads_body,
        out_shape=[out, out],
        in_specs=[SMEM] + [VMEM] * (2 * SIDE + 2),
        out_specs=[VMEM] * 2,
        scratch_shapes=[pltpu.VMEM((tokens, depth), BF16), pltpu.VMEM((units, tokens), BF16)],
        compiler_params=params(),
        cost_estimate=pl.CostEstimate(
            flops=4 * units * depth * tokens,
            bytes_accessed=4 * units * tokens + 2 * tokens * depth + 4 * units * depth,
            transcendentals=0,
        ),
        name="weight_grads",
    )(place, *gateacts, *upacts, mine, other)


def shards(
    tokens, cotangent, gate_pre, up_act, gate_weight, up_weight, down_weight, moment_m, moment_v
):
    z = lax.axis_index("row")
    core = lax.axis_index("col") & 1
    place = jnp.stack([z, core, 1 - 2 * core]).astype(jnp.int32)

    acts = jnp.concatenate([gate_pre.T, up_act.T], axis=0)
    acts, cotangent = lax.optimization_barrier((acts, cotangent))
    acts = lax.all_gather(acts, "row", axis=0, tiled=False)
    cot_mine, cot_other = gather_chips(cotangent)
    cotangent_all, zero, far, odd, even, give_odd, give_even = hidden_partial(
        place, cot_mine, cot_other, down_weight
    )
    tokens, _ = lax.optimization_barrier((tokens, cot_other))
    tok_mine, tok_other = gather_chips(tokens)
    swish, slope, hidden = activations(acts)
    new_m, new_v, update, sums = down_update(
        hidden, cotangent_all, down_weight, moment_m, moment_v
    )
    own, other, ((swish, tok_other), _) = reduce_z(
        zero, far, odd, even, give_odd, give_even, ((swish, tok_other), sums)
    )

    gate_weight, up_weight = gate_weight.T, up_weight.T

    def group(number, grads, *befores):
        return input_group(
            number, place, grads, swish, slope, gate_weight, up_weight, *befores
        )

    others, owns = [other], [own]
    for _ in range(3):
        others.append(shift_z(others[-1], 2))
        owns.append(shift_z(owns[-1], 2))
    even_other, even = jnp.stack(others), jnp.stack(owns)
    odd_other = shift_z(even_other, 1)
    odd = shift_z(even, 1)
    far = shift_z(owns[3], 2)
    ahead_even = swap_core(even_other[1:])
    group_0 = group(0, (even,))
    group_1 = group(1, (ahead_even,), group_0[4], group_0[3])
    odd_other, odd, far, group_0, group_1 = lax.optimization_barrier(
        (odd_other, odd, far, group_0, group_1)
    )
    ahead_odd = swap_core(odd_other)
    group_2 = group(2, (odd,), group_1[4], group_1[3])
    group_3 = group(3, (ahead_odd, far), group_2[4])
    gateacts, upacts, mine, _, _ = zip(group_0, group_1, group_2, group_3)
    merged = merge_cores(
        place, mine, swap_core(group_2[3]), swap_core(group_3[3]), group_3[4]
    )
    merged, tok_mine = lax.optimization_barrier((merged, tok_mine))
    arrived = exchange_chips(merged)
    grad_gate, grad_up = weight_grads(place, gateacts, upacts, tok_mine, tok_other)
    arrived, grad_gate, grad_up = lax.optimization_barrier((arrived, grad_gate, grad_up))
    grad_input, step_down, ratio = finish(arrived, update)
    return grad_input, grad_gate.T, grad_up.T, new_m, new_v, step_down, ratio[0, 0]


def solution(mesh):
    in_specs = (
        P("col", "row"),
        P("col", "row"),
        P("row", "col"),
        P("row", "col"),
        P("row", "col"),
        P("row", "col"),
        P("col", "row"),
        P("col", "row"),
        P("col", "row"),
    )
    out_specs = (
        P("col", "row"),
        P("row", "col"),
        P("row", "col"),
        P("col", "row"),
        P("col", "row"),
        P("col", "row"),
        P(),
    )
    return jax.shard_map(shards, mesh=mesh, in_specs=in_specs, out_specs=out_specs, check_vma=False)
```

```python
import functools

import jax
import jax.numpy as jnp
from jax import lax
from jax.experimental import pallas as pl
from jax.experimental.pallas import tpu as pltpu
from jax.sharding import PartitionSpec as P

D = 8192
FF = 14336
Z = 16
SIDE = 4
CHIPS = 16
COLS = 32
SCALE_WIDTH = float(D) ** (-0.5)
SCALE_HIDDEN = float(FF) ** (-0.5)
BF16 = jnp.bfloat16
F32 = jnp.float32
VMEM = pl.BlockSpec(memory_space=pltpu.VMEM)
SMEM = pl.BlockSpec(memory_space=pltpu.SMEM)
HBM = pl.BlockSpec(memory_space=pltpu.HBM)
DMA = pltpu.SemaphoreType.DMA


def params(mebibytes=20):
    return pltpu.CompilerParams(vmem_limit_bytes=mebibytes * 1024 * 1024)


def shift_z(v, step):
    pairs = []
    for z in range(Z):
        for col in range(COLS):
            way = step if col % 2 == 0 else -step
            pairs.append((z * COLS + col, (z + way) % Z * COLS + col))
    return lax.ppermute(v, ("row", "col"), pairs)


def swap_core(v):
    return lax.ppermute(v, "col", [(c, c ^ 1) for c in range(COLS)])


def exchange_chips(v):
    groups = [[2 * chip + core for chip in range(CHIPS)] for core in range(2)]
    return lax.all_to_all(v, "col", 0, 0, axis_index_groups=groups, tiled=True)


def gather_chips(v):
    mine = exchange_chips(jnp.broadcast_to(v[None], (CHIPS, *v.shape)))
    return mine, swap_core(mine)


def add(*terms):
    total = terms[0].astype(F32)
    for term in terms[1:]:
        total = total + term.astype(F32)
    return total.astype(BF16)


def reduce_z(zero, far, odd, even, give_odd, give_even, beside):
    own = shift_z(odd, 1)
    got_odd = swap_core(give_odd)
    their = shift_z(got_odd, 1)
    far = shift_z(far, SIDE)
    got_even = swap_core(give_even)
    moving_their = add(got_even[2], their[3])
    moving = add(even[2], own[3])
    done = []
    for k in (2, 1, 0):
        moving_their = shift_z(moving_their, 2)
        moving = shift_z(moving, 2)
        if k < 2:
            moving, ready = lax.optimization_barrier((moving, beside[1 - k]))
            done.append(ready)
        if k == 2:
            moving = add(moving, even[1], own[2], far)
        elif k == 1:
            moving = add(moving, even[0], own[1])
        if k > 0:
            moving_their = add(moving_their, got_even[k - 1], their[k])
    extra = done[1]
    other = jnp.concatenate([add(moving_their, their[0]), jnp.zeros_like(extra)], axis=0)
    mine = jnp.concatenate([add(zero, moving, own[0]), extra], axis=0)
    got_mine = swap_core(other)
    got_other = swap_core(mine)
    return add(mine, got_mine), add(other, got_other), done


GROUPS = ((0, -2, -4, -6), (2, 4, 6), (-1, -3, -5, -7), (1, 3, 5, 7, -8))


def owner_of(place_ref, offset):
    z, way = place_ref[0], place_ref[2]
    return lax.rem(z + way * offset + Z, Z)


def hidden_partial_body(place_ref, mine_ref, other_ref, weight_ref, cot_ref, *refs):
    zero_ref, far_ref, odd_ref, even_ref, give_odd_ref, give_even_ref, hold = refs
    core = place_ref[1]
    chips, rows, _ = mine_ref.shape
    for chip in range(chips):
        own = pl.multiple_of(chip * 2 * rows + core * rows, rows)
        their = pl.multiple_of(chip * 2 * rows + (1 - core) * rows, rows)
        cot_ref[pl.ds(own, rows), :] = mine_ref[chip]
        cot_ref[pl.ds(their, rows), :] = other_ref[chip]
    tokens = cot_ref.shape[0]
    width = tokens // Z
    span = tokens // SIDE
    for part in range(SIDE):
        product = lax.dot_general(
            weight_ref[...],
            cot_ref[part * span : (part + 1) * span, :],
            (((1,), (1,)), ((), ())),
            preferred_element_type=F32,
        )
        hold[:, part * span : (part + 1) * span] = (product * SCALE_HIDDEN).astype(BF16)

    def block(offset):
        low = pl.multiple_of(owner_of(place_ref, offset) * width, width)
        return hold[:, pl.ds(low, width)]

    zero_ref[...] = block(0)
    far_ref[...] = block(8)
    for k, offset in enumerate((1, 3, 5, 7)):
        odd_ref[k] = block(offset)
        give_odd_ref[k] = block(-offset)
    for k, offset in enumerate((2, 4, 6)):
        even_ref[k] = block(offset)
        give_even_ref[k] = block(-offset)


def hidden_partial(place, mine, other, weight):
    units, depth = weight.shape
    tokens = mine.shape[0] * mine.shape[1] * 2
    width = tokens // Z
    shapes = [(tokens, depth), (units, width), (units, width)]
    shapes += [(count, units, width) for count in (4, 3, 4, 3)]
    return pl.pallas_call(
        hidden_partial_body,
        out_shape=[jax.ShapeDtypeStruct(shape, BF16) for shape in shapes],
        in_specs=[SMEM] + [VMEM] * 3,
        out_specs=[VMEM] * 7,
        scratch_shapes=[pltpu.VMEM((units, tokens), BF16)],
        compiler_params=params(),
        cost_estimate=pl.CostEstimate(
            flops=2 * units * depth * tokens,
            bytes_accessed=2 * (2 * tokens * depth + units * depth + units * tokens),
            transcendentals=0,
        ),
        name="hidden_partial",
    )(place, mine, other, weight)


def start(source, target, sem):
    copy = pltpu.make_async_copy(source, target, sem)
    copy.start()
    return copy


def activations_body(acts_hbm, *refs):
    outs, (acts_ref, swish_ref, slope_ref, hidden_ref, in_sems, out_sems) = refs[:3], refs[3:]
    blocks, units, width = acts_ref.shape
    units = units // 2
    chunk = 64
    arriving = [start(acts_hbm.at[k], acts_ref.at[k], in_sems.at[k]) for k in range(blocks)]
    leaving = []
    for k in range(blocks):
        cols = slice(k * width, (k + 1) * width)
        arriving[k].wait()

        @pl.loop(0, units // chunk)
        def _(i, k=k, cols=cols):
            low = pl.multiple_of(i * chunk, chunk)
            rows = pl.ds(low, chunk)
            g = acts_ref[k, rows, :].astype(F32)
            u = acts_ref[k, pl.ds(low + units, chunk), :].astype(F32)
            s = jax.nn.sigmoid(g)
            swish = g * s
            slope = u * s * (1.0 + g * (1.0 - s))
            hidden_ref[rows, cols] = (swish * u).astype(BF16)
            swish_ref[rows, cols] = swish.astype(BF16)
            slope_ref[rows, cols] = slope.astype(BF16)

        if k % 4 == 3:
            part = slice((k - 3) * width, (k + 1) * width)
            for n, ref in enumerate((swish_ref, slope_ref, hidden_ref)):
                leaving.append(
                    start(ref.at[:, part], outs[n].at[:, part], out_sems.at[n, k // 4])
                )
    for copy in leaving:
        copy.wait()


def activations(acts):
    blocks, units, width = acts.shape
    units, tokens = units // 2, blocks * width
    return pl.pallas_call(
        activations_body,
        out_shape=[jax.ShapeDtypeStruct((units, tokens), BF16)] * 3,
        in_specs=[HBM],
        out_specs=[HBM] * 3,
        scratch_shapes=[pltpu.VMEM(acts.shape, BF16)]
        + [pltpu.VMEM((units, tokens), BF16)] * 3
        + [DMA((blocks,)), DMA((3, blocks // 4))],
        compiler_params=params(56),
        cost_estimate=pl.CostEstimate(
            flops=30 * units * tokens,
            bytes_accessed=10 * units * tokens,
            transcendentals=units * tokens,
        ),
        name="activations",
    )(acts)


def down_body(hidden_hbm, cot_hbm, weight_hbm, m_hbm, v_hbm, *refs):
    outs, sums_ref = refs[:3], refs[3]
    hidden_ref, cot_ref, weight_ref, m_ref, v_ref = refs[4:9]
    new_m_ref, new_v_ref, update_ref, product, sems, out_sems = refs[9:]
    units = weight_ref.shape[0]
    span = cot_ref.shape[0] // SIDE
    parts = [slice(k * span, (k + 1) * span) for k in range(SIDE)]
    arriving = []
    for k, part in enumerate(parts):
        arriving.append(
            (
                start(hidden_hbm.at[:, part], hidden_ref.at[:, part], sems.at[0, k]),
                start(cot_hbm.at[part], cot_ref.at[part], sems.at[1, k]),
            )
        )
    moments = [
        start(weight_hbm, weight_ref, sems.at[2, 0]),
        start(m_hbm, m_ref, sems.at[2, 1]),
        start(v_hbm, v_ref, sems.at[2, 2]),
    ]
    for k, part in enumerate(parts):
        for copy in arriving[k]:
            copy.wait()
        term = lax.dot_general(
            hidden_ref[:, part],
            cot_ref[part, :],
            (((1,), (0,)), ((), ())),
            preferred_element_type=F32,
        )
        product[...] = term if k == 0 else product[...] + term
    for copy in moments:
        copy.wait()
    step = 16
    depth = product.shape[1]

    def optimizer(i, carry):
        weight_sum, update_sum = carry
        rows = pl.ds(pl.multiple_of(i * step, step), step)
        grad = product[rows, :] * SCALE_HIDDEN
        weight = weight_ref[rows, :].astype(F32)
        first = 0.9 * m_ref[rows, :].astype(F32) + 0.1 * grad
        second = 0.95 * v_ref[rows, :].astype(F32) + 0.05 * grad * grad
        update = first / (jnp.sqrt(second) + 1e-08) + 0.1 * weight
        new_m_ref[rows, :] = first.astype(BF16)
        new_v_ref[rows, :] = second.astype(BF16)
        update_ref[rows, :] = update
        return weight_sum + weight * weight, update_sum + update * update

    zero = jnp.zeros((step, depth), F32)
    weight_sum, update_sum = lax.fori_loop(0, units // step, optimizer, (zero, zero))
    leaving = [
        start(ref, outs[n], out_sems.at[n]) for n, ref in enumerate((new_m_ref, new_v_ref, update_ref))
    ]
    weight_sum = jnp.sum(weight_sum, axis=0, keepdims=True)
    update_sum = jnp.sum(update_sum, axis=0, keepdims=True)
    lanes = sums_ref.shape[1]
    parts = [slice(k, k + lanes) for k in range(0, depth, lanes)]
    weight_sum = sum(weight_sum[:, part] for part in parts)
    update_sum = sum(update_sum[:, part] for part in parts)
    sums_ref[...] = in_rows(weight_sum, update_sum)
    for copy in leaving:
        copy.wait()


def in_rows(first, second):
    row = lax.broadcasted_iota(jnp.int32, (16, first.shape[1]), 0)
    value = jnp.where((row & 1) == 0, first, second)
    high = value.astype(BF16).astype(F32)
    middle = (value - high).astype(BF16).astype(F32)
    low = value - high - middle
    rest = jnp.where(row < 4, middle, jnp.where(row < 6, low, 0.0))
    return jnp.where(row < 2, high, rest).astype(BF16)


def from_rows(rows):
    first = rows[0:1] + rows[2:3] + rows[4:5]
    second = rows[1:2] + rows[3:4] + rows[5:6]
    return jnp.sum(first, axis=1, keepdims=True), jnp.sum(second, axis=1, keepdims=True)


def down_update(hidden, cotangent, weight, moment_m, moment_v):
    units, tokens = hidden.shape
    depth = cotangent.shape[1]
    shapes = [
        jax.ShapeDtypeStruct((units, depth), BF16),
        jax.ShapeDtypeStruct((units, depth), BF16),
        jax.ShapeDtypeStruct((units, depth), F32),
        jax.ShapeDtypeStruct((16, 128), BF16),
    ]
    return pl.pallas_call(
        down_body,
        out_shape=shapes,
        in_specs=[HBM] * 5,
        out_specs=[HBM] * 3 + [VMEM],
        scratch_shapes=[pltpu.VMEM((units, tokens), BF16), pltpu.VMEM((tokens, depth), BF16)]
        + [pltpu.VMEM((units, depth), BF16)] * 5
        + [pltpu.VMEM((units, depth), F32)] * 2
        + [DMA((3, SIDE)), DMA((3,))],
        compiler_params=params(56),
        cost_estimate=pl.CostEstimate(
            flops=2 * units * depth * tokens,
            bytes_accessed=2 * units * tokens + 2 * tokens * depth + 14 * units * depth,
            transcendentals=0,
        ),
        name="down_update",
    )(hidden, cotangent, weight, moment_m, moment_v)


def group_body(number, count, place_ref, *refs):
    grads = refs[:count]
    swish_ref, slope_ref, gate_weight_ref, up_weight_ref = refs[count : count + 4]
    befores = refs[count + 4 : -6]
    gateact_ref, upact_ref, mine_ref, other_ref, sums_ref, hold = refs[-6:]
    units = gateact_ref.shape[0]
    blocks, half, _ = mine_ref.shape
    width = 2 * half
    chunk = 64
    core = place_ref[1]

    def block(k, rows):
        if k == 4:
            return grads[1][rows, :].astype(F32)
        return grads[0][k, rows, :].astype(F32)

    sums = befores[0][...] if befores else 0.0
    for k in range(blocks):
        sums = sums + block(k, slice(units, units + 16))
    sums_ref[...] = sums
    for k, offset in enumerate(GROUPS[number]):
        start = pl.multiple_of(owner_of(place_ref, offset) * width, width)
        cols = slice(k * width, (k + 1) * width)

        @pl.loop(0, units // chunk)
        def _(i, k=k, start=start, cols=cols):
            rows = pl.ds(pl.multiple_of(i * chunk, chunk), chunk)
            grad = block(k, rows)
            swish = swish_ref[rows, pl.ds(start, width)].astype(F32)
            slope = slope_ref[rows, pl.ds(start, width)].astype(F32)
            upact_ref[rows, cols] = (grad * swish).astype(BF16)
            gateact_ref[rows, cols] = (grad * slope).astype(BF16)

    contract_first = (((0,), (0,)), ((), ()))
    product = lax.dot_general(
        gateact_ref[...], gate_weight_ref[...], contract_first, preferred_element_type=F32
    )
    product = product + lax.dot_general(
        upact_ref[...], up_weight_ref[...], contract_first, preferred_element_type=F32
    )
    hold[...] = (product * SCALE_WIDTH).astype(BF16)
    for k in range(blocks):
        own = pl.multiple_of(k * width + core * half, half)
        their = pl.multiple_of(k * width + (1 - core) * half, half)
        mine_ref[k] = hold[pl.ds(own, half), :]
        low = other_ref.shape[0] - (blocks - k) * half - (16 if number == 3 else 0)
        other_ref[low : low + half, :] = hold[pl.ds(their, half), :]
    if number == 3:
        other_ref[blocks * half :, :] = jnp.zeros((16, other_ref.shape[1]), BF16)
        first = sums[0:1] + sums[2:3] + sums[4:5]
        second = sums[1:2] + sums[3:4] + sums[5:6]
        other_ref[blocks * half :, 0:128] = in_rows(first, second)
    elif number > 0:
        earlier = befores[1].shape[0]
        other_ref[0:earlier, :] = befores[1][...]


def input_group(number, place, grads, swish, slope, gate_weight, up_weight, *befores):
    units, tokens = swish.shape
    depth = gate_weight.shape[1]
    width = tokens // Z
    blocks = len(GROUPS[number])
    half = jax.ShapeDtypeStruct((blocks, width // 2, depth), BF16)
    if number == 3:
        other_rows = blocks * width // 2 + 16
    else:
        other_rows = sum(len(offsets) for offsets in GROUPS[: number + 1]) * width // 2
    other = jax.ShapeDtypeStruct((other_rows, depth), BF16)
    acts = jax.ShapeDtypeStruct((units, blocks * width), BF16)
    sums = jax.ShapeDtypeStruct((16, 128), F32)
    return pl.pallas_call(
        functools.partial(group_body, number, len(grads)),
        out_shape=[acts, acts, half, other, sums],
        in_specs=[SMEM] + [VMEM] * (4 + len(grads) + len(befores)),
        out_specs=[VMEM] * 5,
        scratch_shapes=[pltpu.VMEM((blocks * width, depth), BF16)],
        compiler_params=params(),
        cost_estimate=pl.CostEstimate(
            flops=4 * units * depth * blocks * width,
            bytes_accessed=10 * units * blocks * width + 4 * units * depth,
            transcendentals=0,
        ),
        name="input_group",
    )(place, *grads, swish, slope, gate_weight, up_weight, *befores)


def merge_body(place_ref, *refs):
    mine = refs[:SIDE]
    first_other_ref, last_other_ref, sums_ref, out_ref = refs[SIDE:]
    rows, depth = mine[0].shape[1:]
    parts = [(q * rows, slice(q * 128, (q + 1) * 128)) for q in range(depth // 128)]
    for number, offsets in enumerate(GROUPS):
        for k, offset in enumerate(offsets):
            chip = owner_of(place_ref, offset)
            for low, cols in parts:
                out_ref[chip, low : low + rows, :] = mine[number][k, :, cols]
    first = [offset for offsets in GROUPS[:3] for offset in offsets]
    for ref, offsets in ((first_other_ref, first), (last_other_ref, GROUPS[3])):
        for k, offset in enumerate(offsets):
            chip = owner_of(place_ref, -offset)
            for low, cols in parts:
                total = out_ref[chip, low : low + rows, :].astype(F32)
                total = total + ref[k * rows : (k + 1) * rows, cols].astype(F32)
                out_ref[chip, low : low + rows, :] = total.astype(BF16)
    their = last_other_ref[len(GROUPS[3]) * rows :, 0:128].astype(F32)
    first, second = from_rows(sums_ref[...] + their)
    sums = in_rows(jnp.broadcast_to(first, (1, 128)), jnp.broadcast_to(second, (1, 128)))
    for chip in range(out_ref.shape[0]):
        out_ref[chip, len(parts) * rows :, :] = sums


def merge_cores(place, mine, first_other, last_other, sums):
    _, rows, depth = mine[0].shape
    return pl.pallas_call(
        merge_body,
        out_shape=jax.ShapeDtypeStruct((CHIPS, rows * depth // 128 + 16, 128), BF16),
        in_specs=[SMEM] + [VMEM] * (SIDE + 3),
        out_specs=VMEM,
        compiler_params=params(),
        cost_estimate=pl.CostEstimate(
            flops=CHIPS * rows * depth, bytes_accessed=6 * CHIPS * rows * depth, transcendentals=0
        ),
        name="merge_cores",
    )(place, *mine, first_other, last_other, sums)


def finish_body(arrived_ref, update_hbm, grad_input_ref, step_ref, ratio_ref, update_ref, sem):
    copy = start(update_hbm, update_ref, sem)
    chips = arrived_ref.shape[0]
    rows, depth = grad_input_ref.shape
    for q in range(depth // 128):
        for low in range(0, rows, 32):
            part = slice(q * rows + low, q * rows + low + 32)
            total = arrived_ref[0, part, :].astype(F32)
            for chip in range(1, chips):
                total = total + arrived_ref[chip, part, :].astype(F32)
            grad_input_ref[low : low + 32, q * 128 : (q + 1) * 128] = total.astype(BF16)
    part = slice(rows * depth // 128, rows * depth // 128 + 16)
    sums = arrived_ref[0, part, :].astype(F32)
    for chip in range(1, chips):
        sums = sums + arrived_ref[chip, part, :].astype(F32)
    weight_total = sums[0:1] + sums[2:3] + sums[4:5]
    update_total = sums[1:2] + sums[3:4] + sums[5:6]
    ratio = jnp.sqrt(weight_total) / jnp.sqrt(update_total + 1e-06)
    ratio_ref[...] = ratio
    ratio = ratio[:, 0:1]
    step = 16
    copy.wait()

    @pl.loop(0, update_ref.shape[0] // step)
    def _(i):
        part = pl.ds(pl.multiple_of(i * step, step), step)
        step_ref[part, :] = (ratio * update_ref[part, :]).astype(BF16)


def finish(arrived, update):
    chips, rows, _ = arrived.shape
    units, depth = update.shape
    return pl.pallas_call(
        finish_body,
        out_shape=[
            jax.ShapeDtypeStruct(((rows - 16) * 128 // depth, depth), BF16),
            jax.ShapeDtypeStruct((units, depth), BF16),
            jax.ShapeDtypeStruct((1, 128), F32),
        ],
        in_specs=[VMEM, HBM],
        out_specs=[VMEM] * 3,
        scratch_shapes=[pltpu.VMEM((units, depth), F32), DMA],
        compiler_params=params(),
        cost_estimate=pl.CostEstimate(
            flops=chips * rows * 128,
            bytes_accessed=2 * chips * rows * 128 + 6 * units * depth,
            transcendentals=0,
        ),
        name="finish",
    )(arrived, update)


def weight_grads_body(place_ref, *refs):
    gateacts, upacts = refs[:SIDE], refs[SIDE : 2 * SIDE]
    mine_ref, other_ref, grad_gate_ref, grad_up_ref, tokens, act = refs[2 * SIDE :]
    core = place_ref[1]
    chips, half, _ = mine_ref.shape
    width = 2 * half
    for chip in range(chips):
        own = pl.multiple_of(chip * width + core * half, half)
        their = pl.multiple_of(chip * width + (1 - core) * half, half)
        tokens[pl.ds(own, half), :] = mine_ref[chip]
        tokens[pl.ds(their, half), :] = other_ref[chip]
    for acts, out_ref in ((gateacts, grad_gate_ref), (upacts, grad_up_ref)):
        for number, offsets in enumerate(GROUPS):
            for k, offset in enumerate(offsets):
                start = pl.multiple_of(owner_of(place_ref, offset) * width, width)
                act[:, pl.ds(start, width)] = acts[number][:, k * width : (k + 1) * width]
        product = lax.dot_general(
            act[...], tokens[...], (((1,), (0,)), ((), ())), preferred_element_type=F32
        )
        out_ref[...] = (product * SCALE_WIDTH).astype(BF16)


def weight_grads(place, gateacts, upacts, mine, other):
    chips, half, depth = mine.shape
    units = gateacts[0].shape[0]
    tokens = chips * half * 2
    out = jax.ShapeDtypeStruct((units, depth), BF16)
    return pl.pallas_call(
        weight_grads_body,
        out_shape=[out, out],
        in_specs=[SMEM] + [VMEM] * (2 * SIDE + 2),
        out_specs=[VMEM] * 2,
        scratch_shapes=[pltpu.VMEM((tokens, depth), BF16), pltpu.VMEM((units, tokens), BF16)],
        compiler_params=params(),
        cost_estimate=pl.CostEstimate(
            flops=4 * units * depth * tokens,
            bytes_accessed=4 * units * tokens + 2 * tokens * depth + 4 * units * depth,
            transcendentals=0,
        ),
        name="weight_grads",
    )(place, *gateacts, *upacts, mine, other)


def shards(
    tokens, cotangent, gate_pre, up_act, gate_weight, up_weight, down_weight, moment_m, moment_v
):
    z = lax.axis_index("row")
    core = lax.axis_index("col") & 1
    place = jnp.stack([z, core, 1 - 2 * core]).astype(jnp.int32)

    acts = jnp.concatenate([gate_pre.T, up_act.T], axis=0)
    acts, cotangent = lax.optimization_barrier((acts, cotangent))
    acts = lax.all_gather(acts, "row", axis=0, tiled=False)
    cot_mine, cot_other = gather_chips(cotangent)
    cotangent_all, zero, far, odd, even, give_odd, give_even = hidden_partial(
        place, cot_mine, cot_other, down_weight
    )
    tokens, zero = lax.optimization_barrier((tokens, zero))
    tok_mine, tok_other = gather_chips(tokens)
    swish, slope, hidden = activations(acts)
    new_m, new_v, update, sums = down_update(
        hidden, cotangent_all, down_weight, moment_m, moment_v
    )
    own, other, ((swish, tok_other), _) = reduce_z(
        zero, far, odd, even, give_odd, give_even, ((swish, tok_other), sums)
    )

    gate_weight, up_weight = gate_weight.T, up_weight.T

    def group(number, grads, *befores):
        return input_group(
            number, place, grads, swish, slope, gate_weight, up_weight, *befores
        )

    others, owns = [other], [own]
    for _ in range(3):
        others.append(shift_z(others[-1], 2))
        owns.append(shift_z(owns[-1], 2))
    even_other, even = jnp.stack(others), jnp.stack(owns)
    odd_other = shift_z(even_other, 1)
    odd = shift_z(even, 1)
    far = shift_z(owns[3], 2)
    ahead_even = swap_core(even_other[1:])
    group_0 = group(0, (even,))
    group_1 = group(1, (ahead_even,), group_0[4], group_0[3])
    odd_other, odd, far, group_0, group_1 = lax.optimization_barrier(
        (odd_other, odd, far, group_0, group_1)
    )
    ahead_odd = swap_core(odd_other)
    group_2 = group(2, (odd,), group_1[4], group_1[3])
    group_3 = group(3, (ahead_odd, far), group_2[4])
    gateacts, upacts, mine, _, _ = zip(group_0, group_1, group_2, group_3)
    merged = merge_cores(
        place, mine, swap_core(group_2[3]), swap_core(group_3[3]), group_3[4]
    )
    merged, tok_mine = lax.optimization_barrier((merged, tok_mine))
    arrived = exchange_chips(merged)
    grad_gate, grad_up = weight_grads(place, gateacts, upacts, tok_mine, tok_other)
    arrived, grad_gate, grad_up = lax.optimization_barrier((arrived, grad_gate, grad_up))
    grad_input, step_down, ratio = finish(arrived, update)
    return grad_input, grad_gate.T, grad_up.T, new_m, new_v, step_down, ratio[0, 0]


def solution(mesh):
    in_specs = (
        P("col", "row"),
        P("col", "row"),
        P("row", "col"),
        P("row", "col"),
        P("row", "col"),
        P("row", "col"),
        P("col", "row"),
        P("col", "row"),
        P("col", "row"),
    )
    out_specs = (
        P("col", "row"),
        P("row", "col"),
        P("row", "col"),
        P("col", "row"),
        P("col", "row"),
        P("col", "row"),
        P(),
    )
    return jax.shard_map(shards, mesh=mesh, in_specs=in_specs, out_specs=out_specs, check_vma=False)
```
